32 devices in a mesh: pts: 4 (over y, core), cen: 8 (over z, x).
Axes of the slice: x: 2, y: 2, z: 4, core: 2. Of those that a mesh axis runs over, the one named last changes fastest.
Arguments:
- points: bfloat16 [16384, 1024], P('pts'), may hold values from -128 to 128
- centroids: float32 [8192, 1024], P('cen'), may hold values from -10 to 10
Outputs:
- centroid_means: float32 [8192, 1024], P('cen', 'pts')
- log_norms: float32 [16384], P('pts')
The draws below stay inside these ranges and needn't reach their ends.
All inputs are finite; a program needn't handle non-finite values.
Results may differ from the reference program's by a relative error of at most 0.0015.
The reference program's roundings to bfloat16 on the way (of `unit_rows` and `weights`) count: a program that leaves them out, or rounds other values in their place, can miss the bound.
Values may be sent and summed in bfloat16 or wider, within the bound.
No kernel may reach another device: no remote copies, remote signals or barrier semaphores. Data moves between devices by JAX's collectives and lax.ppermute only.
A program may use at most 64 MiB of HBM per device.

```python
import math
import jax
import jax.numpy as jnp
from jax import lax

D = 1024
K = 8192
ITERS = 2
PTS = 16384


def centroid_base(key):
    feature_key, value_key = jax.random.split(jax.random.fold_in(key, 11))
    feature_scale = jnp.exp(jax.random.uniform(feature_key, (1, D), jnp.float32, math.log(0.5), math.log(2.0)))
    values = jnp.clip(jax.random.normal(value_key, (K, D), jnp.float32), -5.0, 5.0)
    return values * feature_scale


def draw_centroids(key, part):
    return centroid_base(key)


def draw_points(key, part):
    row_key, value_key = jax.random.split(jax.random.fold_in(key, 23), 2)
    row_scale = jnp.exp(jax.random.uniform(row_key, (PTS, 1), jnp.float32, math.log(0.3), math.log(3.0)))
    result = jnp.clip(jax.random.normal(value_key, (PTS, D), jnp.float32), -5.0, 5.0) * row_scale
    return jnp.clip(result, -128.0, 128.0).astype(jnp.bfloat16)


def setup_inputs(seed: int = 0) -> dict:
    key_list = jax.random.split(jax.random.key(seed), 3)
    points = draw_points(jax.random.fold_in(key_list[2], 71), 0)
    centroids = draw_centroids(jax.random.fold_in(key_list[2], 71), 0)
    return {"points": points, "centroids": centroids}


def normalize_rows(rows):
    return rows * lax.rsqrt(lax.optimization_barrier(jnp.sum(rows * rows, axis=1, keepdims=True)) + 1e-06)

def reference(points, centroids):
    total_rows = points.shape[0]
    block_rows = min(total_rows, 1024)
    block_count = total_rows // block_rows
    blocks = points.reshape(block_count, block_rows, D)
    unit_rows = normalize_rows(centroids).astype(jnp.bfloat16)
    centroid_means = centroids
    log_values = jnp.zeros((block_count, block_rows), jnp.float32)
    for iteration in range(ITERS):
        current = unit_rows

        def visit(carry, block):
            weighted, point_mass = carry
            logits = jnp.dot(block, current.T, preferred_element_type=jnp.float32)
            row_max = lax.optimization_barrier(jnp.max(logits, axis=1))
            shifted = jnp.exp(logits - row_max[:, None])
            row_total = lax.optimization_barrier(jnp.sum(shifted, axis=1))
            weights = (shifted / row_total[:, None]).astype(jnp.bfloat16)
            weighted = weighted + jnp.dot(weights.T, block, preferred_element_type=jnp.float32)
            point_mass = point_mass + lax.optimization_barrier(jnp.sum(weights.astype(jnp.float32), axis=0))
            return ((weighted, point_mass), row_max + jnp.log(row_total))
        start = (jnp.zeros((K, D), jnp.float32), jnp.zeros((K,), jnp.float32))
        (weighted, point_mass), log_values = lax.scan(visit, start, blocks)
        centroid_means = weighted / jnp.maximum(point_mass, 1.0)[:, None]
        unit_rows = normalize_rows(centroid_means).astype(jnp.bfloat16)
    return (centroid_means, log_values.reshape(total_rows))
```

```python
import functools

import jax
import jax.numpy as jnp
from jax import lax
from jax.experimental import pallas as pl
from jax.experimental.pallas import tpu as pltpu
from jax.sharding import PartitionSpec as P

ITERS = 2
F32 = jnp.float32
BF16 = jnp.bfloat16
VMEM_LIMIT = 40 * 2**20


def divisor(total, wanted):
    size = min(total, wanted)
    while total % size:
        size -= 1
    return size


def normalize_rows(rows):
    return rows * lax.rsqrt(jnp.sum(rows * rows, axis=1, keepdims=True) + 1e-06)


def fill_from_centroids(pos_ref, unit_refs, units):
    rows = units.shape[0]
    step = divisor(rows, 256)
    for start in range(0, rows, step):
        block = unit_refs[0][start : start + step, :]
        units[start : start + step, :] = normalize_rows(block).astype(BF16)


def fill_from_blocks(pos_ref, unit_refs, units):
    rows = unit_refs[0].shape[0]
    for number, ref in enumerate(unit_refs):
        start = pl.multiple_of(pos_ref[number] * rows, rows)
        units[pl.ds(start, rows), :] = ref[...]


def score_body(fill, count, sub, pos_ref, *refs):
    unit_refs = refs[:count]
    x_ref, e_ref, stat_ref, units = refs[count:]

    @pl.when(pl.program_id(0) == 0)
    def _():
        fill(pos_ref, unit_refs, units)

    for start in range(0, x_ref.shape[0], sub):
        part = slice(start, start + sub)
        logits = lax.dot_general(
            units[...], x_ref[part, :], (((1,), (1,)), ((), ())), preferred_element_type=F32
        )
        top = jnp.max(logits, axis=0, keepdims=True)
        shifted = jnp.exp(logits - top)
        e_ref[:, part] = shifted
        stat_ref[0:1, part] = top
        stat_ref[1:2, part] = jnp.sum(shifted, axis=0, keepdims=True)


def scores(fill, pos, unit_arrays, points, rows):
    total, width = points.shape
    block = divisor(total, 512)
    sub = divisor(block, 256)
    whole = [
        pl.BlockSpec(u.shape, lambda i, pos: (0, 0), pipeline_mode=pl.Buffered(1)) for u in unit_arrays
    ]
    return pl.pallas_call(
        functools.partial(score_body, fill, len(unit_arrays), sub),
        grid_spec=pltpu.PrefetchScalarGridSpec(
            num_scalar_prefetch=1,
            grid=(total // block,),
            in_specs=whole + [pl.BlockSpec((block, width), lambda i, pos: (i, 0))],
            out_specs=[
                pl.BlockSpec((rows, block), lambda i, pos: (0, i)),
                pl.BlockSpec((2, block), lambda i, pos: (0, i)),
            ],
            scratch_shapes=[pltpu.VMEM((rows, width), BF16)],
        ),
        out_shape=[
            jax.ShapeDtypeStruct((rows, total), F32),
            jax.ShapeDtypeStruct((2, total), F32),
        ],
        compiler_params=pltpu.CompilerParams(vmem_limit_bytes=VMEM_LIMIT),
        cost_estimate=pl.CostEstimate(
            flops=2 * rows * total * width,
            bytes_accessed=2 * total * width + 4 * rows * total,
            transcendentals=rows * total,
        ),
    )(pos, *unit_arrays, points)


def weigh_body(n_stats, n_e, n_x, pos_ref, *refs):
    stat_refs, refs = refs[:n_stats], refs[n_stats:]
    e_refs, refs = refs[:n_e], refs[n_e:]
    x_refs, refs = refs[:n_x], refs[n_x:]
    mine_ref, theirs_ref, mass_ref, log_ref, scale_ref = refs[:5]
    mass_sums = refs[5:]
    other, chunk = pl.program_id(0), pl.program_id(1)
    width = e_refs[0].shape[1]

    @pl.when(jnp.logical_and(other == 0, chunk == 0))
    def _():
        top = stat_refs[0][0:1, :]
        for ref in stat_refs[1:]:
            top = jnp.maximum(top, ref[0:1, :])
        own = jnp.exp(stat_refs[0][0:1, :] - top)
        total = stat_refs[0][1:2, :] * own
        for ref in stat_refs[1:]:
            total = total + ref[1:2, :] * jnp.exp(ref[0:1, :] - top)
        scale_ref[...] = own / total
        log_ref[...] = top + jnp.log(total)

    @pl.when(chunk == 0)
    def _():
        mine_ref[...] = jnp.zeros_like(mine_ref)
        theirs_ref[...] = jnp.zeros_like(theirs_ref)
        for sums in mass_sums:
            sums[...] = jnp.zeros_like(sums)

    scale = scale_ref[:, pl.ds(pl.multiple_of(chunk * width, width), width)]
    weights = []
    for ref, sums in zip(e_refs, mass_sums):
        rounded = (ref[...] * scale).astype(BF16)
        weights.append(rounded)
        wide = rounded.astype(F32)
        lanes = min(width, 128)
        part = wide[:, :lanes]
        for start in range(lanes, width, lanes):
            part = part + wide[:, start : start + lanes]
        sums[...] += part
    for number, out_ref in enumerate((mine_ref, theirs_ref)):
        out_ref[...] += jnp.dot(
            weights[number % n_e], x_refs[number % n_x][...], preferred_element_type=F32
        )

    @pl.when(chunk == pl.num_programs(1) - 1)
    def _():
        for number, sums in enumerate(mass_sums):
            mass_ref[number : number + 1, :] = jnp.sum(sums[...].T, axis=0, keepdims=True)


def weigh(by_rows, targets, stats, shifted, points, size):
    rows, total = shifted.shape
    width = points.shape[1]
    others = targets.shape[0] // 2
    chunk = divisor(total, 512)
    if by_rows:
        out = (size, width)
        e_specs = [
            pl.BlockSpec((size, chunk), lambda d, k, pos, w=w: (pos[2 * d + w], k)) for w in range(2)
        ]
        x_specs = [pl.BlockSpec((chunk, width), lambda d, k, pos: (k, 0))]
    else:
        out = (rows, size)
        e_specs = [pl.BlockSpec((rows, chunk), lambda d, k, pos: (0, k))]
        x_specs = [
            pl.BlockSpec((chunk, size), lambda d, k, pos, w=w: (k, pos[2 * d + w])) for w in range(2)
        ]
    n_e, n_x = len(e_specs), len(x_specs)
    height = out[0]
    stat_spec = pl.BlockSpec((2, total), lambda d, k, pos: (0, 0), pipeline_mode=pl.Buffered(1))
    return pl.pallas_call(
        functools.partial(weigh_body, len(stats), n_e, n_x),
        grid_spec=pltpu.PrefetchScalarGridSpec(
            num_scalar_prefetch=1,
            grid=(others, total // chunk),
            in_specs=[stat_spec] * len(stats) + e_specs + x_specs,
            out_specs=[
                pl.BlockSpec((None, *out), lambda d, k, pos: (d, 0, 0)),
                pl.BlockSpec((None, *out), lambda d, k, pos: (d, 0, 0)),
                pl.BlockSpec((None, n_e, height), lambda d, k, pos: (d, 0, 0)),
                pl.BlockSpec((1, total), lambda d, k, pos: (0, 0)),
            ],
            scratch_shapes=[pltpu.VMEM((1, total), F32)] + [pltpu.VMEM((height, 128), F32)] * n_e,
        ),
        out_shape=[
            jax.ShapeDtypeStruct((others, *out), F32),
            jax.ShapeDtypeStruct((others, *out), F32),
            jax.ShapeDtypeStruct((others, n_e, height), F32),
            jax.ShapeDtypeStruct((1, total), F32),
        ],
        compiler_params=pltpu.CompilerParams(vmem_limit_bytes=VMEM_LIMIT),
        cost_estimate=pl.CostEstimate(
            flops=4 * others * out[0] * out[1] * total,
            bytes_accessed=others * total * (4 * n_e * height + 2 * n_x * x_specs[0].block_shape[1]),
            transcendentals=0,
        ),
    )(targets, *stats, *[shifted] * n_e, *[points] * n_x)


def finish_body(count, mass_ref, *refs):
    total = refs[0][...]
    for ref in refs[1:count]:
        total = total + ref[...]
    means = total / jnp.maximum(mass_ref[...], 1.0)
    refs[count][...] = normalize_rows(means).astype(BF16)


def finish(mass, terms):
    rows, width = terms[0].shape
    block = divisor(rows, 64)
    spec = pl.BlockSpec((block, width), lambda i: (i, 0))
    return pl.pallas_call(
        functools.partial(finish_body, len(terms)),
        grid=(rows // block,),
        in_specs=[pl.BlockSpec((block, 1), lambda i: (i, 0))] + [spec] * len(terms),
        out_specs=spec,
        out_shape=jax.ShapeDtypeStruct((rows, width), BF16),
        compiler_params=pltpu.CompilerParams(vmem_limit_bytes=VMEM_LIMIT),
        cost_estimate=pl.CostEstimate(
            flops=8 * rows * width, bytes_accessed=4 * rows * width * len(terms), transcendentals=rows
        ),
    )(mass[:, None], *terms)


def on_device(n_pts, n_cen, points, centroids):
    rows, width = centroids.shape
    chips = n_pts // 2
    block = rows // n_pts
    me = lax.axis_index("pts")
    chip, core = me // 2, me % 2

    def to_partner(value):
        return lax.ppermute(value, "pts", [(i, i ^ 1) for i in range(n_pts)])

    def to_chip(value, away):
        moves = [(i, (i + 2 * away) % n_pts) for i in range(n_pts)]
        return lax.ppermute(value, "pts", moves)

    def all_stats(stats):
        found = [stats]
        for away in range(1, n_cen):
            if n_cen & (n_cen - 1):
                moves = [(i, (i + away) % n_cen) for i in range(n_cen)]
            else:
                moves = [(i, i ^ away) for i in range(n_cen)]
            found.append(lax.ppermute(stats, "cen", moves))
        return found

    def blocks_of(aways):
        ids = []
        for away in aways:
            there = (chip + away) % chips
            ids += [2 * there + core, 2 * there + 1 - core]
        return jnp.stack(ids).astype(jnp.int32)

    far = blocks_of(range(1, chips))
    near = blocks_of([0])

    def sums_over_pts(by_rows, stats, shifted, size):
        far_mine, far_theirs, far_mass, logs = weigh(by_rows, far, stats, shifted, points, size)
        far_sums = far_mine + to_partner(far_theirs)
        terms = [to_chip(far_sums[away - 1], away) for away in range(1, chips)]
        near_mine, near_theirs, near_mass, _ = weigh(by_rows, near, stats, shifted, points, size)
        near_terms = [near_mine[0], to_partner(near_theirs)[0]]
        if by_rows:
            mass = jnp.zeros((n_pts, size), F32)
            mass = mass.at[far].set(far_mass.reshape(-1, size)).at[near].set(near_mass.reshape(-1, size))
            mass = lax.psum(mass, "pts")[me]
        else:
            mass = lax.psum(near_mass[0, 0], "pts")
        return near_terms + terms, mass, logs

    pos = jnp.zeros((1,), jnp.int32)
    shifted, stats = scores(fill_from_centroids, pos, [centroids], points, rows)
    for _ in range(ITERS - 1):
        terms, mass, _ = sums_over_pts(True, all_stats(stats), shifted, block)
        mine = finish(mass, terms)
        others = [mine] + [to_chip(mine, away) for away in range(1, chips)]
        units = []
        for unit in others:
            units += [unit, to_partner(unit)]
        order = [near] + [blocks_of([-away]) for away in range(1, chips)]
        shifted, stats = scores(fill_from_blocks, jnp.concatenate(order), units, points, rows)
    terms, mass, logs = sums_over_pts(False, all_stats(stats), shifted, width // n_pts)
    total = terms[0]
    for term in terms[1:]:
        total = total + term
    return (total / jnp.maximum(mass, 1.0)[:, None], logs[0])


def solution(mesh):
    placed = (P("pts", None), P("cen", None))
    return jax.shard_map(
        functools.partial(on_device, mesh.shape["pts"], mesh.shape["cen"]),
        mesh=mesh,
        in_specs=placed,
        out_specs=(P("cen", "pts"), P("pts")),
        check_vma=False,
    )
```

```python
import functools

import jax
import jax.numpy as jnp
from jax import lax
from jax.experimental import pallas as pl
from jax.experimental.pallas import tpu as pltpu
from jax.sharding import PartitionSpec as P

ITERS = 2
F32 = jnp.float32
BF16 = jnp.bfloat16
VMEM_LIMIT = 50 * 2**20
LEVELS = 30000.0
LOWEST = -117.0


def divisor(total, wanted):
    size = min(total, wanted)
    while total % size:
        size -= 1
    return size


def round_up(value, unit):
    return -(-value // unit) * unit


def normalize_rows(rows):
    return rows * lax.rsqrt(jnp.sum(rows * rows, axis=1, keepdims=True) + 1e-06)


def params():
    return pltpu.CompilerParams(vmem_limit_bytes=VMEM_LIMIT)


def fetch(x_ref, buffer, semaphores, step, rows, columns=None):
    slot = lax.rem(step, 2)
    source = x_ref.at[rows, :] if columns is None else x_ref.at[rows, columns]
    return pltpu.make_async_copy(source, buffer.at[slot], semaphores.at[slot])


def merge(stats, other):
    top = jnp.maximum(stats[0], other[0])
    return top, stats[1] * jnp.exp(stats[0] - top) + other[1] * jnp.exp(other[0] - top)


def to_column(row, height):
    return jnp.broadcast_to(row, (128, height)).T


def encode(values, scale):
    steps = jnp.floor(jnp.abs(values) * (LEVELS / scale) + 0.5)
    power = jnp.floor(steps * (1.0 / 128.0))
    size = (1.0 + (steps * (1.0 / 128.0) - power)) * jnp.exp2(power + LOWEST)
    return jnp.where(values < 0.0, -size, size).astype(BF16)


def decode(codes, scale):
    wide = codes.astype(F32)
    size = jnp.abs(wide)
    power = jnp.floor(jnp.log2(size))
    steps = 128.0 * (power - LOWEST + (size * jnp.exp2(-power) - 1.0))
    return jnp.where(wide < 0.0, -steps, steps) * (scale * (1.0 / LEVELS))


def fill_from_centroids(pos_ref, unit_refs, units):
    rows = units.shape[0]
    step = divisor(rows, 256)
    for start in range(0, rows, step):
        block = unit_refs[0][start : start + step, :]
        units[start : start + step, :] = normalize_rows(block).astype(BF16)


def fill_from_blocks(pos_ref, unit_refs, units):
    rows = unit_refs[0].shape[0]
    for number, ref in enumerate(unit_refs):
        start = pl.multiple_of(pos_ref[number] * rows, rows)
        units[pl.ds(start, rows), :] = ref[...]


def score_body(fill, count, sub, pos_ref, *refs):
    unit_refs = refs[:count]
    x_ref, e_ref, stat_ref, units, buffer, semaphores = refs[count:]
    step = pl.program_id(0)
    block = buffer.shape[1]

    def points_of(number):
        rows = pl.ds(pl.multiple_of(number * block, block), block)
        return fetch(x_ref, buffer, semaphores, number, rows)

    @pl.when(step == 0)
    def _():
        points_of(0).start()
        fill(pos_ref, unit_refs, units)

    @pl.when(step + 1 < pl.num_programs(0))
    def _():
        points_of(step + 1).start()

    points_of(step).wait()
    slot = lax.rem(step, 2)
    tops, totals = [], []
    for start in range(0, block, sub):
        part = slice(start, start + sub)
        logits = lax.dot_general(
            units[...], buffer[slot, part, :], (((1,), (1,)), ((), ())), preferred_element_type=F32
        )
        top = jnp.max(logits, axis=0, keepdims=True)
        shifted = jnp.exp(logits - top)
        e_ref[:, part] = shifted
        tops.append(top)
        totals.append(jnp.sum(shifted, axis=0, keepdims=True))
    stat_ref[0, pl.ds(step, 1), :] = jnp.concatenate(tops, axis=1)
    stat_ref[1, pl.ds(step, 1), :] = jnp.concatenate(totals, axis=1)


def scores(fill, pos, unit_arrays, points, rows):
    total, width = points.shape
    block = divisor(total, 512)
    sub = divisor(block, 256)
    stat = (2, total // block, block)
    whole = [
        pl.BlockSpec(u.shape, lambda i, pos: (0, 0), pipeline_mode=pl.Buffered(1)) for u in unit_arrays
    ]
    return pl.pallas_call(
        functools.partial(score_body, fill, len(unit_arrays), sub),
        grid_spec=pltpu.PrefetchScalarGridSpec(
            num_scalar_prefetch=1,
            grid=(total // block,),
            in_specs=whole + [pl.BlockSpec(memory_space=pl.ANY)],
            out_specs=[
                pl.BlockSpec((rows, block), lambda i, pos: (0, i)),
                pl.BlockSpec(stat, lambda i, pos: (0, 0, 0)),
            ],
            scratch_shapes=[
                pltpu.VMEM((rows, width), BF16),
                pltpu.VMEM((2, block, width), BF16),
                pltpu.SemaphoreType.DMA((2,)),
            ],
        ),
        out_shape=[
            jax.ShapeDtypeStruct((rows, total), F32),
            jax.ShapeDtypeStruct(stat, F32),
        ],
        compiler_params=params(),
        cost_estimate=pl.CostEstimate(
            flops=2 * rows * total * width,
            bytes_accessed=2 * total * width + 4 * rows * total,
            transcendentals=rows * total,
        ),
    )(pos, *unit_arrays, points)


def weigh_body(by_rows, n_groups, parts, extra, pos_ref, stat_ref, more_ref, *refs):
    top_refs, refs = refs[:n_groups], refs[n_groups:]
    e_refs, refs = refs[:n_groups], refs[n_groups:]
    x_ref, _ = refs[:2]
    out_refs, refs = refs[2 : 2 + parts], refs[2 + parts :]
    scale_refs, refs = refs[:n_groups], refs[n_groups:]
    mass_refs, refs = refs[:n_groups], refs[n_groups:]
    sum_refs, (buffer, semaphores) = refs[:n_groups], refs[n_groups:]
    other, chunk = pl.program_id(0), pl.program_id(1)
    chunks = pl.num_programs(1)
    step = other * chunks + chunk
    height, span = buffer.shape[1:]
    core, chip = pos_ref[0], pos_ref[1]
    pair = e_refs[0].shape[0]
    line = stat_ref.shape[2]
    lines = e_refs[0].shape[1] // line
    chips = n_groups

    def points_of(number):
        rows = pl.ds(pl.multiple_of(lax.rem(number, chunks) * height, height), height)
        if by_rows:
            return fetch(x_ref, buffer, semaphores, number, rows)
        place = pos_ref[2 + lax.div(number, chunks)]
        columns = pl.ds(pl.multiple_of(place * span, span), span)
        return fetch(x_ref, buffer, semaphores, number, rows, columns)

    @pl.when(step == 0)
    def _():
        points_of(0).start()
        top, total = merge(stat_ref, more_ref)
        for ref, scale_ref in zip(top_refs, scale_refs):
            scale_ref[...] = jnp.exp(ref[0] - top) / total

    @pl.when(step + 1 < pl.num_programs(0) * chunks)
    def _():
        points_of(step + 1).start()

    points_of(step).wait()
    slot = lax.rem(step, 2)

    @pl.when(chunk == 0)
    def _():
        for ref in (*mass_refs, *sum_refs):
            ref[...] = jnp.zeros_like(ref)

    for e_ref, scale_ref, mass_ref, sum_ref in zip(e_refs, scale_refs, mass_refs, sum_refs):
        rounded = []
        mass = mass_ref[...]
        for number in range(lines):
            scale = scale_ref[pl.ds(chunk * lines + number, 1), :]
            weights = (e_ref[:, number * line : (number + 1) * line] * scale).astype(BF16)
            rounded.append(weights)
            wide = weights.astype(F32)
            lanes = min(line, 128)
            for start in range(0, line, lanes):
                mass = mass + wide[:, start : start + lanes]
        mass_ref[...] = mass
        weights = jnp.concatenate(rounded, axis=1) if lines > 1 else rounded[0]
        sum_ref[...] += jnp.dot(weights, buffer[slot], preferred_element_type=F32)

    @pl.when(chunk == chunks - 1)
    def _():
        rows = out_refs[0].shape[0] - extra
        width = out_refs[0].shape[1]
        masses = [jnp.sum(ref[...].T, axis=0, keepdims=True) for ref in mass_refs]
        for part, ref in enumerate(out_refs):
            place = lax.rem(core + part, parts)
            ref[rows:, :] = jnp.zeros((extra, width), F32)
            if by_rows:
                start = pl.multiple_of(place * rows, rows)
                ref[:rows, :] = sum_refs[0][pl.ds(start, rows), :] if parts > 1 else sum_refs[0][...]
                mass = masses[0]
                if parts > 1:
                    mass = jnp.where(place == 0, mass[:, :rows], mass[:, rows:])
                ref[rows : rows + 1, :rows] = mass
                continue
            for group, (sum_ref, mass) in enumerate(zip(sum_refs, masses)):
                owner = lax.rem(chip + group, chips)
                sums = sum_ref[...]
                if parts > 1:
                    sums = jnp.where(place == 0, sums[:, :width], sums[:, width:])
                ref[pl.ds(pl.multiple_of(owner * pair, pair), pair), :] = sums
                for number in range(pair // width):
                    ref[pl.ds(rows + owner * (pair // width) + number, 1), :] = mass[
                        :, number * width : (number + 1) * width
                    ]


def weigh(by_rows, parts, pos, stats, tops, shifted, pair, points, after):
    total, width = points.shape
    others = pos.shape[0] - 2
    cores = 2
    line = stats[0].shape[2]
    chunk = line * divisor(total // line, 2)
    if by_rows:
        rows, cols = pair // cores, width
        height = rows * parts
        sums = (height, width)
        e_specs = [pl.BlockSpec((height, chunk), lambda d, k, pos: (pos[2 + d], k))]
    else:
        rows = sum(e.shape[0] for e in shifted)
        cols = width * pair // (cores * rows)
        height = pair
        sums = (pair, cols * parts)
        e_specs, e_args = [], []
        for e in shifted:
            for number in range(e.shape[0] // pair):
                e_specs.append(pl.BlockSpec((pair, chunk), lambda d, k, pos, n=number: (n, k)))
                e_args.append(e)
        tops = [top for top, e in zip(tops, shifted) for _ in range(e.shape[0] // pair)]
        shifted = e_args
    n_groups = len(e_specs)
    extra = round_up(-(-rows // cols), 8)
    out = (rows + extra, cols)
    stat_spec = pl.BlockSpec(stats[0].shape, lambda d, k, pos: (0, 0, 0))
    out_spec = pl.BlockSpec((None, *out), lambda d, k, pos: (d, 0, 0))
    out_shape = jax.ShapeDtypeStruct((others, *out), F32)
    return pl.pallas_call(
        functools.partial(weigh_body, by_rows, n_groups, parts, extra),
        grid_spec=pltpu.PrefetchScalarGridSpec(
            num_scalar_prefetch=1,
            grid=(others, total // chunk),
            in_specs=[stat_spec] * (2 + n_groups) + e_specs + [pl.BlockSpec(memory_space=pl.ANY)] * 2,
            out_specs=[out_spec] * parts,
            scratch_shapes=[pltpu.VMEM(stats[0].shape[1:], F32)] * n_groups
            + [pltpu.VMEM((height, 128), F32)] * n_groups
            + [pltpu.VMEM(sums, F32)] * n_groups
            + [pltpu.VMEM((2, chunk, sums[1]), BF16), pltpu.SemaphoreType.DMA((2,))],
        ),
        out_shape=[out_shape] * parts,
        compiler_params=params(),
        cost_estimate=pl.CostEstimate(
            flops=2 * others * n_groups * sums[0] * sums[1] * total,
            bytes_accessed=others * total * (4 * n_groups * height + 2 * sums[1]),
            transcendentals=0,
        ),
    )(pos, *stats, *tops, *shifted, points, after)


def fold_body(rows, lines, mine_ref, theirs_ref, after_ref, out_ref):
    width = out_ref.shape[1]
    step = divisor(rows, 128) if lines == 1 else width
    out_ref[rows:, :] = jnp.zeros((out_ref.shape[0] - rows, width), BF16)
    scales = []
    for start in range(0, rows, step):
        part = slice(start, start + step)
        total = mine_ref[part, :] + theirs_ref[part, :]
        top = jnp.max(jnp.abs(total), axis=1, keepdims=True)
        scale = jnp.maximum(top * 1.01, 1e-30).astype(BF16)
        out_ref[part, :] = encode(total, scale.astype(F32))
        scales.append(jnp.broadcast_to(scale.astype(F32), (step, 128)).T[0:1, :])
    mass = mine_ref[rows : rows + lines, :] + theirs_ref[rows : rows + lines, :]
    if lines == 1:
        out_ref[rows : rows + 1, :rows] = jnp.concatenate(scales, axis=1).astype(BF16)
    else:
        out_ref[rows : rows + lines, :] = jnp.concatenate(scales, axis=0).astype(BF16)
    for number in range(1, 4):
        rounded = mass.astype(BF16)
        out_ref[rows + number * lines : rows + (number + 1) * lines, :] = rounded
        mass = mass - rounded.astype(F32)


def fold(mine, theirs, after):
    others, height, width = mine.shape
    return pl.pallas_call(
        functools.partial(fold_body, *shape_of(height, width)),
        grid=(others,),
        in_specs=[pl.BlockSpec((None, height, width), lambda d: (d, 0, 0))] * 2
        + [pl.BlockSpec(memory_space=pl.ANY)],
        out_specs=pl.BlockSpec((None, coded_height(height, width), width), lambda d: (d, 0, 0)),
        out_shape=jax.ShapeDtypeStruct((others, coded_height(height, width), width), BF16),
        compiler_params=params(),
        cost_estimate=pl.CostEstimate(
            flops=20 * others * height * width,
            bytes_accessed=10 * others * height * width,
            transcendentals=others * height * width,
        ),
    )(mine, theirs, after)


def shape_of(height, width):
    rows = height - 8
    while rows + round_up(-(-rows // width), 8) != height:
        rows -= 8
    return rows, -(-rows // width)


def coded_height(height, width):
    rows, lines = shape_of(height, width)
    return rows + round_up(4 * lines, 16)


def finish_body(rows, lines, as_units, mine_ref, theirs_ref, *refs):
    code_refs, out_ref = refs[:-1], refs[-1]
    width = out_ref.shape[1]
    step = divisor(rows, 128) if lines == 1 else width
    mass = mine_ref[rows : rows + lines, :] + theirs_ref[rows : rows + lines, :]
    for ref in code_refs:
        for number in range(1, 4):
            start = rows + number * lines
            mass = mass + ref[start : start + lines, :].astype(F32)

    def column(values, number):
        if lines == 1:
            line = values[:, number * step : (number + 1) * step]
        else:
            line = values[number : number + 1, :]
        return to_column(line, step)[:, 0:1]

    scales = [ref[rows : rows + lines, :].astype(F32) for ref in code_refs]
    for number in range(rows // step):
        part = slice(number * step, (number + 1) * step)
        total = mine_ref[part, :] + theirs_ref[part, :]
        for ref, scale in zip(code_refs, scales):
            total = total + decode(ref[part, :], column(scale, number))
        means = total / jnp.maximum(column(mass, number), 1.0)
        out_ref[part, :] = normalize_rows(means).astype(BF16) if as_units else means


def finish(as_units, mine, theirs, codes):
    height, width = mine.shape
    rows, lines = shape_of(height, width)
    out_type = BF16 if as_units else F32
    return pl.pallas_call(
        functools.partial(finish_body, rows, lines, as_units),
        out_shape=jax.ShapeDtypeStruct((rows, width), out_type),
        compiler_params=params(),
        cost_estimate=pl.CostEstimate(
            flops=30 * rows * width,
            bytes_accessed=(12 + 2 * len(codes)) * rows * width,
            transcendentals=2 * rows * width,
        ),
    )(mine, theirs, *codes)


def merge_body(one_ref, two_ref, out_ref):
    out_ref[0], out_ref[1] = merge(one_ref, two_ref)


def merged(one, two):
    return pl.pallas_call(
        merge_body, out_shape=jax.ShapeDtypeStruct(one.shape, F32), compiler_params=params()
    )(one, two)


def log_body(one_ref, two_ref, out_ref):
    top, total = merge(one_ref, two_ref)
    out_ref[...] = top + jnp.log(total)


def log_norms(one, two):
    return pl.pallas_call(
        log_body, out_shape=jax.ShapeDtypeStruct(one.shape[1:], F32), compiler_params=params()
    )(one, two).reshape(-1)


def on_device(n_pts, n_cen, points, centroids):
    rows, width = centroids.shape
    cores = 2
    chips = n_pts // cores
    pair = rows // chips
    me = lax.axis_index("pts")
    chip, core = lax.div(me, cores), lax.rem(me, cores)

    def to_partner(value):
        return lax.ppermute(value, "pts", [(i, i ^ 1) for i in range(n_pts)])

    def to_chip(value, away):
        moves = [(i, (i + cores * away) % n_pts) for i in range(n_pts)]
        return lax.ppermute(value, "pts", moves)

    def over_centroids(stats):
        if n_cen & (n_cen - 1):
            found = [stats]
            for away in range(1, n_cen):
                moves = [(i, (i + away) % n_cen) for i in range(n_cen)]
                found.append(lax.ppermute(stats, "cen", moves))
            return functools.reduce(merged, found[:-1]), found[-1]
        away = 1
        while True:
            moves = [(i, i ^ away) for i in range(n_cen)]
            other = lax.ppermute(stats, "cen", moves)
            away *= 2
            if away >= n_cen:
                return stats, other
            stats = merged(stats, other)

    def places(blocks):
        return jnp.stack([core, chip, *blocks]).astype(jnp.int32)

    far = places([lax.rem(chip + away, chips) for away in range(1, chips)])
    own_block, partner_block = places([me]), places([cores * chip + 1 - core])

    def sums_over_pts(by_rows, stats, tops, shifted):
        def weighted(parts, pos, after):
            return weigh(by_rows, parts, pos, stats, tops, shifted, pair, points, after)

        far_mine, far_theirs = weighted(cores, far, stats[0])
        far_found = to_partner(far_theirs)
        (near_theirs,) = weighted(1, partner_block, far_theirs)
        near_found = to_partner(near_theirs)
        coded = fold(far_mine, far_found, near_theirs)
        codes = [to_chip(coded[away - 1], away) for away in range(1, chips)]
        (near_mine,) = weighted(1, own_block, coded)
        return finish(by_rows, near_mine[0], near_found[0], codes)

    here = jnp.zeros((1,), jnp.int32)
    shifted, own = scores(fill_from_centroids, here, [centroids], points, rows)
    stats = over_centroids(own)
    tops, shifted = [own], [shifted]
    for _ in range(ITERS - 1):
        mine = sums_over_pts(True, stats, tops, shifted)
        away_units = [to_chip(mine, -away) for away in range(1, chips)]
        order = jnp.stack([core, 1 - core]).astype(jnp.int32)
        near_e, near_own = scores(fill_from_blocks, order, [mine, to_partner(mine)], points, pair)
        blocks = [unit for mine in away_units for unit in (mine, to_partner(mine))]
        order = jnp.stack([cores * i + place for i in range(chips - 1) for place in (core, 1 - core)])
        far_e, far_own = scores(
            fill_from_blocks, order.astype(jnp.int32), blocks, points, rows - pair
        )
        tops, shifted = [near_own, far_own], [near_e, far_e]
        stats = over_centroids(merged(near_own, far_own))
    means = sums_over_pts(False, stats, tops, shifted)
    return (means, log_norms(*stats))


def solution(mesh):
    placed = (P("pts", None), P("cen", None))
    return jax.shard_map(
        functools.partial(on_device, mesh.shape["pts"], mesh.shape["cen"]),
        mesh=mesh,
        in_specs=placed,
        out_specs=(P("cen", "pts"), P("pts")),
        check_vma=False,
    )
```

```python
import functools

import jax
import jax.numpy as jnp
from jax import lax
from jax.experimental import pallas as pl
from jax.experimental.pallas import tpu as pltpu
from jax.sharding import PartitionSpec as P

ITERS = 2
F32 = jnp.float32
BF16 = jnp.bfloat16
LOAD_VMEM = 38
SCORE_VMEM = 34
WEIGH_VMEM = 34
LEVELS = 30000.0
LOWEST = -117.0


def divisor(total, wanted):
    size = min(total, wanted)
    while total % size:
        size -= 1
    return size


def round_up(value, unit):
    return -(-value // unit) * unit


def normalize_rows(rows):
    return rows * lax.rsqrt(jnp.sum(rows * rows, axis=1, keepdims=True) + 1e-06)


CORES = 2


def place():
    me = lax.axis_index("pts")
    return lax.div(me, CORES), lax.rem(me, CORES)


def params(mebibytes):
    return pltpu.CompilerParams(vmem_limit_bytes=mebibytes * 2**20)


VMEM = pl.BlockSpec(memory_space=pltpu.VMEM)
ANY = pl.BlockSpec(memory_space=pl.ANY)


def merge(stats, other):
    top = jnp.maximum(stats[0], other[0])
    return top, stats[1] * jnp.exp(stats[0] - top) + other[1] * jnp.exp(other[0] - top)


def to_column(row, height):
    return jnp.broadcast_to(row, (128, height)).T


def encode(values, scale):
    steps = jnp.floor(jnp.abs(values) * (LEVELS / scale) + 0.5)
    power = jnp.floor(steps * (1.0 / 128.0))
    size = (1.0 + (steps * (1.0 / 128.0) - power)) * jnp.exp2(power + LOWEST)
    return jnp.where(values < 0.0, -size, size).astype(BF16)


def decode(codes, scale):
    wide = codes.astype(F32)
    size = jnp.abs(wide)
    power = jnp.floor(jnp.log2(size))
    steps = 128.0 * (power - LOWEST + (size * jnp.exp2(-power) - 1.0))
    return jnp.where(wide < 0.0, -steps, steps) * (scale * (1.0 / LEVELS))


def load_body(c_hbm, sums_ref, x_hbm, x_ref, units_ref, rows_ref, row_sems, point_sem):
    row_step = rows_ref.shape[0] // row_sems.shape[0]

    def rows_of(number):
        part = pl.ds(number * row_step, row_step)
        return pltpu.make_async_copy(c_hbm.at[part, :], rows_ref.at[part, :], row_sems.at[number])

    all_points = pltpu.make_async_copy(x_hbm, x_ref, point_sem)
    for number in range(row_sems.shape[0]):
        rows_of(number).start()
    all_points.start()
    for number in range(row_sems.shape[0]):
        rows_of(number).wait()
        part = slice(number * row_step, (number + 1) * row_step)
        scale = to_column(lax.rsqrt(sums_ref[:, part] + 1e-06), row_step)[:, 0:1]
        units_ref[part, :] = (rows_ref[part, :] * scale).astype(BF16)
    all_points.wait()


def load(centroids, points):
    square_sums = jnp.sum(centroids * centroids, axis=1)[None]
    return pl.pallas_call(
        load_body,
        in_specs=[ANY, VMEM, ANY],
        out_specs=[VMEM] * 2,
        out_shape=[
            jax.ShapeDtypeStruct(points.shape, BF16),
            jax.ShapeDtypeStruct(centroids.shape, BF16),
        ],
        scratch_shapes=[
            pltpu.VMEM(centroids.shape, F32),
            pltpu.SemaphoreType.DMA((divisor(centroids.shape[0] // 16, 4),)),
            pltpu.SemaphoreType.DMA(()),
        ],
        compiler_params=params(LOAD_VMEM),
        cost_estimate=pl.CostEstimate(
            flops=4 * centroids.size, bytes_accessed=4 * centroids.size + 2 * points.size, transcendentals=0
        ),
    )(centroids, square_sums, points)


def score_points(raw, units, x_ref, e_parts, stat_ref, stage, semaphores):
    line = stat_ref.shape[2]
    lines = stage.shape[0]
    sub = divisor(line, 256)

    def copies(number, slot):
        columns = pl.ds(pl.multiple_of(number * line, line), line)
        return [
            pltpu.make_async_copy(stage.at[slot, rows, :], target(columns), semaphores.at[slot, part])
            for part, (rows, target) in enumerate(e_parts)
        ]

    def visit(step, carry):
        for slot in range(lines):
            number = step * lines + slot

            @pl.when(step > 0)
            def _():
                for copy in copies(number - lines, slot):
                    copy.wait()

            tops, totals = [], []
            for offset in range(0, line, sub):
                logits = lax.dot_general(
                    units[...],
                    x_ref[pl.ds(pl.multiple_of(number * line + offset, sub), sub), :],
                    (((1,), (1,)), ((), ())),
                    preferred_element_type=F32,
                )
                top = jnp.max(logits, axis=0, keepdims=True)
                shifted = jnp.exp(logits - top)
                stage[slot, :, offset : offset + sub] = logits if raw else shifted
                tops.append(top)
                totals.append(jnp.sum(shifted, axis=0, keepdims=True))
            stat_ref[0, pl.ds(number, 1), :] = jnp.concatenate(tops, axis=1)
            stat_ref[1, pl.ds(number, 1), :] = jnp.concatenate(totals, axis=1)
            for copy in copies(number, slot):
                copy.start()
        return carry

    steps = stat_ref.shape[1] // lines
    lax.fori_loop(0, steps, visit, 0)
    for slot in range(lines):
        for copy in copies((steps - 1) * lines + slot, slot):
            copy.wait()


def stat_shape(total):
    line = divisor(total, 512)
    return (2, total // line, line)


def first_scores_body(raw, units, x_ref, _, e_hbm, stat_ref, stage, semaphores):
    target = [(slice(None), lambda columns: e_hbm.at[:, columns])]
    score_points(raw, units, x_ref, target, stat_ref, stage, semaphores)


def next_scores_body(raw, count, away, *refs):
    unit_refs = refs[:count]
    x_ref = refs[count]
    e_hbm, stat_ref, units, stage, semaphores = refs[-5:]
    rows = unit_refs[0].shape[0]
    pair = CORES * rows
    chip, core = place()
    chips = e_hbm.shape[0] // pair
    for number, ref in enumerate(unit_refs):
        of_pair = core if number % CORES == 0 else 1 - core
        start = pl.multiple_of((number - number % CORES + of_pair) * rows, rows)
        units[pl.ds(start, rows), :] = ref[...]

    def target_of(number):
        start = pl.multiple_of(lax.rem(chip + away + number, chips) * pair, pair)
        return lambda columns: e_hbm.at[pl.ds(start, pair), columns]

    targets = [
        (slice(number * pair, (number + 1) * pair), target_of(number)) for number in range(count // CORES)
    ]
    score_points(raw, units, x_ref, targets, stat_ref, stage, semaphores)


def scores(raw, blocks, points, away=None, shifted=None):
    total, width = points.shape
    count = len(blocks)
    rows = sum(block.shape[0] for block in blocks)
    all_rows = rows if shifted is None else shifted.shape[0]
    stat = stat_shape(total)
    parts = 1 if away is None else count // CORES
    more = [] if shifted is None or away == 0 else [shifted]
    scratch = [
        pltpu.VMEM((divisor(stat[1], 2), rows, stat[2]), F32),
        pltpu.SemaphoreType.DMA((divisor(stat[1], 2), parts)),
    ]
    if away is not None:
        scratch = [pltpu.VMEM((rows, width), BF16)] + scratch
    if away is None:
        body = functools.partial(first_scores_body, raw)
    else:
        body = functools.partial(next_scores_body, raw, count, away)
    return pl.pallas_call(
        body,
        in_specs=[VMEM] * (count + 1) + [ANY] * len(more),
        out_specs=[VMEM, ANY, VMEM],
        out_shape=[
            jax.ShapeDtypeStruct(points.shape, BF16),
            jax.ShapeDtypeStruct((all_rows, total), F32),
            jax.ShapeDtypeStruct(stat, F32),
        ],
        input_output_aliases={count + number: number for number in range(1 + len(more))},
        scratch_shapes=scratch,
        compiler_params=params(SCORE_VMEM),
        cost_estimate=pl.CostEstimate(
            flops=2 * rows * total * width,
            bytes_accessed=2 * total * width + 4 * rows * total,
            transcendentals=rows * total,
        ),
    )(*blocks, points, *more)


FAR, THEIRS, OWN = range(3)


def weigh_body(by_rows, n_tops, kind, others, extra, pair, stat_ref, more_ref, *refs):
    parts = CORES if kind == FAR else 1
    top_refs, (e_hbm, x_ref, _), refs = refs[:n_tops], refs[n_tops : n_tops + 3], refs[n_tops + 3 :]
    out_refs, refs = refs[:parts], refs[parts + 1 :]
    scale_refs, refs = refs[:2], refs[2:]
    weights_refs, (stage, mass_ref, sum_ref, semaphores) = refs[:2], refs[2:]
    chip, core = place()
    line = stat_ref.shape[2]
    total = x_ref.shape[0]
    height, span = sum_ref.shape
    slots, _, chunk = stage.shape
    steps = total // chunk
    lanes = min(line, 128)

    def block_of(other):
        if kind == FAR:
            return lax.rem(chip + 1 + other, others + 1)
        return chip * CORES + (core if kind == OWN else 1 - core)

    def copy_of(number):
        other, step = divmod(number, steps)
        rows = pl.ds(pl.multiple_of(block_of(other) * height, height), height) if by_rows else slice(None)
        columns = slice(step * chunk, (step + 1) * chunk)
        slot = number % slots
        return pltpu.make_async_copy(e_hbm.at[rows, columns], stage.at[slot], semaphores.at[slot])

    for number in range(min(slots, others * steps)):
        copy_of(number).start()
    top, all_total = merge(stat_ref, more_ref)
    if by_rows:
        scale_refs[0][...] = top
        scale_refs[1][...] = 1.0 / all_total
    else:
        for ref, scale_ref in zip((top_refs[0], top_refs[-1]), scale_refs):
            scale_ref[...] = jnp.exp(ref[0] - top) / all_total

    def weights_of(values, group, number):
        one, two = (ref[number : number + 1, :] for ref in scale_refs)
        if by_rows:
            return jnp.exp(values - one) * two
        return values * jnp.where(chip == group, one, two)

    group_rows = height if by_rows else pair
    for number in range(others * steps):
        other, step = divmod(number, steps)
        slot = number % slots
        weights_ref = weights_refs[step % 2]
        copy_of(number).wait()
        for group in range(height // group_rows):
            rows = slice(group * group_rows, (group + 1) * group_rows)
            mass = None
            for offset in range(0, chunk, line):
                values = stage[slot, rows, offset : offset + line]
                weights = weights_of(values, group, (step * chunk + offset) // line).astype(BF16)
                weights_ref[rows, offset : offset + line] = weights
                wide = weights.astype(F32)
                for lane in range(0, line, lanes):
                    piece = wide[:, lane : lane + lanes]
                    mass = piece if mass is None else mass + piece
            mass_ref[rows, :] = mass if step == 0 else mass_ref[rows, :] + mass
        if number + slots < others * steps:
            copy_of(number + slots).start()
        columns = slice(None)
        if not by_rows:
            columns = pl.ds(pl.multiple_of(block_of(other) * span, span), span)
        product = jnp.dot(
            weights_ref[...],
            x_ref[step * chunk : (step + 1) * chunk, columns],
            preferred_element_type=F32,
        )
        sum_ref[...] = product if step == 0 else sum_ref[...] + product
        if step < steps - 1:
            continue

        rows = out_refs[0].shape[1] - extra
        width = out_refs[0].shape[2]
        mass = jnp.sum(mass_ref[...].T, axis=0, keepdims=True)
        for part, ref in enumerate(out_refs):
            side = lax.rem(core + part, parts)
            ref[other, rows:, :] = jnp.zeros((extra, width), F32)
            if by_rows:
                found = mass
                if parts > 1:
                    found = jnp.where(side == 0, mass[:, :rows], mass[:, rows:])
                    ref[other, :rows, :] = sum_ref[pl.ds(pl.multiple_of(side * rows, rows), rows), :]
                else:
                    ref[other, :rows, :] = sum_ref[...]
                ref[other, rows : rows + 1, :rows] = found
            else:
                sums = sum_ref[...]
                if parts > 1:
                    sums = jnp.where(side == 0, sums[:, :width], sums[:, width:])
                ref[other, :rows, :] = sums
                for line_number in range(rows // width):
                    ref[other, rows + line_number : rows + line_number + 1, :] = mass[
                        :, line_number * width : (line_number + 1) * width
                    ]


def weigh(by_rows, kind, chips, stats, tops, shifted, points, after):
    total, width = points.shape
    pair = shifted.shape[0] // chips
    parts, others = (CORES, chips - 1) if kind == FAR else (1, 1)
    line = stats[0].shape[2]
    chunk = line * divisor(total // line, 2)
    if by_rows:
        rows, cols = pair // CORES, width
        sums = (rows * parts, width)
    else:
        rows, cols = shifted.shape[0], width // (CORES * chips)
        sums = (rows, cols * parts)
    n_tops = len(tops)
    extra = round_up(-(-rows // cols), 8)
    return pl.pallas_call(
        functools.partial(weigh_body, by_rows, n_tops, kind, others, extra, pair),
        in_specs=[VMEM] * (2 + n_tops) + [ANY, VMEM, ANY],
        out_specs=[VMEM] * (parts + 1),
        input_output_aliases={3 + n_tops: parts},
        scratch_shapes=[pltpu.VMEM(stats[0].shape[1:], F32)] * 2
        + [pltpu.VMEM((sums[0], chunk), BF16)] * 2
        + [
            pltpu.VMEM((2, sums[0], chunk), F32),
            pltpu.VMEM((sums[0], 128), F32),
            pltpu.VMEM(sums, F32),
            pltpu.SemaphoreType.DMA((2,)),
        ],
        out_shape=[jax.ShapeDtypeStruct((others, rows + extra, cols), F32)] * parts
        + [jax.ShapeDtypeStruct(points.shape, BF16)],
        compiler_params=params(WEIGH_VMEM),
        cost_estimate=pl.CostEstimate(
            flops=2 * others * sums[0] * sums[1] * total,
            bytes_accessed=2 * others * total * (sums[1] + 2 * sums[0]),
            transcendentals=0,
        ),
    )(*stats, *tops, shifted, points, after)


def fold_body(rows, lines, mine_ref, theirs_ref, after_ref, out_ref):
    width = out_ref.shape[1]
    step = divisor(rows, 128) if lines == 1 else width
    out_ref[rows:, :] = jnp.zeros((out_ref.shape[0] - rows, width), BF16)
    scales = []
    for start in range(0, rows, step):
        part = slice(start, start + step)
        total = mine_ref[part, :] + theirs_ref[part, :]
        top = jnp.max(jnp.abs(total), axis=1, keepdims=True)
        scale = jnp.maximum(top * 1.01, 1e-30).astype(BF16)
        out_ref[part, :] = encode(total, scale.astype(F32))
        scales.append(jnp.broadcast_to(scale.astype(F32), (step, 128)).T[0:1, :])
    mass = mine_ref[rows : rows + lines, :] + theirs_ref[rows : rows + lines, :]
    if lines == 1:
        out_ref[rows : rows + 1, :rows] = jnp.concatenate(scales, axis=1).astype(BF16)
    else:
        out_ref[rows : rows + lines, :] = jnp.concatenate(scales, axis=0).astype(BF16)
    for number in range(1, 4):
        rounded = mass.astype(BF16)
        out_ref[rows + number * lines : rows + (number + 1) * lines, :] = rounded
        mass = mass - rounded.astype(F32)


def fold(mine, theirs, after):
    others, height, width = mine.shape
    out_height = coded_height(height, width)
    return pl.pallas_call(
        functools.partial(fold_body, *shape_of(height, width)),
        grid=(others,),
        in_specs=[pl.BlockSpec((None, height, width), lambda d: (d, 0, 0))] * 2 + [ANY],
        out_specs=pl.BlockSpec((None, out_height, width), lambda d: (d, 0, 0)),
        out_shape=jax.ShapeDtypeStruct((others, out_height, width), BF16),
        compiler_params=params(10),
        cost_estimate=pl.CostEstimate(
            flops=20 * others * height * width,
            bytes_accessed=10 * others * height * width,
            transcendentals=others * height * width,
        ),
    )(mine, theirs, after)


def shape_of(height, width):
    rows = height - 8
    while rows + round_up(-(-rows // width), 8) != height:
        rows -= 8
    return rows, -(-rows // width)


def coded_height(height, width):
    rows, lines = shape_of(height, width)
    return rows + round_up(4 * lines, 16)


def finish_body(rows, lines, as_units, mine_ref, theirs_ref, *refs):
    code_refs, out_ref = refs[:-1], refs[-1]
    width = out_ref.shape[1]
    step = divisor(rows, 128) if lines == 1 else width
    mass = mine_ref[rows : rows + lines, :] + theirs_ref[rows : rows + lines, :]
    for ref in code_refs:
        for number in range(1, 4):
            start = rows + number * lines
            mass = mass + ref[start : start + lines, :].astype(F32)

    def column(values, number):
        if lines == 1:
            line = values[:, number * step : (number + 1) * step]
        else:
            line = values[number : number + 1, :]
        return to_column(line, step)[:, 0:1]

    scales = [ref[rows : rows + lines, :].astype(F32) for ref in code_refs]
    for number in range(rows // step):
        part = slice(number * step, (number + 1) * step)
        total = mine_ref[part, :] + theirs_ref[part, :]
        for ref, scale in zip(code_refs, scales):
            total = total + decode(ref[part, :], column(scale, number))
        means = total / jnp.maximum(column(mass, number), 1.0)
        out_ref[part, :] = normalize_rows(means).astype(BF16) if as_units else means


def finish(as_units, mine, theirs, codes):
    height, width = mine.shape
    rows, lines = shape_of(height, width)
    out_type = BF16 if as_units else F32
    return pl.pallas_call(
        functools.partial(finish_body, rows, lines, as_units),
        out_shape=jax.ShapeDtypeStruct((rows, width), out_type),
        compiler_params=params(10),
        cost_estimate=pl.CostEstimate(
            flops=30 * rows * width,
            bytes_accessed=(12 + 2 * len(codes)) * rows * width,
            transcendentals=2 * rows * width,
        ),
    )(mine, theirs, *codes)


def keep_body(value_ref, after_ref, out_ref):
    pass


def keep_until(value, after):
    return pl.pallas_call(
        keep_body,
        in_specs=[VMEM, ANY],
        out_specs=VMEM,
        out_shape=jax.ShapeDtypeStruct(value.shape, value.dtype),
        input_output_aliases={0: 0},
        compiler_params=params(10),
    )(value, after)


def merge_body(one_ref, two_ref, out_ref):
    out_ref[0], out_ref[1] = merge(one_ref, two_ref)


def merged(one, two):
    return pl.pallas_call(
        merge_body, out_shape=jax.ShapeDtypeStruct(one.shape, F32), compiler_params=params(10)
    )(one, two)


def log_body(one_ref, two_ref, out_ref):
    top, total = merge(one_ref, two_ref)
    out_ref[...] = top + jnp.log(total)


def log_norms(one, two):
    return pl.pallas_call(
        log_body, out_shape=jax.ShapeDtypeStruct(one.shape[1:], F32), compiler_params=params(10)
    )(one, two).reshape(-1)


def on_device(n_pts, n_cen, points, centroids):
    chips = n_pts // CORES

    def to_partner(value):
        return lax.ppermute(value, "pts", [(i, i ^ 1) for i in range(n_pts)])

    def to_chip(value, away):
        moves = [(i, (i + CORES * away) % n_pts) for i in range(n_pts)]
        return lax.ppermute(value, "pts", moves)

    def over_centroids(stats):
        if n_cen & (n_cen - 1):
            found = [stats]
            for away in range(1, n_cen):
                moves = [(i, (i + away) % n_cen) for i in range(n_cen)]
                found.append(lax.ppermute(stats, "cen", moves))
            return functools.reduce(merged, found[:-1]), found[-1]
        away = 1
        while True:
            moves = [(i, i ^ away) for i in range(n_cen)]
            other = lax.ppermute(stats, "cen", moves)
            away *= 2
            if away >= n_cen:
                return stats, other
            stats = merged(stats, other)

    def sums_over_pts(by_rows, stats, tops, shifted, points):
        def weighted(kind, after):
            nonlocal points
            *found, points = weigh(by_rows, kind, chips, stats, tops, shifted, points, after)
            return found

        far_mine, far_theirs = weighted(FAR, stats[0])
        far_found = to_partner(far_theirs)
        (near_theirs,) = weighted(THEIRS, far_theirs)
        near_found = to_partner(near_theirs)
        coded = fold(far_mine, far_found, near_theirs)
        codes = [to_chip(coded[away - 1], away) for away in range(1, chips)]
        (near_mine,) = weighted(OWN, coded)
        return finish(by_rows, near_mine[0], near_found[0], codes), points

    points, units = load(centroids, points)
    points, shifted, own = scores(ITERS > 1, [units], points)
    stats = over_centroids(own)
    tops = [own]
    for iteration in range(1, ITERS):
        raw = iteration + 1 < ITERS
        mine, points = sums_over_pts(True, stats, tops, shifted, points)
        away_units = [to_chip(mine, -away) for away in range(1, chips)]
        points, shifted, near_own = scores(raw, [mine, to_partner(mine)], points, 0, shifted)
        away_units = [keep_until(unit, near_own) for unit in away_units]
        blocks = [unit for mine in away_units for unit in (mine, to_partner(mine))]
        points, shifted, far_own = scores(raw, blocks, points, 1, shifted)
        tops = [near_own, far_own]
        stats = over_centroids(merged(near_own, far_own))
    means, _ = sums_over_pts(False, stats, tops, shifted, points)
    return (means, log_norms(*stats))


def solution(mesh):
    placed = (P("pts", None), P("cen", None))
    return jax.shard_map(
        functools.partial(on_device, mesh.shape["pts"], mesh.shape["cen"]),
        mesh=mesh,
        in_specs=placed,
        out_specs=(P("cen", "pts"), P("pts")),
        check_vma=False,
    )
```

```python
import functools

import jax
import jax.numpy as jnp
from jax import lax
from jax.experimental import pallas as pl
from jax.experimental.pallas import tpu as pltpu
from jax.sharding import PartitionSpec as P

ITERS = 2
F32 = jnp.float32
BF16 = jnp.bfloat16
LOAD_VMEM = 38
SCORE_VMEM = 34
WEIGH_VMEM = 34
LEVELS = 30000.0
LOWEST = -117.0


def divisor(total, wanted):
    size = min(total, wanted)
    while total % size:
        size -= 1
    return size


def round_up(value, unit):
    return -(-value // unit) * unit


def normalize_rows(rows):
    return rows * lax.rsqrt(jnp.sum(rows * rows, axis=1, keepdims=True) + 1e-06)


CORES = 2


def place():
    me = lax.axis_index("pts")
    return lax.div(me, CORES), lax.rem(me, CORES)


def params(mebibytes):
    return pltpu.CompilerParams(vmem_limit_bytes=mebibytes * 2**20)


VMEM = pl.BlockSpec(memory_space=pltpu.VMEM)
ANY = pl.BlockSpec(memory_space=pl.ANY)


def merge(found):
    found = list(found)
    top = functools.reduce(jnp.maximum, [stats[0] for stats in found])
    total = functools.reduce(jnp.add, [stats[1] * jnp.exp(stats[0] - top) for stats in found])
    return top, total


def split(ref):
    return [(ref[i, 0], ref[i, 1]) for i in range(ref.shape[0])]


def to_column(row, height):
    return jnp.broadcast_to(row, (128, height)).T


def encode(values, scale):
    steps = jnp.floor(jnp.abs(values) * (LEVELS / scale) + 0.5)
    power = jnp.floor(steps * (1.0 / 128.0))
    size = (1.0 + (steps * (1.0 / 128.0) - power)) * jnp.exp2(power + LOWEST)
    return jnp.where(values < 0.0, -size, size).astype(BF16)


def decode(codes, scale):
    wide = codes.astype(F32)
    size = jnp.abs(wide)
    power = jnp.floor(jnp.log2(size))
    steps = 128.0 * (power - LOWEST + (size * jnp.exp2(-power) - 1.0))
    return jnp.where(wide < 0.0, -steps, steps) * (scale * (1.0 / LEVELS))


def load_body(c_hbm, sums_ref, x_hbm, x_ref, units_ref, rows_ref, row_sems, point_sem):
    row_step = rows_ref.shape[0] // row_sems.shape[0]

    def rows_of(number):
        part = pl.ds(number * row_step, row_step)
        return pltpu.make_async_copy(c_hbm.at[part, :], rows_ref.at[part, :], row_sems.at[number])

    all_points = pltpu.make_async_copy(x_hbm, x_ref, point_sem)
    for number in range(row_sems.shape[0]):
        rows_of(number).start()
    all_points.start()
    for number in range(row_sems.shape[0]):
        rows_of(number).wait()
        part = slice(number * row_step, (number + 1) * row_step)
        scale = to_column(lax.rsqrt(sums_ref[:, part] + 1e-06), row_step)[:, 0:1]
        units_ref[part, :] = (rows_ref[part, :] * scale).astype(BF16)
    all_points.wait()


def load(centroids, points):
    square_sums = jnp.sum(centroids * centroids, axis=1)[None]
    return pl.pallas_call(
        load_body,
        in_specs=[ANY, VMEM, ANY],
        out_specs=[VMEM] * 2,
        out_shape=[
            jax.ShapeDtypeStruct(points.shape, BF16),
            jax.ShapeDtypeStruct(centroids.shape, BF16),
        ],
        scratch_shapes=[
            pltpu.VMEM(centroids.shape, F32),
            pltpu.SemaphoreType.DMA((divisor(centroids.shape[0] // 16, 4),)),
            pltpu.SemaphoreType.DMA(()),
        ],
        compiler_params=params(LOAD_VMEM),
        cost_estimate=pl.CostEstimate(
            flops=4 * centroids.size, bytes_accessed=4 * centroids.size + 2 * points.size, transcendentals=0
        ),
    )(centroids, square_sums, points)


def score_points(raw, units, x_ref, e_parts, stat_ref, stage, semaphores):
    line = stat_ref.shape[2]
    lines = stage.shape[0]
    sub = divisor(line, 256)

    def copies(number, slot):
        columns = pl.ds(pl.multiple_of(number * line, line), line)
        return [
            pltpu.make_async_copy(stage.at[slot, rows, :], target(columns), semaphores.at[slot, part])
            for part, (rows, target) in enumerate(e_parts)
        ]

    def visit(step, carry):
        for slot in range(lines):
            number = step * lines + slot

            @pl.when(step > 0)
            def _():
                for copy in copies(number - lines, slot):
                    copy.wait()

            tops, totals = [], []
            for offset in range(0, line, sub):
                logits = lax.dot_general(
                    units[...],
                    x_ref[pl.ds(pl.multiple_of(number * line + offset, sub), sub), :],
                    (((1,), (1,)), ((), ())),
                    preferred_element_type=F32,
                )
                top = jnp.max(logits, axis=0, keepdims=True)
                shifted = jnp.exp(logits - top)
                stage[slot, :, offset : offset + sub] = logits if raw else shifted
                tops.append(top)
                totals.append(jnp.sum(shifted, axis=0, keepdims=True))
            stat_ref[0, pl.ds(number, 1), :] = jnp.concatenate(tops, axis=1)
            stat_ref[1, pl.ds(number, 1), :] = jnp.concatenate(totals, axis=1)
            for copy in copies(number, slot):
                copy.start()
        return carry

    steps = stat_ref.shape[1] // lines
    lax.fori_loop(0, steps, visit, 0)
    for slot in range(lines):
        for copy in copies((steps - 1) * lines + slot, slot):
            copy.wait()


def stat_shape(total):
    line = divisor(total, 512)
    return (2, total // line, line)


def first_scores_body(raw, units, x_ref, _, e_hbm, stat_ref, stage, semaphores):
    target = [(slice(None), lambda columns: e_hbm.at[:, columns])]
    score_points(raw, units, x_ref, target, stat_ref, stage, semaphores)


def next_scores_body(raw, count, away, *refs):
    unit_refs = refs[:count]
    x_ref = refs[count]
    e_hbm, stat_ref, units, stage, semaphores = refs[-5:]
    rows = unit_refs[0].shape[0]
    pair = CORES * rows
    chip, core = place()
    chips = e_hbm.shape[0] // pair
    for number, ref in enumerate(unit_refs):
        of_pair = core if number % CORES == 0 else 1 - core
        start = pl.multiple_of((number - number % CORES + of_pair) * rows, rows)
        units[pl.ds(start, rows), :] = ref[...]

    def target_of(number):
        start = pl.multiple_of(lax.rem(chip + away + number, chips) * pair, pair)
        return lambda columns: e_hbm.at[pl.ds(start, pair), columns]

    targets = [
        (slice(number * pair, (number + 1) * pair), target_of(number)) for number in range(count // CORES)
    ]
    score_points(raw, units, x_ref, targets, stat_ref, stage, semaphores)


def scores(raw, blocks, points, away=None, shifted=None):
    total, width = points.shape
    count = len(blocks)
    rows = sum(block.shape[0] for block in blocks)
    all_rows = rows if shifted is None else shifted.shape[0]
    stat = stat_shape(total)
    parts = 1 if away is None else count // CORES
    more = [] if shifted is None or away == 0 else [shifted]
    scratch = [
        pltpu.VMEM((divisor(stat[1], 2), rows, stat[2]), F32),
        pltpu.SemaphoreType.DMA((divisor(stat[1], 2), parts)),
    ]
    if away is not None:
        scratch = [pltpu.VMEM((rows, width), BF16)] + scratch
    if away is None:
        body = functools.partial(first_scores_body, raw)
    else:
        body = functools.partial(next_scores_body, raw, count, away)
    return pl.pallas_call(
        body,
        in_specs=[VMEM] * (count + 1) + [ANY] * len(more),
        out_specs=[VMEM, ANY, VMEM],
        out_shape=[
            jax.ShapeDtypeStruct(points.shape, BF16),
            jax.ShapeDtypeStruct((all_rows, total), F32),
            jax.ShapeDtypeStruct(stat, F32),
        ],
        input_output_aliases={count + number: number for number in range(1 + len(more))},
        scratch_shapes=scratch,
        compiler_params=params(SCORE_VMEM),
        cost_estimate=pl.CostEstimate(
            flops=2 * rows * total * width,
            bytes_accessed=2 * total * width + 4 * rows * total,
            transcendentals=rows * total,
        ),
    )(*blocks, points, *more)


FAR, THEIRS, OWN = range(3)


def weigh_body(by_rows, n_tops, kind, others, extra, pair, stat_ref, *refs):
    parts = CORES if kind == FAR else 1
    top_refs, (e_hbm, x_ref, _), refs = refs[:n_tops], refs[n_tops : n_tops + 3], refs[n_tops + 3 :]
    out_refs, refs = refs[:parts], refs[parts + 1 :]
    scale_refs, refs = refs[:2], refs[2:]
    weights_refs, (stage, mass_ref, sum_ref, semaphores) = refs[:2], refs[2:]
    chip, core = place()
    line = stat_ref.shape[3]
    total = x_ref.shape[0]
    height, span = sum_ref.shape
    slots, _, chunk = stage.shape
    steps = total // chunk
    lanes = min(line, 128)

    def block_of(other):
        if kind == FAR:
            return lax.rem(chip + 1 + other, others + 1)
        return chip * CORES + (core if kind == OWN else 1 - core)

    def copy_of(number):
        other, step = divmod(number, steps)
        rows = pl.ds(pl.multiple_of(block_of(other) * height, height), height) if by_rows else slice(None)
        columns = slice(step * chunk, (step + 1) * chunk)
        slot = number % slots
        return pltpu.make_async_copy(e_hbm.at[rows, columns], stage.at[slot], semaphores.at[slot])

    for number in range(min(slots, others * steps)):
        copy_of(number).start()
    top, all_total = merge(split(stat_ref))
    if by_rows:
        scale_refs[0][...] = top
        scale_refs[1][...] = 1.0 / all_total
    else:
        for ref, scale_ref in zip((top_refs[0], top_refs[-1]), scale_refs):
            scale_ref[...] = jnp.exp(ref[0] - top) / all_total

    def weights_of(values, group, number):
        one, two = (ref[number : number + 1, :] for ref in scale_refs)
        if by_rows:
            return jnp.exp(values - one) * two
        return values * jnp.where(chip == group, one, two)

    group_rows = height if by_rows else pair
    for number in range(others * steps):
        other, step = divmod(number, steps)
        slot = number % slots
        weights_ref = weights_refs[step % 2]
        copy_of(number).wait()
        for group in range(height // group_rows):
            rows = slice(group * group_rows, (group + 1) * group_rows)
            mass = None
            for offset in range(0, chunk, line):
                values = stage[slot, rows, offset : offset + line]
                weights = weights_of(values, group, (step * chunk + offset) // line).astype(BF16)
                weights_ref[rows, offset : offset + line] = weights
                wide = weights.astype(F32)
                for lane in range(0, line, lanes):
                    piece = wide[:, lane : lane + lanes]
                    mass = piece if mass is None else mass + piece
            mass_ref[rows, :] = mass if step == 0 else mass_ref[rows, :] + mass
        if number + slots < others * steps:
            copy_of(number + slots).start()
        columns = slice(None)
        if not by_rows:
            columns = pl.ds(pl.multiple_of(block_of(other) * span, span), span)
        product = jnp.dot(
            weights_ref[...],
            x_ref[step * chunk : (step + 1) * chunk, columns],
            preferred_element_type=F32,
        )
        sum_ref[...] = product if step == 0 else sum_ref[...] + product
        if step < steps - 1:
            continue

        rows = out_refs[0].shape[1] - extra
        width = out_refs[0].shape[2]
        mass = jnp.sum(mass_ref[...].T, axis=0, keepdims=True)
        for part, ref in enumerate(out_refs):
            side = lax.rem(core + part, parts)
            ref[other, rows:, :] = jnp.zeros((extra, width), F32)
            if by_rows:
                found = mass
                if parts > 1:
                    found = jnp.where(side == 0, mass[:, :rows], mass[:, rows:])
                    ref[other, :rows, :] = sum_ref[pl.ds(pl.multiple_of(side * rows, rows), rows), :]
                else:
                    ref[other, :rows, :] = sum_ref[...]
                ref[other, rows : rows + 1, :rows] = found
            else:
                sums = sum_ref[...]
                if parts > 1:
                    sums = jnp.where(side == 0, sums[:, :width], sums[:, width:])
                ref[other, :rows, :] = sums
                for line_number in range(rows // width):
                    ref[other, rows + line_number : rows + line_number + 1, :] = mass[
                        :, line_number * width : (line_number + 1) * width
                    ]


def weigh(by_rows, kind, chips, stats, tops, shifted, points, after):
    total, width = points.shape
    pair = shifted.shape[0] // chips
    parts, others = (CORES, chips - 1) if kind == FAR else (1, 1)
    line = stats.shape[3]
    chunk = line * divisor(total // line, 2)
    if by_rows:
        rows, cols = pair // CORES, width
        sums = (rows * parts, width)
    else:
        rows, cols = shifted.shape[0], width // (CORES * chips)
        sums = (rows, cols * parts)
    n_tops = len(tops)
    extra = round_up(-(-rows // cols), 8)
    return pl.pallas_call(
        functools.partial(weigh_body, by_rows, n_tops, kind, others, extra, pair),
        in_specs=[VMEM] * (1 + n_tops) + [ANY, VMEM, ANY],
        out_specs=[VMEM] * (parts + 1),
        input_output_aliases={2 + n_tops: parts},
        scratch_shapes=[pltpu.VMEM(stats.shape[2:], F32)] * 2
        + [pltpu.VMEM((sums[0], chunk), BF16)] * 2
        + [
            pltpu.VMEM((2, sums[0], chunk), F32),
            pltpu.VMEM((sums[0], 128), F32),
            pltpu.VMEM(sums, F32),
            pltpu.SemaphoreType.DMA((2,)),
        ],
        out_shape=[jax.ShapeDtypeStruct((others, rows + extra, cols), F32)] * parts
        + [jax.ShapeDtypeStruct(points.shape, BF16)],
        compiler_params=params(WEIGH_VMEM),
        cost_estimate=pl.CostEstimate(
            flops=2 * others * sums[0] * sums[1] * total,
            bytes_accessed=2 * others * total * (sums[1] + 2 * sums[0]),
            transcendentals=0,
        ),
    )(stats, *tops, shifted, points, after)


def fold_body(rows, lines, mine_ref, theirs_ref, after_ref, out_ref):
    width = out_ref.shape[1]
    step = divisor(rows, 128) if lines == 1 else width
    out_ref[rows:, :] = jnp.zeros((out_ref.shape[0] - rows, width), BF16)
    scales = []
    for start in range(0, rows, step):
        part = slice(start, start + step)
        total = mine_ref[part, :] + theirs_ref[part, :]
        top = jnp.max(jnp.abs(total), axis=1, keepdims=True)
        scale = jnp.maximum(top * 1.01, 1e-30).astype(BF16)
        out_ref[part, :] = encode(total, scale.astype(F32))
        scales.append(jnp.broadcast_to(scale.astype(F32), (step, 128)).T[0:1, :])
    mass = mine_ref[rows : rows + lines, :] + theirs_ref[rows : rows + lines, :]
    if lines == 1:
        out_ref[rows : rows + 1, :rows] = jnp.concatenate(scales, axis=1).astype(BF16)
    else:
        out_ref[rows : rows + lines, :] = jnp.concatenate(scales, axis=0).astype(BF16)
    for number in range(1, 4):
        rounded = mass.astype(BF16)
        out_ref[rows + number * lines : rows + (number + 1) * lines, :] = rounded
        mass = mass - rounded.astype(F32)


def fold(mine, theirs, after):
    others, height, width = mine.shape
    out_height = coded_height(height, width)
    return pl.pallas_call(
        functools.partial(fold_body, *shape_of(height, width)),
        grid=(others,),
        in_specs=[pl.BlockSpec((None, height, width), lambda d: (d, 0, 0))] * 2 + [ANY],
        out_specs=pl.BlockSpec((None, out_height, width), lambda d: (d, 0, 0)),
        out_shape=jax.ShapeDtypeStruct((others, out_height, width), BF16),
        compiler_params=params(10),
        cost_estimate=pl.CostEstimate(
            flops=20 * others * height * width,
            bytes_accessed=10 * others * height * width,
            transcendentals=others * height * width,
        ),
    )(mine, theirs, after)


def shape_of(height, width):
    rows = height - 8
    while rows + round_up(-(-rows // width), 8) != height:
        rows -= 8
    return rows, -(-rows // width)


def coded_height(height, width):
    rows, lines = shape_of(height, width)
    return rows + round_up(4 * lines, 16)


def finish_body(rows, lines, as_units, mine_ref, theirs_ref, *refs):
    code_refs, out_ref = refs[:-1], refs[-1]
    width = out_ref.shape[1]
    step = divisor(rows, 128) if lines == 1 else width
    mass = mine_ref[rows : rows + lines, :] + theirs_ref[rows : rows + lines, :]
    for ref in code_refs:
        for number in range(1, 4):
            start = rows + number * lines
            mass = mass + ref[start : start + lines, :].astype(F32)

    def column(values, number):
        if lines == 1:
            line = values[:, number * step : (number + 1) * step]
        else:
            line = values[number : number + 1, :]
        return to_column(line, step)[:, 0:1]

    scales = [ref[rows : rows + lines, :].astype(F32) for ref in code_refs]
    for number in range(rows // step):
        part = slice(number * step, (number + 1) * step)
        total = mine_ref[part, :] + theirs_ref[part, :]
        for ref, scale in zip(code_refs, scales):
            total = total + decode(ref[part, :], column(scale, number))
        means = total / jnp.maximum(column(mass, number), 1.0)
        out_ref[part, :] = normalize_rows(means).astype(BF16) if as_units else means


def finish(as_units, mine, theirs, codes):
    height, width = mine.shape
    rows, lines = shape_of(height, width)
    out_type = BF16 if as_units else F32
    return pl.pallas_call(
        functools.partial(finish_body, rows, lines, as_units),
        out_shape=jax.ShapeDtypeStruct((rows, width), out_type),
        compiler_params=params(10),
        cost_estimate=pl.CostEstimate(
            flops=30 * rows * width,
            bytes_accessed=(12 + 2 * len(codes)) * rows * width,
            transcendentals=2 * rows * width,
        ),
    )(mine, theirs, *codes)


def keep_body(value_ref, after_ref, out_ref):
    pass


def keep_until(value, after):
    return pl.pallas_call(
        keep_body,
        in_specs=[VMEM, ANY],
        out_specs=VMEM,
        out_shape=jax.ShapeDtypeStruct(value.shape, value.dtype),
        input_output_aliases={0: 0},
        compiler_params=params(10),
    )(value, after)


def merge_body(one_ref, two_ref, out_ref):
    out_ref[0], out_ref[1] = merge([one_ref, two_ref])


def merged(one, two):
    return pl.pallas_call(
        merge_body, out_shape=jax.ShapeDtypeStruct(one.shape, F32), compiler_params=params(10)
    )(one, two)


def log_body(stats_ref, out_ref):
    top, total = merge(split(stats_ref))
    out_ref[...] = top + jnp.log(total)


def log_norms(stats):
    return pl.pallas_call(
        log_body, out_shape=jax.ShapeDtypeStruct(stats.shape[2:], F32), compiler_params=params(10)
    )(stats).reshape(-1)


def on_device(n_pts, n_cen, points, centroids):
    chips = n_pts // CORES

    def to_partner(value):
        return lax.ppermute(value, "pts", [(i, i ^ 1) for i in range(n_pts)])

    def to_chip(value, away):
        moves = [(i, (i + CORES * away) % n_pts) for i in range(n_pts)]
        return lax.ppermute(value, "pts", moves)

    def over_centroids(stats):
        return lax.all_to_all(jnp.broadcast_to(stats[None], (n_cen, *stats.shape)), "cen", 0, 0)

    def sums_over_pts(by_rows, stats, tops, shifted, points):
        def weighted(kind, after):
            nonlocal points
            *found, points = weigh(by_rows, kind, chips, stats, tops, shifted, points, after)
            return found

        far_mine, far_theirs = weighted(FAR, stats)
        far_found = to_partner(far_theirs)
        (near_theirs,) = weighted(THEIRS, far_theirs)
        near_found = to_partner(near_theirs)
        coded = fold(far_mine, far_found, near_theirs)
        codes = [to_chip(coded[away - 1], away) for away in range(1, chips)]
        (near_mine,) = weighted(OWN, coded)
        return finish(by_rows, near_mine[0], near_found[0], codes), points

    points, units = load(centroids, points)
    points, shifted, own = scores(ITERS > 1, [units], points)
    stats = over_centroids(own)
    tops = [own]
    for iteration in range(1, ITERS):
        raw = iteration + 1 < ITERS
        mine, points = sums_over_pts(True, stats, tops, shifted, points)
        away_units = [to_chip(mine, -away) for away in range(1, chips)]
        points, shifted, near_own = scores(raw, [mine, to_partner(mine)], points, 0, shifted)
        away_units = [keep_until(unit, near_own) for unit in away_units]
        blocks = [unit for mine in away_units for unit in (mine, to_partner(mine))]
        points, shifted, far_own = scores(raw, blocks, points, 1, shifted)
        tops = [near_own, far_own]
        stats = over_centroids(merged(near_own, far_own))
    means, _ = sums_over_pts(False, stats, tops, shifted, points)
    return (means, log_norms(stats))


def solution(mesh):
    placed = (P("pts", None), P("cen", None))
    return jax.shard_map(
        functools.partial(on_device, mesh.shape["pts"], mesh.shape["cen"]),
        mesh=mesh,
        in_specs=placed,
        out_specs=(P("cen", "pts"), P("pts")),
        check_vma=False,
    )
```

```python
import functools

import jax
import jax.numpy as jnp
from jax import lax
from jax.experimental import pallas as pl
from jax.experimental.pallas import tpu as pltpu
from jax.sharding import PartitionSpec as P

ITERS = 2
F32 = jnp.float32
BF16 = jnp.bfloat16
LOAD_VMEM = 38
SCORE_VMEM = 34
WEIGH_VMEM = 34
KEPT_VMEM = 20
SLOTS = 4
CHUNK_LINES = 2
WEIGH_SLOTS = 3
LEVELS = 30000.0
LOWEST = -117.0


def divisor(total, wanted):
    size = min(total, wanted)
    while total % size:
        size -= 1
    return size


def round_up(value, unit):
    return -(-value // unit) * unit


def normalize_rows(rows):
    return rows * lax.rsqrt(jnp.sum(rows * rows, axis=1, keepdims=True) + 1e-06)


CORES = 2


def place():
    me = lax.axis_index("pts")
    return lax.div(me, CORES), lax.rem(me, CORES)


def params(mebibytes):
    return pltpu.CompilerParams(vmem_limit_bytes=mebibytes * 2**20)


VMEM = pl.BlockSpec(memory_space=pltpu.VMEM)
ANY = pl.BlockSpec(memory_space=pl.ANY)


def merge(stats, other):
    top = jnp.maximum(stats[0], other[0])
    return top, stats[1] * jnp.exp(stats[0] - top) + other[1] * jnp.exp(other[0] - top)


def to_column(row, height):
    return jnp.broadcast_to(row, (128, height)).T


def encode(values, scale):
    steps = jnp.floor(jnp.abs(values) * (LEVELS / scale) + 0.5)
    power = jnp.floor(steps * (1.0 / 128.0))
    size = (1.0 + (steps * (1.0 / 128.0) - power)) * jnp.exp2(power + LOWEST)
    return jnp.where(values < 0.0, -size, size).astype(BF16)


def decode(codes, scale):
    wide = codes.astype(F32)
    size = jnp.abs(wide)
    power = jnp.floor(jnp.log2(size))
    steps = 128.0 * (power - LOWEST + (size * jnp.exp2(-power) - 1.0))
    return jnp.where(wide < 0.0, -steps, steps) * (scale * (1.0 / LEVELS))


def load_body(c_hbm, sums_ref, x_hbm, x_ref, units_ref, rows_ref, row_sems, point_sem):
    row_step = rows_ref.shape[0] // row_sems.shape[0]

    def rows_of(number):
        part = pl.ds(number * row_step, row_step)
        return pltpu.make_async_copy(c_hbm.at[part, :], rows_ref.at[part, :], row_sems.at[number])

    all_points = pltpu.make_async_copy(x_hbm, x_ref, point_sem)
    for number in range(row_sems.shape[0]):
        rows_of(number).start()
    all_points.start()
    for number in range(row_sems.shape[0]):
        rows_of(number).wait()
        part = slice(number * row_step, (number + 1) * row_step)
        scale = to_column(lax.rsqrt(sums_ref[:, part] + 1e-06), row_step)[:, 0:1]
        units_ref[part, :] = (rows_ref[part, :] * scale).astype(BF16)
    all_points.wait()


def load(centroids, points):
    square_sums = jnp.sum(centroids * centroids, axis=1)[None]
    return pl.pallas_call(
        load_body,
        in_specs=[ANY, VMEM, ANY],
        out_specs=[VMEM] * 2,
        out_shape=[
            jax.ShapeDtypeStruct(points.shape, BF16),
            jax.ShapeDtypeStruct(centroids.shape, BF16),
        ],
        scratch_shapes=[
            pltpu.VMEM(centroids.shape, F32),
            pltpu.SemaphoreType.DMA((divisor(centroids.shape[0] // 16, 4),)),
            pltpu.SemaphoreType.DMA(()),
        ],
        compiler_params=params(LOAD_VMEM),
        cost_estimate=pl.CostEstimate(
            flops=4 * centroids.size, bytes_accessed=4 * centroids.size + 2 * points.size, transcendentals=0
        ),
    )(centroids, square_sums, points)


def score_points(raw, units, x_ref, e_parts, stat_ref, stage, semaphores):
    line = stat_ref.shape[2]
    slots, _, sub = stage.shape
    count = x_ref.shape[0] // sub

    def copies(number):
        columns = slice(number * sub, (number + 1) * sub)
        slot = number % slots
        return [
            pltpu.make_async_copy(stage.at[slot, rows, :], target(columns), semaphores.at[slot, part])
            for part, (rows, target) in enumerate(e_parts)
        ]

    def multiply(number):
        stage[number % slots] = lax.dot_general(
            units[...],
            x_ref[number * sub : (number + 1) * sub, :],
            (((1,), (1,)), ((), ())),
            preferred_element_type=F32,
        )

    def finish_scores(number):
        logits = stage[number % slots]
        top = jnp.max(logits, axis=0, keepdims=True)
        shifted = jnp.exp(logits - top)
        if not raw:
            stage[number % slots] = shifted
        place, offset = divmod(number * sub, line)
        stat_ref[0, place : place + 1, offset : offset + sub] = top
        stat_ref[1, place : place + 1, offset : offset + sub] = jnp.sum(shifted, axis=0, keepdims=True)

    multiply(0)
    for number in range(count):
        if number + 1 >= slots and number + 1 < count:
            for copy in copies(number + 1 - slots):
                copy.wait()
        if number + 1 < count:
            multiply(number + 1)
        finish_scores(number)
        for copy in copies(number):
            copy.start()
    for number in range(max(0, count - slots), count):
        for copy in copies(number):
            copy.wait()


def stat_shape(total):
    line = divisor(total, 512)
    return (2, total // line, line)


def first_scores_body(raw, units, x_ref, _, e_hbm, stat_ref, stage, semaphores):
    target = [(slice(None), lambda columns: e_hbm.at[:, columns])]
    score_points(raw, units, x_ref, target, stat_ref, stage, semaphores)


def next_scores_body(raw, count, away, *refs):
    unit_refs = refs[:count]
    x_ref = refs[count]
    e_hbm, stat_ref, units, stage, semaphores = refs[-5:]
    rows = unit_refs[0].shape[0]
    pair = CORES * rows
    chip, core = place()
    chips = e_hbm.shape[0] // pair
    for number, ref in enumerate(unit_refs):
        of_pair = core if number % CORES == 0 else 1 - core
        start = pl.multiple_of((number - number % CORES + of_pair) * rows, rows)
        units[pl.ds(start, rows), :] = ref[...]

    def target_of(number):
        start = pl.multiple_of(lax.rem(chip + away + number, chips) * pair, pair)
        return lambda columns: e_hbm.at[pl.ds(start, pair), columns]

    targets = [
        (slice(number * pair, (number + 1) * pair), target_of(number)) for number in range(count // CORES)
    ]
    score_points(raw, units, x_ref, targets, stat_ref, stage, semaphores)


def scores(raw, blocks, points, away=None, shifted=None):
    total, width = points.shape
    count = len(blocks)
    rows = sum(block.shape[0] for block in blocks)
    all_rows = rows if shifted is None else shifted.shape[0]
    stat = stat_shape(total)
    parts = 1 if away is None else count // CORES
    more = [] if shifted is None or away == 0 else [shifted]
    scratch = [
        pltpu.VMEM((SLOTS, rows, divisor(stat[2], 256)), F32),
        pltpu.SemaphoreType.DMA((SLOTS, parts)),
    ]
    if away is not None:
        scratch = [pltpu.VMEM((rows, width), BF16)] + scratch
    if away is None:
        body = functools.partial(first_scores_body, raw)
    else:
        body = functools.partial(next_scores_body, raw, count, away)
    return pl.pallas_call(
        body,
        in_specs=[VMEM] * (count + 1) + [ANY] * len(more),
        out_specs=[VMEM, ANY, VMEM],
        out_shape=[
            jax.ShapeDtypeStruct(points.shape, BF16),
            jax.ShapeDtypeStruct((all_rows, total), F32),
            jax.ShapeDtypeStruct(stat, F32),
        ],
        input_output_aliases={count + number: number for number in range(1 + len(more))},
        scratch_shapes=scratch,
        compiler_params=params(SCORE_VMEM),
        cost_estimate=pl.CostEstimate(
            flops=2 * rows * total * width,
            bytes_accessed=2 * total * width + 4 * rows * total,
            transcendentals=rows * total,
        ),
    )(*blocks, points, *more)


FAR, THEIRS, OWN = range(3)


def weigh_body(by_rows, n_tops, kind, others, extra, pair, stat_ref, more_ref, *refs):
    parts = CORES if kind == FAR else 1
    top_refs, (e_hbm, x_ref, _), refs = refs[:n_tops], refs[n_tops : n_tops + 3], refs[n_tops + 3 :]
    out_refs, refs = refs[:parts], refs[parts + 1 :]
    if not by_rows:
        (kept_ref, kept_mass_ref), refs = refs[:2], refs[2:]
    scale_refs, refs = refs[:2], refs[2:]
    n_weights = 2 if by_rows else 0
    weights_refs, (stage, mass_ref, sum_ref, semaphores) = refs[:n_weights], refs[n_weights:]
    chip, core = place()
    line = stat_ref.shape[2]
    total = x_ref.shape[0]
    height, span = sum_ref.shape
    slots, _, chunk = stage.shape
    steps = total // chunk
    lanes = min(line, 128)

    def block_of(other):
        if kind == FAR:
            return lax.rem(chip + 1 + other, others + 1)
        return chip * CORES + (core if kind == OWN else 1 - core)

    def copy_of(number):
        other, step = divmod(number, steps)
        rows = pl.ds(pl.multiple_of(block_of(other) * height, height), height) if by_rows else slice(None)
        columns = slice(step * chunk, (step + 1) * chunk)
        slot = number % slots
        return pltpu.make_async_copy(e_hbm.at[rows, columns], stage.at[slot], semaphores.at[slot])

    for number in range(min(slots, others * steps)):
        copy_of(number).start()
    top, all_total = merge(stat_ref, more_ref)
    if by_rows:
        scale_refs[0][...] = top
        scale_refs[1][...] = 1.0 / all_total
    else:
        for ref, scale_ref in zip((top_refs[0], top_refs[-1]), scale_refs):
            scale_ref[...] = jnp.exp(ref[0] - top) / all_total

    def weights_of(values, group, number):
        one, two = (ref[number : number + 1, :] for ref in scale_refs)
        if by_rows:
            return jnp.exp(values - one) * two
        return values * jnp.where(chip == group, one, two)

    group_rows = height if by_rows else pair
    kept = not by_rows

    def weights_part(step):
        columns = slice(step * chunk, (step + 1) * chunk)
        return kept_ref.at[:, columns] if kept else weights_refs[step % 2]

    def weigh_step(number):
        step = number % steps
        weights_ref = weights_part(step)
        for group in range(height // group_rows):
            rows = slice(group * group_rows, (group + 1) * group_rows)
            mass = None
            for offset in range(0, chunk, line):
                values = stage[number % slots, rows, offset : offset + line]
                weights = weights_of(values, group, (step * chunk + offset) // line).astype(BF16)
                weights_ref[rows, offset : offset + line] = weights
                wide = weights.astype(F32)
                for lane in range(0, line, lanes):
                    piece = wide[:, lane : lane + lanes]
                    mass = piece if mass is None else mass + piece
            mass_ref[rows, :] = mass if step == 0 else mass_ref[rows, :] + mass

    weighed = steps if kept else others * steps
    copy_of(0).wait()
    weigh_step(0)
    for number in range(others * steps):
        other, step = divmod(number, steps)
        if number + slots < weighed:
            copy_of(number + slots).start()
        if number + 1 < weighed:
            copy_of(number + 1).wait()
        columns = slice(None)
        if not by_rows:
            columns = pl.ds(pl.multiple_of(block_of(other) * span, span), span)
        product = jnp.dot(
            weights_part(step)[...],
            x_ref[step * chunk : (step + 1) * chunk, columns],
            preferred_element_type=F32,
        )
        sum_ref[...] = product if step == 0 else sum_ref[...] + product
        if step == steps - 1:
            mass = jnp.sum(mass_ref[...].T, axis=0, keepdims=True)
            if kept:
                kept_mass_ref[...] = mass
            write_sums(by_rows, other, core, out_refs, sum_ref, mass, extra)
        if number + 1 < weighed:
            weigh_step(number + 1)


def write_sums(by_rows, other, core, out_refs, sum_ref, mass, extra):
    parts = len(out_refs)
    rows = out_refs[0].shape[1] - extra
    width = out_refs[0].shape[2]
    for part, ref in enumerate(out_refs):
        side = lax.rem(core + part, parts)
        ref[other, rows:, :] = jnp.zeros((extra, width), F32)
        if by_rows:
            found = mass
            if parts > 1:
                found = jnp.where(side == 0, mass[:, :rows], mass[:, rows:])
                ref[other, :rows, :] = sum_ref[pl.ds(pl.multiple_of(side * rows, rows), rows), :]
            else:
                ref[other, :rows, :] = sum_ref[...]
            ref[other, rows : rows + 1, :rows] = found
        else:
            sums = sum_ref[...]
            if parts > 1:
                sums = jnp.where(side == 0, sums[:, :width], sums[:, width:])
            ref[other, :rows, :] = sums
            for number in range(rows // width):
                ref[other, rows + number : rows + number + 1, :] = mass[
                    :, number * width : (number + 1) * width
                ]


def weigh_kept_body(kind, extra, kept_ref, mass_ref, x_ref, _, out_ref, kept_out, x_out, sum_ref):
    chip, core = place()
    span = sum_ref.shape[1]
    total = x_ref.shape[0]
    block = chip * CORES + (core if kind == OWN else 1 - core)
    columns = pl.ds(pl.multiple_of(block * span, span), span)
    sum_ref[...] = jnp.dot(kept_ref[...], x_ref[:, columns], preferred_element_type=F32)
    write_sums(False, 0, core, [out_ref], sum_ref, mass_ref[...], extra)


def weigh_kept(kind, n_pts, kept, mass, points, after):
    total, width = points.shape
    rows, cols = kept.shape[0], width // n_pts
    extra = round_up(-(-rows // cols), 8)
    return pl.pallas_call(
        functools.partial(weigh_kept_body, kind, extra),
        in_specs=[VMEM] * 3 + [ANY],
        out_specs=[VMEM] * 3,
        input_output_aliases={0: 1, 2: 2},
        scratch_shapes=[pltpu.VMEM((rows, cols), F32)],
        out_shape=[
            jax.ShapeDtypeStruct((1, rows + extra, cols), F32),
            jax.ShapeDtypeStruct(kept.shape, BF16),
            jax.ShapeDtypeStruct(points.shape, BF16),
        ],
        compiler_params=params(KEPT_VMEM),
        cost_estimate=pl.CostEstimate(
            flops=2 * rows * cols * total, bytes_accessed=2 * total * (rows + cols), transcendentals=0
        ),
    )(kept, mass, points, after)


def weigh(by_rows, kind, chips, stats, tops, shifted, points, after):
    total, width = points.shape
    pair = shifted.shape[0] // chips
    parts, others = (CORES, chips - 1) if kind == FAR else (1, 1)
    line = stats[0].shape[2]
    chunk = line * divisor(total // line, CHUNK_LINES)
    slots = min(WEIGH_SLOTS, total // chunk)
    kept = []
    if not by_rows:
        kept = [
            jax.ShapeDtypeStruct((shifted.shape[0], total), BF16),
            jax.ShapeDtypeStruct((1, shifted.shape[0]), F32),
        ]
    if by_rows:
        rows, cols = pair // CORES, width
        sums = (rows * parts, width)
    else:
        rows, cols = shifted.shape[0], width // (CORES * chips)
        sums = (rows, cols * parts)
    n_tops = len(tops)
    extra = round_up(-(-rows // cols), 8)
    return pl.pallas_call(
        functools.partial(weigh_body, by_rows, n_tops, kind, others, extra, pair),
        in_specs=[VMEM] * (2 + n_tops) + [ANY, VMEM, ANY],
        out_specs=[VMEM] * (parts + (1 if by_rows else 3)),
        input_output_aliases={3 + n_tops: parts},
        scratch_shapes=[pltpu.VMEM(stats[0].shape[1:], F32)] * 2
        + [pltpu.VMEM((sums[0], chunk), BF16)] * (2 if by_rows else 0)
        + [
            pltpu.VMEM((slots, sums[0], chunk), F32),
            pltpu.VMEM((sums[0], 128), F32),
            pltpu.VMEM(sums, F32),
            pltpu.SemaphoreType.DMA((slots,)),
        ],
        out_shape=[jax.ShapeDtypeStruct((others, rows + extra, cols), F32)] * parts
        + [jax.ShapeDtypeStruct(points.shape, BF16)]
        + kept,
        compiler_params=params(WEIGH_VMEM),
        cost_estimate=pl.CostEstimate(
            flops=2 * others * sums[0] * sums[1] * total,
            bytes_accessed=2 * others * total * (sums[1] + 2 * sums[0]),
            transcendentals=0,
        ),
    )(*stats, *tops, shifted, points, after)


def fold_body(rows, lines, mine_ref, theirs_ref, after_ref, out_ref):
    width = out_ref.shape[1]
    step = divisor(rows, 128) if lines == 1 else width
    out_ref[rows:, :] = jnp.zeros((out_ref.shape[0] - rows, width), BF16)
    scales = []
    for start in range(0, rows, step):
        part = slice(start, start + step)
        total = mine_ref[part, :] + theirs_ref[part, :]
        top = jnp.max(jnp.abs(total), axis=1, keepdims=True)
        scale = jnp.maximum(top * 1.01, 1e-30).astype(BF16)
        out_ref[part, :] = encode(total, scale.astype(F32))
        scales.append(jnp.broadcast_to(scale.astype(F32), (step, 128)).T[0:1, :])
    mass = mine_ref[rows : rows + lines, :] + theirs_ref[rows : rows + lines, :]
    if lines == 1:
        out_ref[rows : rows + 1, :rows] = jnp.concatenate(scales, axis=1).astype(BF16)
    else:
        out_ref[rows : rows + lines, :] = jnp.concatenate(scales, axis=0).astype(BF16)
    for number in range(1, 4):
        rounded = mass.astype(BF16)
        out_ref[rows + number * lines : rows + (number + 1) * lines, :] = rounded
        mass = mass - rounded.astype(F32)


def fold(mine, theirs, after):
    others, height, width = mine.shape
    out_height = coded_height(height, width)
    return pl.pallas_call(
        functools.partial(fold_body, *shape_of(height, width)),
        grid=(others,),
        in_specs=[pl.BlockSpec((None, height, width), lambda d: (d, 0, 0))] * 2 + [ANY],
        out_specs=pl.BlockSpec((None, out_height, width), lambda d: (d, 0, 0)),
        out_shape=jax.ShapeDtypeStruct((others, out_height, width), BF16),
        compiler_params=params(10),
        cost_estimate=pl.CostEstimate(
            flops=20 * others * height * width,
            bytes_accessed=10 * others * height * width,
            transcendentals=others * height * width,
        ),
    )(mine, theirs, after)


def shape_of(height, width):
    rows = height - 8
    while rows + round_up(-(-rows // width), 8) != height:
        rows -= 8
    return rows, -(-rows // width)


def coded_height(height, width):
    rows, lines = shape_of(height, width)
    return rows + round_up(4 * lines, 16)


def finish_body(rows, lines, as_units, mine_ref, theirs_ref, *refs):
    code_refs, out_ref = refs[:-1], refs[-1]
    width = out_ref.shape[1]
    step = divisor(rows, 128) if lines == 1 else width
    mass = mine_ref[rows : rows + lines, :] + theirs_ref[rows : rows + lines, :]
    for ref in code_refs:
        for number in range(1, 4):
            start = rows + number * lines
            mass = mass + ref[start : start + lines, :].astype(F32)

    def column(values, number):
        if lines == 1:
            line = values[:, number * step : (number + 1) * step]
        else:
            line = values[number : number + 1, :]
        return to_column(line, step)[:, 0:1]

    scales = [ref[rows : rows + lines, :].astype(F32) for ref in code_refs]
    for number in range(rows // step):
        part = slice(number * step, (number + 1) * step)
        total = mine_ref[part, :] + theirs_ref[part, :]
        for ref, scale in zip(code_refs, scales):
            total = total + decode(ref[part, :], column(scale, number))
        means = total / jnp.maximum(column(mass, number), 1.0)
        out_ref[part, :] = normalize_rows(means).astype(BF16) if as_units else means


def finish(as_units, mine, theirs, codes):
    height, width = mine.shape
    rows, lines = shape_of(height, width)
    out_type = BF16 if as_units else F32
    return pl.pallas_call(
        functools.partial(finish_body, rows, lines, as_units),
        out_shape=jax.ShapeDtypeStruct((rows, width), out_type),
        compiler_params=params(10),
        cost_estimate=pl.CostEstimate(
            flops=30 * rows * width,
            bytes_accessed=(12 + 2 * len(codes)) * rows * width,
            transcendentals=2 * rows * width,
        ),
    )(mine, theirs, *codes)


def keep_body(value_ref, after_ref, out_ref):
    pass


def keep_until(value, after):
    return pl.pallas_call(
        keep_body,
        in_specs=[VMEM, ANY],
        out_specs=VMEM,
        out_shape=jax.ShapeDtypeStruct(value.shape, value.dtype),
        input_output_aliases={0: 0},
        compiler_params=params(10),
    )(value, after)


def merge_body(one_ref, two_ref, out_ref):
    out_ref[0], out_ref[1] = merge(one_ref, two_ref)


def merged(one, two):
    return pl.pallas_call(
        merge_body, out_shape=jax.ShapeDtypeStruct(one.shape, F32), compiler_params=params(10)
    )(one, two)


def log_body(one_ref, two_ref, out_ref):
    top, total = merge(one_ref, two_ref)
    out_ref[...] = top + jnp.log(total)


def log_norms(one, two):
    return pl.pallas_call(
        log_body, out_shape=jax.ShapeDtypeStruct(one.shape[1:], F32), compiler_params=params(10)
    )(one, two).reshape(-1)


def on_device(n_pts, n_cen, points, centroids):
    chips = n_pts // CORES

    def to_partner(value):
        return lax.ppermute(value, "pts", [(i, i ^ 1) for i in range(n_pts)])

    def to_chip(value, away):
        moves = [(i, (i + CORES * away) % n_pts) for i in range(n_pts)]
        return lax.ppermute(value, "pts", moves)

    def over_centroids(stats):
        if n_cen & (n_cen - 1):
            found = [stats]
            for away in range(1, n_cen):
                moves = [(i, (i + away) % n_cen) for i in range(n_cen)]
                found.append(lax.ppermute(stats, "cen", moves))
            return functools.reduce(merged, found[:-1]), found[-1]
        away = 1
        while True:
            moves = [(i, i ^ away) for i in range(n_cen)]
            other = lax.ppermute(stats, "cen", moves)
            away *= 2
            if away >= n_cen:
                return stats, other
            stats = merged(stats, other)

    def sums_over_pts(by_rows, stats, tops, shifted, points):
        kept = mass = None

        def weighted(kind, after):
            nonlocal points, kept, mass
            if by_rows:
                *found, points = weigh(by_rows, kind, chips, stats, tops, shifted, points, after)
                return found
            if kind == FAR:
                *found, points, kept, mass = weigh(by_rows, kind, chips, stats, tops, shifted, points, after)
                return found
            *found, kept, points = weigh_kept(kind, n_pts, kept, mass, points, after)
            return found

        far_mine, far_theirs = weighted(FAR, stats[0])
        far_found = to_partner(far_theirs)
        (near_theirs,) = weighted(THEIRS, far_theirs)
        near_found = to_partner(near_theirs)
        coded = fold(far_mine, far_found, near_theirs)
        codes = [to_chip(coded[away - 1], away) for away in range(1, chips)]
        (near_mine,) = weighted(OWN, coded)
        return finish(by_rows, near_mine[0], near_found[0], codes), points

    points, units = load(centroids, points)
    points, shifted, own = scores(ITERS > 1, [units], points)
    stats = over_centroids(own)
    tops = [own]
    for iteration in range(1, ITERS):
        raw = iteration + 1 < ITERS
        mine, points = sums_over_pts(True, stats, tops, shifted, points)
        away_units = [to_chip(mine, -away) for away in range(1, chips)]
        points, shifted, near_own = scores(raw, [mine, to_partner(mine)], points, 0, shifted)
        away_units = [keep_until(unit, near_own) for unit in away_units]
        blocks = [unit for mine in away_units for unit in (mine, to_partner(mine))]
        points, shifted, far_own = scores(raw, blocks, points, 1, shifted)
        tops = [near_own, far_own]
        stats = over_centroids(merged(near_own, far_own))
    means, _ = sums_over_pts(False, stats, tops, shifted, points)
    return (means, log_norms(*stats))


def solution(mesh):
    placed = (P("pts", None), P("cen", None))
    return jax.shard_map(
        functools.partial(on_device, mesh.shape["pts"], mesh.shape["cen"]),
        mesh=mesh,
        in_specs=placed,
        out_specs=(P("cen", "pts"), P("pts")),
        check_vma=False,
    )
```

```python
import functools

import jax
import jax.numpy as jnp
from jax import lax
from jax.experimental import pallas as pl
from jax.experimental.pallas import tpu as pltpu
from jax.sharding import PartitionSpec as P

ITERS = 2
F32 = jnp.float32
BF16 = jnp.bfloat16
SCORE_VMEM = 34
WEIGH_VMEM = 34
KEPT_VMEM = 20
CHUNK_LINES = 2
WEIGH_SLOTS = 2
LEVELS = 30000.0
LOWEST = -117.0


def divisor(total, wanted):
    size = min(total, wanted)
    while total % size:
        size -= 1
    return size


def round_up(value, unit):
    return -(-value // unit) * unit


def normalize_rows(rows):
    return rows * lax.rsqrt(jnp.sum(rows * rows, axis=1, keepdims=True) + 1e-06)


CORES = 2


def place():
    me = lax.axis_index("pts")
    return lax.div(me, CORES), lax.rem(me, CORES)


def params(mebibytes):
    return pltpu.CompilerParams(vmem_limit_bytes=mebibytes * 2**20)


VMEM = pl.BlockSpec(memory_space=pltpu.VMEM)
ANY = pl.BlockSpec(memory_space=pl.ANY)


def merge(sets):
    top = functools.reduce(jnp.maximum, [stats[0] for stats in sets])
    return top, functools.reduce(jnp.add, [stats[1] * jnp.exp(stats[0] - top) for stats in sets])


def to_column(row, height):
    return jnp.broadcast_to(row, (128, height)).T


def encode(values, scale):
    steps = jnp.floor(jnp.abs(values) * (LEVELS / scale) + 0.5)
    power = jnp.floor(steps * (1.0 / 128.0))
    size = (1.0 + (steps * (1.0 / 128.0) - power)) * jnp.exp2(power + LOWEST)
    return jnp.where(values < 0.0, -size, size).astype(BF16)


def decode(codes, scale):
    wide = codes.astype(F32)
    size = jnp.abs(wide)
    power = jnp.floor(jnp.log2(size))
    steps = 128.0 * (power - LOWEST + (size * jnp.exp2(-power) - 1.0))
    return jnp.where(wide < 0.0, -steps, steps) * (scale * (1.0 / LEVELS))


def score_points(raw, units, x_ref, e_parts, stat_ref, stage, semaphores):
    line = stat_ref.shape[2]
    lines = stage.shape[0]
    sub = divisor(line, 256)

    def copies(number, slot):
        columns = pl.ds(pl.multiple_of(number * line, line), line)
        return [
            pltpu.make_async_copy(stage.at[slot, rows, :], target(columns), semaphores.at[slot, part])
            for part, (rows, target) in enumerate(e_parts)
        ]

    def visit(step, carry):
        for slot in range(lines):
            number = step * lines + slot

            @pl.when(step > 0)
            def _():
                for copy in copies(number - lines, slot):
                    copy.wait()

            tops, totals = [], []
            for offset in range(0, line, sub):
                logits = lax.dot_general(
                    units[...],
                    x_ref[pl.ds(pl.multiple_of(number * line + offset, sub), sub), :],
                    (((1,), (1,)), ((), ())),
                    preferred_element_type=F32,
                )
                top = jnp.max(logits, axis=0, keepdims=True)
                shifted = jnp.exp(logits - top)
                stage[slot, :, offset : offset + sub] = logits if raw else shifted
                tops.append(top)
                totals.append(jnp.sum(shifted, axis=0, keepdims=True))
            stat_ref[0, pl.ds(number, 1), :] = jnp.concatenate(tops, axis=1)
            stat_ref[1, pl.ds(number, 1), :] = jnp.concatenate(totals, axis=1)
            for copy in copies(number, slot):
                copy.start()
        return carry

    steps = stat_ref.shape[1] // lines
    lax.fori_loop(0, steps, visit, 0)
    for slot in range(lines):
        for copy in copies((steps - 1) * lines + slot, slot):
            copy.wait()


def stat_shape(total):
    line = divisor(total, 512)
    return (2, total // line, line)


def first_scores_body(raw, units, x_ref, _, e_hbm, stat_ref, stage, semaphores):
    target = [(slice(None), lambda columns: e_hbm.at[:, columns])]
    score_points(raw, units, x_ref, target, stat_ref, stage, semaphores)


def next_scores_body(raw, count, away, *refs):
    unit_refs = refs[:count]
    x_ref = refs[count]
    e_hbm, stat_ref, units, stage, semaphores = refs[-5:]
    rows = unit_refs[0].shape[0]
    pair = CORES * rows
    chip, core = place()
    chips = e_hbm.shape[0] // pair
    for number, ref in enumerate(unit_refs):
        of_pair = core if number % CORES == 0 else 1 - core
        start = pl.multiple_of((number - number % CORES + of_pair) * rows, rows)
        units[pl.ds(start, rows), :] = ref[...]

    def target_of(number):
        start = pl.multiple_of(lax.rem(chip + away + number, chips) * pair, pair)
        return lambda columns: e_hbm.at[pl.ds(start, pair), columns]

    targets = [
        (slice(number * pair, (number + 1) * pair), target_of(number)) for number in range(count // CORES)
    ]
    score_points(raw, units, x_ref, targets, stat_ref, stage, semaphores)


def scores(raw, blocks, points, away=None, shifted=None):
    total, width = points.shape
    count = len(blocks)
    rows = sum(block.shape[0] for block in blocks)
    all_rows = rows if shifted is None else shifted.shape[0]
    stat = stat_shape(total)
    parts = 1 if away is None else count // CORES
    more = [] if shifted is None or away == 0 else [shifted]
    scratch = [
        pltpu.VMEM((divisor(stat[1], 2), rows, stat[2]), F32),
        pltpu.SemaphoreType.DMA((divisor(stat[1], 2), parts)),
    ]
    if away is not None:
        scratch = [pltpu.VMEM((rows, width), BF16)] + scratch
    if away is None:
        body = functools.partial(first_scores_body, raw)
    else:
        body = functools.partial(next_scores_body, raw, count, away)
    return pl.pallas_call(
        body,
        in_specs=[VMEM] * (count + 1) + [ANY] * len(more),
        out_specs=[VMEM, ANY, VMEM],
        out_shape=[
            jax.ShapeDtypeStruct(points.shape, BF16),
            jax.ShapeDtypeStruct((all_rows, total), F32),
            jax.ShapeDtypeStruct(stat, F32),
        ],
        input_output_aliases={count + number: number for number in range(1 + len(more))},
        scratch_shapes=scratch,
        compiler_params=params(SCORE_VMEM),
        cost_estimate=pl.CostEstimate(
            flops=2 * rows * total * width,
            bytes_accessed=2 * total * width + 4 * rows * total,
            transcendentals=rows * total,
        ),
    )(*blocks, points, *more)


FAR, THEIRS, OWN = range(3)


def weigh_body(by_rows, n_sets, n_tops, kind, others, extra, pair, *refs):
    parts = CORES if kind == FAR else 1
    stat_refs, refs = refs[:n_sets], refs[n_sets:]
    top_refs, (e_hbm, x_ref, _), refs = refs[:n_tops], refs[n_tops : n_tops + 3], refs[n_tops + 3 :]
    out_refs, refs = refs[:parts], refs[parts + 1 :]
    if not by_rows:
        (kept_ref, kept_mass_ref), refs = refs[:2], refs[2:]
    scale_refs, refs = refs[:2], refs[2:]
    n_weights = 2 if by_rows else 0
    weights_refs, (stage, mass_ref, sum_ref, semaphores) = refs[:n_weights], refs[n_weights:]
    chip, core = place()
    line = stat_refs[0].shape[2]
    total = x_ref.shape[0]
    height, span = sum_ref.shape
    slots, _, chunk = stage.shape
    steps = total // chunk
    lanes = min(line, 128)

    def block_of(other):
        if kind == FAR:
            return lax.rem(chip + 1 + other, others + 1)
        return chip * CORES + (core if kind == OWN else 1 - core)

    def copy_of(number):
        other, step = divmod(number, steps)
        rows = pl.ds(pl.multiple_of(block_of(other) * height, height), height) if by_rows else slice(None)
        columns = slice(step * chunk, (step + 1) * chunk)
        slot = number % slots
        return pltpu.make_async_copy(e_hbm.at[rows, columns], stage.at[slot], semaphores.at[slot])

    for number in range(min(slots, others * steps)):
        copy_of(number).start()
    top, all_total = merge(stat_refs)
    if by_rows:
        scale_refs[0][...] = top
        scale_refs[1][...] = 1.0 / all_total
    else:
        for ref, scale_ref in zip((top_refs[0], top_refs[-1]), scale_refs):
            scale_ref[...] = jnp.exp(ref[0] - top) / all_total

    def weights_of(values, group, number):
        one, two = (ref[number : number + 1, :] for ref in scale_refs)
        if by_rows:
            return jnp.exp(values - one) * two
        return values * jnp.where(chip == group, one, two)

    group_rows = height if by_rows else pair
    kept = not by_rows

    def weights_part(step):
        columns = slice(step * chunk, (step + 1) * chunk)
        return kept_ref.at[:, columns] if kept else weights_refs[step % 2]

    def weigh_step(number):
        step = number % steps
        weights_ref = weights_part(step)
        for group in range(height // group_rows):
            rows = slice(group * group_rows, (group + 1) * group_rows)
            mass = None
            for offset in range(0, chunk, line):
                values = stage[number % slots, rows, offset : offset + line]
                weights = weights_of(values, group, (step * chunk + offset) // line).astype(BF16)
                weights_ref[rows, offset : offset + line] = weights
                wide = weights.astype(F32)
                for lane in range(0, line, lanes):
                    piece = wide[:, lane : lane + lanes]
                    mass = piece if mass is None else mass + piece
            mass_ref[rows, :] = mass if step == 0 else mass_ref[rows, :] + mass

    weighed = steps if kept else others * steps
    for number in range(others * steps):
        other, step = divmod(number, steps)
        if number < weighed:
            copy_of(number).wait()
            weigh_step(number)
        if number + slots < weighed:
            copy_of(number + slots).start()
        columns = slice(None)
        if not by_rows:
            columns = pl.ds(pl.multiple_of(block_of(other) * span, span), span)
        product = jnp.dot(
            weights_part(step)[...],
            x_ref[step * chunk : (step + 1) * chunk, columns],
            preferred_element_type=F32,
        )
        sum_ref[...] = product if step == 0 else sum_ref[...] + product
        if step == steps - 1:
            mass = jnp.sum(mass_ref[...].T, axis=0, keepdims=True)
            if kept:
                kept_mass_ref[...] = mass
            write_sums(by_rows, other, core, out_refs, sum_ref, mass, extra)


def write_sums(by_rows, other, core, out_refs, sum_ref, mass, extra):
    parts = len(out_refs)
    rows = out_refs[0].shape[1] - extra
    width = out_refs[0].shape[2]
    for part, ref in enumerate(out_refs):
        side = lax.rem(core + part, parts)
        ref[other, rows:, :] = jnp.zeros((extra, width), F32)
        if by_rows:
            found = mass
            if parts > 1:
                found = jnp.where(side == 0, mass[:, :rows], mass[:, rows:])
                ref[other, :rows, :] = sum_ref[pl.ds(pl.multiple_of(side * rows, rows), rows), :]
            else:
                ref[other, :rows, :] = sum_ref[...]
            ref[other, rows : rows + 1, :rows] = found
        else:
            sums = sum_ref[...]
            if parts > 1:
                sums = jnp.where(side == 0, sums[:, :width], sums[:, width:])
            ref[other, :rows, :] = sums
            for number in range(rows // width):
                ref[other, rows + number : rows + number + 1, :] = mass[
                    :, number * width : (number + 1) * width
                ]


def weigh_kept_body(kind, extra, kept_ref, mass_ref, x_ref, _, out_ref, kept_out, x_out, sum_ref):
    chip, core = place()
    span = sum_ref.shape[1]
    total = x_ref.shape[0]
    block = chip * CORES + (core if kind == OWN else 1 - core)
    columns = pl.ds(pl.multiple_of(block * span, span), span)
    sum_ref[...] = jnp.dot(kept_ref[...], x_ref[:, columns], preferred_element_type=F32)
    write_sums(False, 0, core, [out_ref], sum_ref, mass_ref[...], extra)


def weigh_kept(kind, n_pts, kept, mass, points, after):
    total, width = points.shape
    rows, cols = kept.shape[0], width // n_pts
    extra = round_up(-(-rows // cols), 8)
    return pl.pallas_call(
        functools.partial(weigh_kept_body, kind, extra),
        in_specs=[VMEM] * 3 + [ANY],
        out_specs=[VMEM] * 3,
        input_output_aliases={0: 1, 2: 2},
        scratch_shapes=[pltpu.VMEM((rows, cols), F32)],
        out_shape=[
            jax.ShapeDtypeStruct((1, rows + extra, cols), F32),
            jax.ShapeDtypeStruct(kept.shape, BF16),
            jax.ShapeDtypeStruct(points.shape, BF16),
        ],
        compiler_params=params(KEPT_VMEM),
        cost_estimate=pl.CostEstimate(
            flops=2 * rows * cols * total, bytes_accessed=2 * total * (rows + cols), transcendentals=0
        ),
    )(kept, mass, points, after)


def weigh(by_rows, kind, chips, stats, tops, shifted, points, after):
    total, width = points.shape
    pair = shifted.shape[0] // chips
    parts, others = (CORES, chips - 1) if kind == FAR else (1, 1)
    line = stats[0].shape[2]
    chunk = line * divisor(total // line, CHUNK_LINES)
    slots = min(WEIGH_SLOTS, total // chunk)
    kept = []
    if not by_rows:
        kept = [
            jax.ShapeDtypeStruct((shifted.shape[0], total), BF16),
            jax.ShapeDtypeStruct((1, shifted.shape[0]), F32),
        ]
    if by_rows:
        rows, cols = pair // CORES, width
        sums = (rows * parts, width)
    else:
        rows, cols = shifted.shape[0], width // (CORES * chips)
        sums = (rows, cols * parts)
    n_tops = len(tops)
    extra = round_up(-(-rows // cols), 8)
    return pl.pallas_call(
        functools.partial(weigh_body, by_rows, len(stats), n_tops, kind, others, extra, pair),
        in_specs=[VMEM] * (len(stats) + n_tops) + [ANY, VMEM, ANY],
        out_specs=[VMEM] * (parts + (1 if by_rows else 3)),
        input_output_aliases={len(stats) + n_tops + 1: parts},
        scratch_shapes=[pltpu.VMEM(stats[0].shape[1:], F32)] * 2
        + [pltpu.VMEM((sums[0], chunk), BF16)] * (2 if by_rows else 0)
        + [
            pltpu.VMEM((slots, sums[0], chunk), F32),
            pltpu.VMEM((sums[0], 128), F32),
            pltpu.VMEM(sums, F32),
            pltpu.SemaphoreType.DMA((slots,)),
        ],
        out_shape=[jax.ShapeDtypeStruct((others, rows + extra, cols), F32)] * parts
        + [jax.ShapeDtypeStruct(points.shape, BF16)]
        + kept,
        compiler_params=params(WEIGH_VMEM),
        cost_estimate=pl.CostEstimate(
            flops=2 * others * sums[0] * sums[1] * total,
            bytes_accessed=2 * others * total * (sums[1] + 2 * sums[0]),
            transcendentals=0,
        ),
    )(*stats, *tops, shifted, points, after)


def fold_body(rows, lines, mine_ref, theirs_ref, after_ref, out_ref):
    width = out_ref.shape[1]
    step = divisor(rows, 128) if lines == 1 else width
    out_ref[rows:, :] = jnp.zeros((out_ref.shape[0] - rows, width), BF16)
    scales = []
    for start in range(0, rows, step):
        part = slice(start, start + step)
        total = mine_ref[part, :] + theirs_ref[part, :]
        top = jnp.max(jnp.abs(total), axis=1, keepdims=True)
        scale = jnp.maximum(top * 1.01, 1e-30).astype(BF16)
        out_ref[part, :] = encode(total, scale.astype(F32))
        scales.append(jnp.broadcast_to(scale.astype(F32), (step, 128)).T[0:1, :])
    mass = mine_ref[rows : rows + lines, :] + theirs_ref[rows : rows + lines, :]
    if lines == 1:
        out_ref[rows : rows + 1, :rows] = jnp.concatenate(scales, axis=1).astype(BF16)
    else:
        out_ref[rows : rows + lines, :] = jnp.concatenate(scales, axis=0).astype(BF16)
    for number in range(1, 4):
        rounded = mass.astype(BF16)
        out_ref[rows + number * lines : rows + (number + 1) * lines, :] = rounded
        mass = mass - rounded.astype(F32)


def fold(mine, theirs, after):
    others, height, width = mine.shape
    out_height = coded_height(height, width)
    return pl.pallas_call(
        functools.partial(fold_body, *shape_of(height, width)),
        grid=(others,),
        in_specs=[pl.BlockSpec((None, height, width), lambda d: (d, 0, 0))] * 2 + [ANY],
        out_specs=pl.BlockSpec((None, out_height, width), lambda d: (d, 0, 0)),
        out_shape=jax.ShapeDtypeStruct((others, out_height, width), BF16),
        compiler_params=params(10),
        cost_estimate=pl.CostEstimate(
            flops=20 * others * height * width,
            bytes_accessed=10 * others * height * width,
            transcendentals=others * height * width,
        ),
    )(mine, theirs, after)


def shape_of(height, width):
    rows = height - 8
    while rows + round_up(-(-rows // width), 8) != height:
        rows -= 8
    return rows, -(-rows // width)


def coded_height(height, width):
    rows, lines = shape_of(height, width)
    return rows + round_up(4 * lines, 16)


def finish_body(rows, lines, as_units, mine_ref, theirs_ref, *refs):
    code_refs, out_ref = refs[:-1], refs[-1]
    width = out_ref.shape[1]
    step = divisor(rows, 128) if lines == 1 else width
    mass = mine_ref[rows : rows + lines, :] + theirs_ref[rows : rows + lines, :]
    for ref in code_refs:
        for number in range(1, 4):
            start = rows + number * lines
            mass = mass + ref[start : start + lines, :].astype(F32)

    def column(values, number):
        if lines == 1:
            line = values[:, number * step : (number + 1) * step]
        else:
            line = values[number : number + 1, :]
        return to_column(line, step)[:, 0:1]

    scales = [ref[rows : rows + lines, :].astype(F32) for ref in code_refs]
    for number in range(rows // step):
        part = slice(number * step, (number + 1) * step)
        total = mine_ref[part, :] + theirs_ref[part, :]
        for ref, scale in zip(code_refs, scales):
            total = total + decode(ref[part, :], column(scale, number))
        means = total / jnp.maximum(column(mass, number), 1.0)
        out_ref[part, :] = normalize_rows(means).astype(BF16) if as_units else means


def finish(as_units, mine, theirs, codes):
    height, width = mine.shape
    rows, lines = shape_of(height, width)
    out_type = BF16 if as_units else F32
    return pl.pallas_call(
        functools.partial(finish_body, rows, lines, as_units),
        out_shape=jax.ShapeDtypeStruct((rows, width), out_type),
        compiler_params=params(10),
        cost_estimate=pl.CostEstimate(
            flops=30 * rows * width,
            bytes_accessed=(12 + 2 * len(codes)) * rows * width,
            transcendentals=2 * rows * width,
        ),
    )(mine, theirs, *codes)


def keep_body(value_ref, after_ref, out_ref):
    pass


def keep_until(value, after):
    return pl.pallas_call(
        keep_body,
        in_specs=[VMEM, ANY],
        out_specs=VMEM,
        out_shape=jax.ShapeDtypeStruct(value.shape, value.dtype),
        input_output_aliases={0: 0},
        compiler_params=params(10),
    )(value, after)


def merge_body(*refs):
    refs[-1][0], refs[-1][1] = merge(refs[:-1])


def merged(sets):
    return pl.pallas_call(
        merge_body, out_shape=jax.ShapeDtypeStruct(sets[0].shape, F32), compiler_params=params(10)
    )(*sets)


def log_body(*refs):
    top, total = merge(refs[:-1])
    refs[-1][...] = top + jnp.log(total)


def log_norms(sets):
    return pl.pallas_call(
        log_body, out_shape=jax.ShapeDtypeStruct(sets[0].shape[1:], F32), compiler_params=params(10)
    )(*sets).reshape(-1)


def on_device(n_pts, n_cen, points, centroids):
    chips = n_pts // CORES

    def to_partner(value):
        return lax.ppermute(value, "pts", [(i, i ^ 1) for i in range(n_pts)])

    def to_chip(value, away):
        moves = [(i, (i + CORES * away) % n_pts) for i in range(n_pts)]
        return lax.ppermute(value, "pts", moves)

    def over_centroids(stats):
        if n_cen & (n_cen - 1):
            moves = [[(i, (i + away) % n_cen) for i in range(n_cen)] for away in range(1, n_cen)]
            return [stats] + [lax.ppermute(stats, "cen", move) for move in moves]
        done, sets = 1, [stats]
        while done < n_cen:
            if done > 1:
                sets = [merged(sets)]
            ways = 4 if (n_cen // done).bit_length() % 2 else 2
            for way in range(1, ways):
                moves = [(i, i ^ (way * done)) for i in range(n_cen)]
                sets.append(lax.ppermute(sets[0], "cen", moves))
            done *= ways
        return sets

    def sums_over_pts(by_rows, stats, tops, shifted, points):
        kept = mass = None

        def weighted(kind, after):
            nonlocal points, kept, mass
            if by_rows:
                *found, points = weigh(by_rows, kind, chips, stats, tops, shifted, points, after)
                return found
            if kind == FAR:
                *found, points, kept, mass = weigh(by_rows, kind, chips, stats, tops, shifted, points, after)
                return found
            *found, kept, points = weigh_kept(kind, n_pts, kept, mass, points, after)
            return found

        far_mine, far_theirs = weighted(FAR, stats[0])
        far_found = to_partner(far_theirs)
        (near_theirs,) = weighted(THEIRS, far_theirs)
        near_found = to_partner(near_theirs)
        coded = fold(far_mine, far_found, near_theirs)
        codes = [to_chip(coded[away - 1], away) for away in range(1, chips)]
        (near_mine,) = weighted(OWN, coded)
        return finish(by_rows, near_mine[0], near_found[0], codes), points

    square_sums = jnp.sum(centroids * centroids, axis=1)
    units = (centroids * lax.rsqrt(square_sums + 1e-06)[:, None]).astype(BF16)
    points, shifted, own = scores(ITERS > 1, [units], points)
    stats = over_centroids(own)
    tops = [own]
    for iteration in range(1, ITERS):
        raw = iteration + 1 < ITERS
        mine, points = sums_over_pts(True, stats, tops, shifted, points)
        away_units = [to_chip(mine, -away) for away in range(1, chips)]
        points, shifted, near_own = scores(raw, [mine, to_partner(mine)], points, 0, shifted)
        away_units = [keep_until(unit, near_own) for unit in away_units]
        blocks = [unit for mine in away_units for unit in (mine, to_partner(mine))]
        points, shifted, far_own = scores(raw, blocks, points, 1, shifted)
        tops = [near_own, far_own]
        stats = over_centroids(merged([near_own, far_own]))
    means, _ = sums_over_pts(False, stats, tops, shifted, points)
    return (means, log_norms(stats))


def solution(mesh):
    placed = (P("pts", None), P("cen", None))
    return jax.shard_map(
        functools.partial(on_device, mesh.shape["pts"], mesh.shape["cen"]),
        mesh=mesh,
        in_specs=placed,
        out_specs=(P("cen", "pts"), P("pts")),
        check_vma=False,
    )
```

```python
import functools

import jax
import jax.numpy as jnp
from jax import lax
from jax.experimental import pallas as pl
from jax.experimental.pallas import tpu as pltpu
from jax.sharding import PartitionSpec as P

ITERS = 2
F32 = jnp.float32
BF16 = jnp.bfloat16
LOAD_VMEM = 38
SCORE_VMEM = 34
WEIGH_VMEM = 34
KEPT_VMEM = 20
CHUNK_LINES = 2
WEIGH_SLOTS = 2
LEVELS = 30000.0
LOWEST = -117.0


def divisor(total, wanted):
    size = min(total, wanted)
    while total % size:
        size -= 1
    return size


def round_up(value, unit):
    return -(-value // unit) * unit


def normalize_rows(rows):
    return rows * lax.rsqrt(jnp.sum(rows * rows, axis=1, keepdims=True) + 1e-06)


CORES = 2


def place():
    me = lax.axis_index("pts")
    return lax.div(me, CORES), lax.rem(me, CORES)


def params(mebibytes):
    return pltpu.CompilerParams(vmem_limit_bytes=mebibytes * 2**20)


VMEM = pl.BlockSpec(memory_space=pltpu.VMEM)
ANY = pl.BlockSpec(memory_space=pl.ANY)


def merge(sets):
    top = functools.reduce(jnp.maximum, [stats[0] for stats in sets])
    return top, functools.reduce(jnp.add, [stats[1] * jnp.exp(stats[0] - top) for stats in sets])


def to_column(row, height):
    return jnp.broadcast_to(row, (128, height)).T


def encode(values, scale):
    steps = jnp.floor(jnp.abs(values) * (LEVELS / scale) + 0.5)
    power = jnp.floor(steps * (1.0 / 128.0))
    size = (1.0 + (steps * (1.0 / 128.0) - power)) * jnp.exp2(power + LOWEST)
    return jnp.where(values < 0.0, -size, size).astype(BF16)


def decode(codes, scale):
    wide = codes.astype(F32)
    size = jnp.abs(wide)
    power = jnp.floor(jnp.log2(size))
    steps = 128.0 * (power - LOWEST + (size * jnp.exp2(-power) - 1.0))
    return jnp.where(wide < 0.0, -steps, steps) * (scale * (1.0 / LEVELS))


def load_body(c_hbm, sums_ref, x_hbm, x_ref, units_ref, rows_ref, row_sems, point_sem):
    row_step = rows_ref.shape[0] // row_sems.shape[0]

    def rows_of(number):
        part = pl.ds(number * row_step, row_step)
        return pltpu.make_async_copy(c_hbm.at[part, :], rows_ref.at[part, :], row_sems.at[number])

    all_points = pltpu.make_async_copy(x_hbm, x_ref, point_sem)
    for number in range(row_sems.shape[0]):
        rows_of(number).start()
    all_points.start()
    for number in range(row_sems.shape[0]):
        rows_of(number).wait()
        part = slice(number * row_step, (number + 1) * row_step)
        scale = to_column(lax.rsqrt(sums_ref[:, part] + 1e-06), row_step)[:, 0:1]
        units_ref[part, :] = (rows_ref[part, :] * scale).astype(BF16)
    all_points.wait()


def load(centroids, points):
    square_sums = jnp.sum(centroids * centroids, axis=1)[None]
    return pl.pallas_call(
        load_body,
        in_specs=[ANY, VMEM, ANY],
        out_specs=[VMEM] * 2,
        out_shape=[
            jax.ShapeDtypeStruct(points.shape, BF16),
            jax.ShapeDtypeStruct(centroids.shape, BF16),
        ],
        scratch_shapes=[
            pltpu.VMEM(centroids.shape, F32),
            pltpu.SemaphoreType.DMA((divisor(centroids.shape[0] // 16, 4),)),
            pltpu.SemaphoreType.DMA(()),
        ],
        compiler_params=params(LOAD_VMEM),
        cost_estimate=pl.CostEstimate(
            flops=4 * centroids.size, bytes_accessed=4 * centroids.size + 2 * points.size, transcendentals=0
        ),
    )(centroids, square_sums, points)


def score_points(raw, units, x_ref, e_parts, stat_ref, stage, semaphores):
    line = stat_ref.shape[2]
    lines = stage.shape[0]
    sub = divisor(line, 256)

    def copies(number, slot):
        columns = pl.ds(pl.multiple_of(number * line, line), line)
        return [
            pltpu.make_async_copy(stage.at[slot, rows, :], target(columns), semaphores.at[slot, part])
            for part, (rows, target) in enumerate(e_parts)
        ]

    def visit(step, carry):
        for slot in range(lines):
            number = step * lines + slot

            @pl.when(step > 0)
            def _():
                for copy in copies(number - lines, slot):
                    copy.wait()

            tops, totals = [], []
            for offset in range(0, line, sub):
                logits = lax.dot_general(
                    units[...],
                    x_ref[pl.ds(pl.multiple_of(number * line + offset, sub), sub), :],
                    (((1,), (1,)), ((), ())),
                    preferred_element_type=F32,
                )
                top = jnp.max(logits, axis=0, keepdims=True)
                shifted = jnp.exp(logits - top)
                stage[slot, :, offset : offset + sub] = logits if raw else shifted
                tops.append(top)
                totals.append(jnp.sum(shifted, axis=0, keepdims=True))
            stat_ref[0, pl.ds(number, 1), :] = jnp.concatenate(tops, axis=1)
            stat_ref[1, pl.ds(number, 1), :] = jnp.concatenate(totals, axis=1)
            for copy in copies(number, slot):
                copy.start()
        return carry

    steps = stat_ref.shape[1] // lines
    lax.fori_loop(0, steps, visit, 0)
    for slot in range(lines):
        for copy in copies((steps - 1) * lines + slot, slot):
            copy.wait()


def stat_shape(total):
    line = divisor(total, 512)
    return (2, total // line, line)


def first_scores_body(raw, units, x_ref, _, e_hbm, stat_ref, stage, semaphores):
    target = [(slice(None), lambda columns: e_hbm.at[:, columns])]
    score_points(raw, units, x_ref, target, stat_ref, stage, semaphores)


def next_scores_body(raw, count, pieces, away, *refs):
    unit_refs = refs[:count]
    x_ref = refs[count]
    e_hbm, stat_ref, units, stage, semaphores = refs[-5:]
    rows = unit_refs[0].shape[0]
    pair = CORES * pieces * rows
    chip, core = place()
    chips = e_hbm.shape[0] // pair
    for number, ref in enumerate(unit_refs):
        group, who, piece = number // (CORES * pieces), number // pieces % CORES, number % pieces
        of_pair = (core if who == 0 else 1 - core) * pieces + piece
        start = pl.multiple_of((group * CORES * pieces + of_pair) * rows, rows)
        units[pl.ds(start, rows), :] = ref[...]

    def target_of(number):
        start = pl.multiple_of(lax.rem(chip + away + number, chips) * pair, pair)
        return lambda columns: e_hbm.at[pl.ds(start, pair), columns]

    targets = [
        (slice(number * pair, (number + 1) * pair), target_of(number)) for number in range(count // (CORES * pieces))
    ]
    score_points(raw, units, x_ref, targets, stat_ref, stage, semaphores)


def scores(raw, blocks, points, pieces=1, away=None, shifted=None):
    total, width = points.shape
    count = len(blocks)
    rows = sum(block.shape[0] for block in blocks)
    all_rows = rows if shifted is None else shifted.shape[0]
    stat = stat_shape(total)
    parts = 1 if away is None else count // (CORES * pieces)
    more = [] if shifted is None or away == 0 else [shifted]
    scratch = [
        pltpu.VMEM((divisor(stat[1], 2), rows, stat[2]), F32),
        pltpu.SemaphoreType.DMA((divisor(stat[1], 2), parts)),
    ]
    if away is not None:
        scratch = [pltpu.VMEM((rows, width), BF16)] + scratch
    if away is None:
        body = functools.partial(first_scores_body, raw)
    else:
        body = functools.partial(next_scores_body, raw, count, pieces, away)
    return pl.pallas_call(
        body,
        in_specs=[VMEM] * (count + 1) + [ANY] * len(more),
        out_specs=[VMEM, ANY, VMEM],
        out_shape=[
            jax.ShapeDtypeStruct(points.shape, BF16),
            jax.ShapeDtypeStruct((all_rows, total), F32),
            jax.ShapeDtypeStruct(stat, F32),
        ],
        input_output_aliases={count + number: number for number in range(1 + len(more))},
        scratch_shapes=scratch,
        compiler_params=params(SCORE_VMEM),
        cost_estimate=pl.CostEstimate(
            flops=2 * rows * total * width,
            bytes_accessed=2 * total * width + 4 * rows * total,
            transcendentals=rows * total,
        ),
    )(*blocks, points, *more)


FAR, THEIRS, OWN = range(3)


def weigh_body(by_rows, n_sets, n_tops, kind, others, extra, pair, *refs):
    parts = CORES if kind == FAR else 1
    stat_refs, refs = refs[:n_sets], refs[n_sets:]
    top_refs, (e_hbm, x_ref, _), refs = refs[:n_tops], refs[n_tops : n_tops + 3], refs[n_tops + 3 :]
    out_refs, refs = refs[:parts], refs[parts + 1 :]
    if not by_rows:
        (kept_ref, kept_mass_ref), refs = refs[:2], refs[2:]
    scale_refs, refs = refs[:2], refs[2:]
    n_weights = 2 if by_rows else 0
    weights_refs, (stage, mass_ref, sum_ref, semaphores) = refs[:n_weights], refs[n_weights:]
    chip, core = place()
    line = stat_refs[0].shape[2]
    total = x_ref.shape[0]
    height, span = sum_ref.shape
    slots, _, chunk = stage.shape
    steps = total // chunk
    lanes = min(line, 128)

    def block_of(other):
        if kind == FAR:
            return lax.rem(chip + 1 + other, others + 1)
        return chip * CORES + (core if kind == OWN else 1 - core)

    def copy_of(number):
        other, step = divmod(number, steps)
        rows = pl.ds(pl.multiple_of(block_of(other) * height, height), height) if by_rows else slice(None)
        columns = slice(step * chunk, (step + 1) * chunk)
        slot = number % slots
        return pltpu.make_async_copy(e_hbm.at[rows, columns], stage.at[slot], semaphores.at[slot])

    for number in range(min(slots, others * steps)):
        copy_of(number).start()
    top, all_total = merge(stat_refs)
    if by_rows:
        scale_refs[0][...] = top
        scale_refs[1][...] = 1.0 / all_total
    else:
        for ref, scale_ref in zip((top_refs[0], top_refs[-1]), scale_refs):
            scale_ref[...] = jnp.exp(ref[0] - top) / all_total

    def weights_of(values, group, number):
        one, two = (ref[number : number + 1, :] for ref in scale_refs)
        if by_rows:
            return jnp.exp(values - one) * two
        return values * jnp.where(chip == group, one, two)

    group_rows = height if by_rows else pair
    kept = not by_rows

    def weights_part(step):
        columns = slice(step * chunk, (step + 1) * chunk)
        return kept_ref.at[:, columns] if kept else weights_refs[step % 2]

    def weigh_step(number):
        step = number % steps
        weights_ref = weights_part(step)
        for group in range(height // group_rows):
            rows = slice(group * group_rows, (group + 1) * group_rows)
            mass = None
            for offset in range(0, chunk, line):
                values = stage[number % slots, rows, offset : offset + line]
                weights = weights_of(values, group, (step * chunk + offset) // line).astype(BF16)
                weights_ref[rows, offset : offset + line] = weights
                wide = weights.astype(F32)
                for lane in range(0, line, lanes):
                    piece = wide[:, lane : lane + lanes]
                    mass = piece if mass is None else mass + piece
            mass_ref[rows, :] = mass if step == 0 else mass_ref[rows, :] + mass

    weighed = steps if kept else others * steps
    for number in range(others * steps):
        other, step = divmod(number, steps)
        if number < weighed:
            copy_of(number).wait()
            weigh_step(number)
        if number + slots < weighed:
            copy_of(number + slots).start()
        columns = slice(None)
        if not by_rows:
            columns = pl.ds(pl.multiple_of(block_of(other) * span, span), span)
        product = jnp.dot(
            weights_part(step)[...],
            x_ref[step * chunk : (step + 1) * chunk, columns],
            preferred_element_type=F32,
        )
        sum_ref[...] = product if step == 0 else sum_ref[...] + product
        if step == steps - 1:
            mass = jnp.sum(mass_ref[...].T, axis=0, keepdims=True)
            if kept:
                kept_mass_ref[...] = mass
            write_sums(by_rows, other, core, out_refs, sum_ref, mass, extra)


def write_sums(by_rows, other, core, out_refs, sum_ref, mass, extra):
    parts = len(out_refs)
    rows = out_refs[0].shape[1] - extra
    width = out_refs[0].shape[2]
    for part, ref in enumerate(out_refs):
        side = lax.rem(core + part, parts)
        ref[other, rows:, :] = jnp.zeros((extra, width), F32)
        if by_rows:
            found = mass
            if parts > 1:
                found = jnp.where(side == 0, mass[:, :rows], mass[:, rows:])
                ref[other, :rows, :] = sum_ref[pl.ds(pl.multiple_of(side * rows, rows), rows), :]
            else:
                ref[other, :rows, :] = sum_ref[...]
            ref[other, rows : rows + 1, :rows] = found
        else:
            sums = sum_ref[...]
            if parts > 1:
                sums = jnp.where(side == 0, sums[:, :width], sums[:, width:])
            ref[other, :rows, :] = sums
            for number in range(rows // width):
                ref[other, rows + number : rows + number + 1, :] = mass[
                    :, number * width : (number + 1) * width
                ]


def weigh_kept_body(kind, extra, kept_ref, mass_ref, x_ref, _, out_ref, kept_out, x_out, sum_ref):
    chip, core = place()
    span = sum_ref.shape[1]
    total = x_ref.shape[0]
    block = chip * CORES + (core if kind == OWN else 1 - core)
    columns = pl.ds(pl.multiple_of(block * span, span), span)
    sum_ref[...] = jnp.dot(kept_ref[...], x_ref[:, columns], preferred_element_type=F32)
    write_sums(False, 0, core, [out_ref], sum_ref, mass_ref[...], extra)


def weigh_kept(kind, n_pts, kept, mass, points, after):
    total, width = points.shape
    rows, cols = kept.shape[0], width // n_pts
    extra = round_up(-(-rows // cols), 8)
    return pl.pallas_call(
        functools.partial(weigh_kept_body, kind, extra),
        in_specs=[VMEM] * 3 + [ANY],
        out_specs=[VMEM] * 3,
        input_output_aliases={0: 1, 2: 2},
        scratch_shapes=[pltpu.VMEM((rows, cols), F32)],
        out_shape=[
            jax.ShapeDtypeStruct((1, rows + extra, cols), F32),
            jax.ShapeDtypeStruct(kept.shape, BF16),
            jax.ShapeDtypeStruct(points.shape, BF16),
        ],
        compiler_params=params(KEPT_VMEM),
        cost_estimate=pl.CostEstimate(
            flops=2 * rows * cols * total, bytes_accessed=2 * total * (rows + cols), transcendentals=0
        ),
    )(kept, mass, points, after)


def weigh(by_rows, kind, chips, stats, tops, shifted, points, after):
    total, width = points.shape
    pair = shifted.shape[0] // chips
    parts, others = (CORES, chips - 1) if kind == FAR else (1, 1)
    line = stats[0].shape[2]
    chunk = line * divisor(total // line, CHUNK_LINES)
    slots = min(WEIGH_SLOTS, total // chunk)
    kept = []
    if not by_rows:
        kept = [
            jax.ShapeDtypeStruct((shifted.shape[0], total), BF16),
            jax.ShapeDtypeStruct((1, shifted.shape[0]), F32),
        ]
    if by_rows:
        rows, cols = pair // CORES, width
        sums = (rows * parts, width)
    else:
        rows, cols = shifted.shape[0], width // (CORES * chips)
        sums = (rows, cols * parts)
    n_tops = len(tops)
    extra = round_up(-(-rows // cols), 8)
    return pl.pallas_call(
        functools.partial(weigh_body, by_rows, len(stats), n_tops, kind, others, extra, pair),
        in_specs=[VMEM] * (len(stats) + n_tops) + [ANY, VMEM, ANY],
        out_specs=[VMEM] * (parts + (1 if by_rows else 3)),
        input_output_aliases={len(stats) + n_tops + 1: parts},
        scratch_shapes=[pltpu.VMEM(stats[0].shape[1:], F32)] * 2
        + [pltpu.VMEM((sums[0], chunk), BF16)] * (2 if by_rows else 0)
        + [
            pltpu.VMEM((slots, sums[0], chunk), F32),
            pltpu.VMEM((sums[0], 128), F32),
            pltpu.VMEM(sums, F32),
            pltpu.SemaphoreType.DMA((slots,)),
        ],
        out_shape=[jax.ShapeDtypeStruct((others, rows + extra, cols), F32)] * parts
        + [jax.ShapeDtypeStruct(points.shape, BF16)]
        + kept,
        compiler_params=params(WEIGH_VMEM),
        cost_estimate=pl.CostEstimate(
            flops=2 * others * sums[0] * sums[1] * total,
            bytes_accessed=2 * others * total * (sums[1] + 2 * sums[0]),
            transcendentals=0,
        ),
    )(*stats, *tops, shifted, points, after)


def fold_body(rows, lines, pieces, mine_ref, theirs_ref, after_ref, *out_refs):
    width = out_refs[0].shape[1]
    count = rows // pieces
    step = divisor(count, 128) if lines == 1 else width
    all_masses = mine_ref[rows : rows + lines, :] + theirs_ref[rows : rows + lines, :]
    for piece, out_ref in enumerate(out_refs):
        out_ref[count:, :] = jnp.zeros((out_ref.shape[0] - count, width), BF16)
        scales = []
        for start in range(0, count, step):
            part = slice(piece * count + start, piece * count + start + step)
            total = mine_ref[part, :] + theirs_ref[part, :]
            top = jnp.max(jnp.abs(total), axis=1, keepdims=True)
            scale = jnp.maximum(top * 1.01, 1e-30).astype(BF16).astype(F32)
            out_ref[start : start + step, :] = encode(total, scale)
            scales.append(jnp.broadcast_to(scale, (step, 128)).T[0:1, :])
        if lines == 1:
            out_ref[count : count + 1, :count] = jnp.concatenate(scales, axis=1).astype(BF16)
            mass, used = all_masses[:, piece * count : (piece + 1) * count], slice(0, count)
        else:
            out_ref[count : count + lines, :] = jnp.concatenate(scales, axis=0).astype(BF16)
            mass, used = all_masses, slice(None)
        for number in range(1, 4):
            rounded = mass.astype(BF16)
            out_ref[count + number * lines : count + (number + 1) * lines, used] = rounded
            mass = mass - rounded.astype(F32)


def fold(pieces, mine, theirs, after):
    others, height, width = mine.shape
    rows, lines = shape_of(height, width)
    coded = (rows // pieces + round_up(4 * lines, 16), width)
    return pl.pallas_call(
        functools.partial(fold_body, rows, lines, pieces),
        grid=(others,),
        in_specs=[pl.BlockSpec((None, height, width), lambda d: (d, 0, 0))] * 2 + [ANY],
        out_specs=[pl.BlockSpec((None, *coded), lambda d: (d, 0, 0))] * pieces,
        out_shape=[jax.ShapeDtypeStruct((others, *coded), BF16)] * pieces,
        compiler_params=params(10),
        cost_estimate=pl.CostEstimate(
            flops=20 * others * height * width,
            bytes_accessed=10 * others * height * width,
            transcendentals=others * height * width,
        ),
    )(mine, theirs, after)


def shape_of(height, width):
    rows = height - 8
    while rows + round_up(-(-rows // width), 8) != height:
        rows -= 8
    return rows, -(-rows // width)


def finish_body(rows, lines, piece, as_units, mine_ref, theirs_ref, *refs):
    code_refs, (_, out_ref) = refs[:-2], refs[-2:]
    count, width = out_ref.shape
    step = divisor(count, 128) if lines == 1 else width
    mass = mine_ref[rows : rows + lines, :] + theirs_ref[rows : rows + lines, :]
    if lines == 1:
        mass = mass[:, piece * count : (piece + 1) * count]
    used = slice(0, count) if lines == 1 else slice(None)
    for ref in code_refs:
        for number in range(1, 4):
            start = count + number * lines
            mass = mass + ref[start : start + lines, used].astype(F32)

    def column(values, number):
        if lines == 1:
            line = values[:, number * step : (number + 1) * step]
        else:
            line = values[number : number + 1, :]
        return to_column(line, step)[:, 0:1]

    scales = [ref[count : count + lines, used].astype(F32) for ref in code_refs]
    for number in range(count // step):
        part = slice(number * step, (number + 1) * step)
        near = slice(piece * count + number * step, piece * count + (number + 1) * step)
        total = mine_ref[near, :] + theirs_ref[near, :]
        for ref, scale in zip(code_refs, scales):
            total = total + decode(ref[part, :], column(scale, number))
        means = total / jnp.maximum(column(mass, number), 1.0)
        out_ref[part, :] = normalize_rows(means).astype(BF16) if as_units else means


def finish(as_units, piece, pieces, mine, theirs, codes, after):
    height, width = mine.shape
    rows, lines = shape_of(height, width)
    count = rows // pieces
    return pl.pallas_call(
        functools.partial(finish_body, rows, lines, piece, as_units),
        in_specs=[VMEM] * (2 + len(codes)) + [ANY],
        out_specs=VMEM,
        out_shape=jax.ShapeDtypeStruct((count, width), BF16 if as_units else F32),
        compiler_params=params(10),
        cost_estimate=pl.CostEstimate(
            flops=30 * count * width,
            bytes_accessed=(12 + 2 * len(codes)) * count * width,
            transcendentals=2 * count * width,
        ),
    )(mine, theirs, *codes, after)


def keep_body(value_ref, after_ref, out_ref):
    pass


def keep_until(value, after):
    return pl.pallas_call(
        keep_body,
        in_specs=[VMEM, ANY],
        out_specs=VMEM,
        out_shape=jax.ShapeDtypeStruct(value.shape, value.dtype),
        input_output_aliases={0: 0},
        compiler_params=params(10),
    )(value, after)


def merge_body(*refs):
    refs[-1][0], refs[-1][1] = merge(refs[:-1])


def merged(sets):
    return pl.pallas_call(
        merge_body, out_shape=jax.ShapeDtypeStruct(sets[0].shape, F32), compiler_params=params(10)
    )(*sets)


def log_body(*refs):
    top, total = merge(refs[:-1])
    refs[-1][...] = top + jnp.log(total)


def log_norms(sets):
    return pl.pallas_call(
        log_body, out_shape=jax.ShapeDtypeStruct(sets[0].shape[1:], F32), compiler_params=params(10)
    )(*sets).reshape(-1)


def on_device(n_pts, n_cen, points, centroids):
    chips = n_pts // CORES

    def to_partner(value):
        return lax.ppermute(value, "pts", [(i, i ^ 1) for i in range(n_pts)])

    def to_chip(value, away):
        moves = [(i, (i + CORES * away) % n_pts) for i in range(n_pts)]
        return lax.ppermute(value, "pts", moves)

    def over_centroids(stats):
        if n_cen & (n_cen - 1):
            moves = [[(i, (i + away) % n_cen) for i in range(n_cen)] for away in range(1, n_cen)]
            return [stats] + [lax.ppermute(stats, "cen", move) for move in moves]
        done, sets = 1, [stats]
        while done < n_cen:
            if done > 1:
                sets = [merged(sets)]
            ways = 4 if (n_cen // done).bit_length() % 2 else 2
            for way in range(1, ways):
                moves = [(i, i ^ (way * done)) for i in range(n_cen)]
                sets.append(lax.ppermute(sets[0], "cen", moves))
            done *= ways
        return sets

    def sums_over_pts(by_rows, stats, tops, shifted, points):
        kept = mass = None

        def weighted(kind, after):
            nonlocal points, kept, mass
            if by_rows:
                *found, points = weigh(by_rows, kind, chips, stats, tops, shifted, points, after)
                return found
            if kind == FAR:
                *found, points, kept, mass = weigh(by_rows, kind, chips, stats, tops, shifted, points, after)
                return found
            *found, kept, points = weigh_kept(kind, n_pts, kept, mass, points, after)
            return found

        far_mine, far_theirs = weighted(FAR, stats[0])
        far_found = to_partner(far_theirs)
        (near_theirs,) = weighted(THEIRS, far_theirs)
        near_found = to_partner(near_theirs)
        coded = fold(pieces if by_rows else 1, far_mine, far_found, near_theirs)
        codes = [[to_chip(each[away - 1], away) for away in range(1, chips)] for each in coded]
        (near_mine,) = weighted(OWN, coded[0])
        found, away_found, after = [], [], coded[0]
        for piece, each in enumerate(codes):
            found.append(finish(by_rows, piece, len(codes), near_mine[0], near_found[0], each, after))
            if by_rows:
                away_found.append([to_chip(found[-1], -away) for away in range(1, chips)])
                after = away_found[-1][-1]
        return found, away_found, points

    block = centroids.shape[0] // n_pts
    pieces = 2 if block % 256 == 0 else 1
    points, units = load(centroids, points)
    points, shifted, own = scores(ITERS > 1, [units], points)
    stats = over_centroids(own)
    tops = [own]
    for iteration in range(1, ITERS):
        raw = iteration + 1 < ITERS
        mine, away_mine, points = sums_over_pts(True, stats, tops, shifted, points)
        near_units = mine + [to_partner(unit) for unit in mine]
        points, shifted, near_own = scores(raw, near_units, points, pieces, 0, shifted)
        far_units = []
        for units in zip(*away_mine):
            units = [keep_until(unit, near_own) for unit in units]
            far_units += units + [to_partner(unit) for unit in units]
        points, shifted, far_own = scores(raw, far_units, points, pieces, 1, shifted)
        tops = [near_own, far_own]
        stats = over_centroids(merged([near_own, far_own]))
    (means,), _, _ = sums_over_pts(False, stats, tops, shifted, points)
    return (means, log_norms(stats))


def solution(mesh):
    placed = (P("pts", None), P("cen", None))
    return jax.shard_map(
        functools.partial(on_device, mesh.shape["pts"], mesh.shape["cen"]),
        mesh=mesh,
        in_specs=placed,
        out_specs=(P("cen", "pts"), P("pts")),
        check_vma=False,
    )
```

```python
import functools

import jax
import jax.numpy as jnp
from jax import lax
from jax.experimental import pallas as pl
from jax.experimental.pallas import tpu as pltpu
from jax.sharding import PartitionSpec as P

ITERS = 2
F32 = jnp.float32
BF16 = jnp.bfloat16
LOAD_VMEM = 38
SCORE_VMEM = 34
WEIGH_VMEM = 34
KEPT_VMEM = 20
CHUNK_LINES = 2
WEIGH_SLOTS = 2
LEVELS = 30000.0
LOWEST = -117.0


def divisor(total, wanted):
    size = min(total, wanted)
    while total % size:
        size -= 1
    return size


def round_up(value, unit):
    return -(-value // unit) * unit


def normalize_rows(rows):
    return rows * lax.rsqrt(jnp.sum(rows * rows, axis=1, keepdims=True) + 1e-06)


CORES = 2


def place():
    me = lax.axis_index("pts")
    return lax.div(me, CORES), lax.rem(me, CORES)


def params(mebibytes):
    return pltpu.CompilerParams(vmem_limit_bytes=mebibytes * 2**20)


VMEM = pl.BlockSpec(memory_space=pltpu.VMEM)
ANY = pl.BlockSpec(memory_space=pl.ANY)


def merge(sets):
    top = functools.reduce(jnp.maximum, [stats[0] for stats in sets])
    return top, functools.reduce(jnp.add, [stats[1] * jnp.exp(stats[0] - top) for stats in sets])


def to_column(row, height):
    return jnp.broadcast_to(row, (128, height)).T


def encode(values, scale):
    steps = jnp.floor(jnp.abs(values) * (LEVELS / scale) + 0.5)
    power = jnp.floor(steps * (1.0 / 128.0))
    size = (1.0 + (steps * (1.0 / 128.0) - power)) * jnp.exp2(power + LOWEST)
    return jnp.where(values < 0.0, -size, size).astype(BF16)


def decode(codes, scale):
    wide = codes.astype(F32)
    size = jnp.abs(wide)
    power = jnp.floor(jnp.log2(size))
    steps = 128.0 * (power - LOWEST + (size * jnp.exp2(-power) - 1.0))
    return jnp.where(wide < 0.0, -steps, steps) * (scale * (1.0 / LEVELS))


def first_units_body(c_ref, sums_ref, units_ref):
    step = divisor(units_ref.shape[0], 128)
    for start in range(0, units_ref.shape[0], step):
        part = slice(start, start + step)
        scale = to_column(lax.rsqrt(sums_ref[:, part] + 1e-06), step)[:, 0:1]
        units_ref[part, :] = (c_ref[part, :] * scale).astype(BF16)


def first_units(centroids):
    square_sums = jnp.sum(centroids * centroids, axis=1)[None]
    return pl.pallas_call(
        first_units_body,
        in_specs=[VMEM, VMEM],
        out_specs=VMEM,
        out_shape=jax.ShapeDtypeStruct(centroids.shape, BF16),
        compiler_params=params(10),
        cost_estimate=pl.CostEstimate(
            flops=4 * centroids.size, bytes_accessed=4 * centroids.size, transcendentals=0
        ),
    )(centroids, square_sums)


def score_points(raw, units, x_ref, e_parts, stat_ref, stage, semaphores):
    line = stat_ref.shape[2]
    lines = stage.shape[0]
    sub = divisor(line, 256)

    def copies(number, slot):
        columns = pl.ds(pl.multiple_of(number * line, line), line)
        return [
            pltpu.make_async_copy(stage.at[slot, rows, :], target(columns), semaphores.at[slot, part])
            for part, (rows, target) in enumerate(e_parts)
        ]

    def visit(step, carry):
        for slot in range(lines):
            number = step * lines + slot

            @pl.when(step > 0)
            def _():
                for copy in copies(number - lines, slot):
                    copy.wait()

            tops, totals = [], []
            for offset in range(0, line, sub):
                logits = lax.dot_general(
                    units[...],
                    x_ref[pl.ds(pl.multiple_of(number * line + offset, sub), sub), :],
                    (((1,), (1,)), ((), ())),
                    preferred_element_type=F32,
                )
                top = jnp.max(logits, axis=0, keepdims=True)
                shifted = jnp.exp(logits - top)
                stage[slot, :, offset : offset + sub] = logits if raw else shifted
                tops.append(top)
                totals.append(jnp.sum(shifted, axis=0, keepdims=True))
            stat_ref[0, pl.ds(number, 1), :] = jnp.concatenate(tops, axis=1)
            stat_ref[1, pl.ds(number, 1), :] = jnp.concatenate(totals, axis=1)
            for copy in copies(number, slot):
                copy.start()
        return carry

    steps = stat_ref.shape[1] // lines
    lax.fori_loop(0, steps, visit, 0)
    for slot in range(lines):
        for copy in copies((steps - 1) * lines + slot, slot):
            copy.wait()


def stat_shape(total):
    line = divisor(total, 512)
    return (2, total // line, line)


def first_scores_body(raw, units, x_ref, e_hbm, stat_ref, stage, semaphores):
    target = [(slice(None), lambda columns: e_hbm.at[:, columns])]
    score_points(raw, units, x_ref, target, stat_ref, stage, semaphores)


def next_scores_body(raw, count, pieces, away, *refs):
    unit_refs = refs[:count]
    x_ref = refs[count]
    e_hbm, stat_ref, units, stage, semaphores = refs[-5:]
    rows = unit_refs[0].shape[0]
    pair = CORES * pieces * rows
    chip, core = place()
    chips = e_hbm.shape[0] // pair
    for number, ref in enumerate(unit_refs):
        group, who, piece = number // (CORES * pieces), number // pieces % CORES, number % pieces
        of_pair = (core if who == 0 else 1 - core) * pieces + piece
        start = pl.multiple_of((group * CORES * pieces + of_pair) * rows, rows)
        units[pl.ds(start, rows), :] = ref[...]

    def target_of(number):
        start = pl.multiple_of(lax.rem(chip + away + number, chips) * pair, pair)
        return lambda columns: e_hbm.at[pl.ds(start, pair), columns]

    targets = [
        (slice(number * pair, (number + 1) * pair), target_of(number)) for number in range(count // (CORES * pieces))
    ]
    score_points(raw, units, x_ref, targets, stat_ref, stage, semaphores)


def scores(raw, blocks, points, pieces=1, away=None, shifted=None):
    total, width = points.shape
    count = len(blocks)
    rows = sum(block.shape[0] for block in blocks)
    all_rows = rows if shifted is None else shifted.shape[0]
    stat = stat_shape(total)
    parts = 1 if away is None else count // (CORES * pieces)
    more = [] if shifted is None or away == 0 else [shifted]
    scratch = [
        pltpu.VMEM((divisor(stat[1], 2), rows, stat[2]), F32),
        pltpu.SemaphoreType.DMA((divisor(stat[1], 2), parts)),
    ]
    if away is not None:
        scratch = [pltpu.VMEM((rows, width), BF16)] + scratch
    if away is None:
        body = functools.partial(first_scores_body, raw)
    else:
        body = functools.partial(next_scores_body, raw, count, pieces, away)
    return pl.pallas_call(
        body,
        in_specs=[VMEM] * (count + 1) + [ANY] * len(more),
        out_specs=[ANY, VMEM],
        out_shape=[
            jax.ShapeDtypeStruct((all_rows, total), F32),
            jax.ShapeDtypeStruct(stat, F32),
        ],
        input_output_aliases={count + 1: 0} if more else {},
        scratch_shapes=scratch,
        compiler_params=params(SCORE_VMEM),
        cost_estimate=pl.CostEstimate(
            flops=2 * rows * total * width,
            bytes_accessed=2 * total * width + 4 * rows * total,
            transcendentals=rows * total,
        ),
    )(*blocks, points, *more)


FAR, THEIRS, OWN = range(3)


def weigh_body(by_rows, n_sets, n_tops, kind, others, extra, pair, *refs):
    parts = CORES if kind == FAR else 1
    stat_refs, refs = refs[:n_sets], refs[n_sets:]
    top_refs, (e_hbm, x_ref, _), refs = refs[:n_tops], refs[n_tops : n_tops + 3], refs[n_tops + 3 :]
    out_refs, refs = refs[:parts], refs[parts:]
    if not by_rows:
        (kept_ref, kept_mass_ref), refs = refs[:2], refs[2:]
    scale_refs, refs = refs[:2], refs[2:]
    n_weights = 2 if by_rows else 0
    weights_refs, (stage, mass_ref, sum_ref, semaphores) = refs[:n_weights], refs[n_weights:]
    chip, core = place()
    line = stat_refs[0].shape[2]
    total = x_ref.shape[0]
    height, span = sum_ref.shape
    slots, _, chunk = stage.shape
    steps = total // chunk
    lanes = min(line, 128)

    def block_of(other):
        if kind == FAR:
            return lax.rem(chip + 1 + other, others + 1)
        return chip * CORES + (core if kind == OWN else 1 - core)

    def copy_of(number):
        other, step = divmod(number, steps)
        rows = pl.ds(pl.multiple_of(block_of(other) * height, height), height) if by_rows else slice(None)
        columns = slice(step * chunk, (step + 1) * chunk)
        slot = number % slots
        return pltpu.make_async_copy(e_hbm.at[rows, columns], stage.at[slot], semaphores.at[slot])

    for number in range(min(slots, others * steps)):
        copy_of(number).start()
    top, all_total = merge(stat_refs)
    if by_rows:
        scale_refs[0][...] = top
        scale_refs[1][...] = 1.0 / all_total
    else:
        for ref, scale_ref in zip((top_refs[0], top_refs[-1]), scale_refs):
            scale_ref[...] = jnp.exp(ref[0] - top) / all_total

    def weights_of(values, group, number):
        one, two = (ref[number : number + 1, :] for ref in scale_refs)
        if by_rows:
            return jnp.exp(values - one) * two
        return values * jnp.where(chip == group, one, two)

    group_rows = height if by_rows else pair
    kept = not by_rows

    def weights_part(step):
        columns = slice(step * chunk, (step + 1) * chunk)
        return kept_ref.at[:, columns] if kept else weights_refs[step % 2]

    def weigh_step(number):
        step = number % steps
        weights_ref = weights_part(step)
        for group in range(height // group_rows):
            rows = slice(group * group_rows, (group + 1) * group_rows)
            mass = None
            for offset in range(0, chunk, line):
                values = stage[number % slots, rows, offset : offset + line]
                weights = weights_of(values, group, (step * chunk + offset) // line).astype(BF16)
                weights_ref[rows, offset : offset + line] = weights
                wide = weights.astype(F32)
                for lane in range(0, line, lanes):
                    piece = wide[:, lane : lane + lanes]
                    mass = piece if mass is None else mass + piece
            mass_ref[rows, :] = mass if step == 0 else mass_ref[rows, :] + mass

    weighed = steps if kept else others * steps
    for number in range(others * steps):
        other, step = divmod(number, steps)
        if number < weighed:
            copy_of(number).wait()
            weigh_step(number)
        if number + slots < weighed:
            copy_of(number + slots).start()
        columns = slice(None)
        if not by_rows:
            columns = pl.ds(pl.multiple_of(block_of(other) * span, span), span)
        product = jnp.dot(
            weights_part(step)[...],
            x_ref[step * chunk : (step + 1) * chunk, columns],
            preferred_element_type=F32,
        )
        sum_ref[...] = product if step == 0 else sum_ref[...] + product
        if step == steps - 1:
            mass = jnp.sum(mass_ref[...].T, axis=0, keepdims=True)
            if kept:
                kept_mass_ref[...] = mass
            write_sums(by_rows, other, core, out_refs, sum_ref, mass, extra)


def write_sums(by_rows, other, core, out_refs, sum_ref, mass, extra):
    parts = len(out_refs)
    rows = out_refs[0].shape[1] - extra
    width = out_refs[0].shape[2]
    for part, ref in enumerate(out_refs):
        side = lax.rem(core + part, parts)
        ref[other, rows:, :] = jnp.zeros((extra, width), F32)
        if by_rows:
            found = mass
            if parts > 1:
                found = jnp.where(side == 0, mass[:, :rows], mass[:, rows:])
                ref[other, :rows, :] = sum_ref[pl.ds(pl.multiple_of(side * rows, rows), rows), :]
            else:
                ref[other, :rows, :] = sum_ref[...]
            ref[other, rows : rows + 1, :rows] = found
        else:
            sums = sum_ref[...]
            if parts > 1:
                sums = jnp.where(side == 0, sums[:, :width], sums[:, width:])
            ref[other, :rows, :] = sums
            for number in range(rows // width):
                ref[other, rows + number : rows + number + 1, :] = mass[
                    :, number * width : (number + 1) * width
                ]


def weigh_kept_body(kind, extra, kept_ref, mass_ref, x_ref, _, out_ref, kept_out, sum_ref):
    chip, core = place()
    span = sum_ref.shape[1]
    total = x_ref.shape[0]
    block = chip * CORES + (core if kind == OWN else 1 - core)
    columns = pl.ds(pl.multiple_of(block * span, span), span)
    sum_ref[...] = jnp.dot(kept_ref[...], x_ref[:, columns], preferred_element_type=F32)
    write_sums(False, 0, core, [out_ref], sum_ref, mass_ref[...], extra)


def weigh_kept(kind, n_pts, kept, mass, points, after):
    total, width = points.shape
    rows, cols = kept.shape[0], width // n_pts
    extra = round_up(-(-rows // cols), 8)
    return pl.pallas_call(
        functools.partial(weigh_kept_body, kind, extra),
        in_specs=[VMEM] * 3 + [ANY],
        out_specs=[VMEM] * 2,
        input_output_aliases={0: 1},
        scratch_shapes=[pltpu.VMEM((rows, cols), F32)],
        out_shape=[
            jax.ShapeDtypeStruct((1, rows + extra, cols), F32),
            jax.ShapeDtypeStruct(kept.shape, BF16),
        ],
        compiler_params=params(KEPT_VMEM),
        cost_estimate=pl.CostEstimate(
            flops=2 * rows * cols * total, bytes_accessed=2 * total * (rows + cols), transcendentals=0
        ),
    )(kept, mass, points, after)


def weigh(by_rows, kind, chips, stats, tops, shifted, points, after):
    total, width = points.shape
    pair = shifted.shape[0] // chips
    parts, others = (CORES, chips - 1) if kind == FAR else (1, 1)
    line = stats[0].shape[2]
    chunk = line * divisor(total // line, CHUNK_LINES)
    slots = min(WEIGH_SLOTS, total // chunk)
    kept = []
    if not by_rows:
        kept = [
            jax.ShapeDtypeStruct((shifted.shape[0], total), BF16),
            jax.ShapeDtypeStruct((1, shifted.shape[0]), F32),
        ]
    if by_rows:
        rows, cols = pair // CORES, width
        sums = (rows * parts, width)
    else:
        rows, cols = shifted.shape[0], width // (CORES * chips)
        sums = (rows, cols * parts)
    n_tops = len(tops)
    extra = round_up(-(-rows // cols), 8)
    return pl.pallas_call(
        functools.partial(weigh_body, by_rows, len(stats), n_tops, kind, others, extra, pair),
        in_specs=[VMEM] * (len(stats) + n_tops) + [ANY, VMEM, ANY],
        out_specs=[VMEM] * (parts + len(kept)),
        scratch_shapes=[pltpu.VMEM(stats[0].shape[1:], F32)] * 2
        + [pltpu.VMEM((sums[0], chunk), BF16)] * (2 if by_rows else 0)
        + [
            pltpu.VMEM((slots, sums[0], chunk), F32),
            pltpu.VMEM((sums[0], 128), F32),
            pltpu.VMEM(sums, F32),
            pltpu.SemaphoreType.DMA((slots,)),
        ],
        out_shape=[jax.ShapeDtypeStruct((others, rows + extra, cols), F32)] * parts
        + kept,
        compiler_params=params(WEIGH_VMEM),
        cost_estimate=pl.CostEstimate(
            flops=2 * others * sums[0] * sums[1] * total,
            bytes_accessed=2 * others * total * (sums[1] + 2 * sums[0]),
            transcendentals=0,
        ),
    )(*stats, *tops, shifted, points, after)


def fold_body(rows, lines, pieces, mine_ref, theirs_ref, after_ref, *out_refs):
    width = out_refs[0].shape[1]
    count = rows // pieces
    step = divisor(count, 128) if lines == 1 else width
    all_masses = mine_ref[rows : rows + lines, :] + theirs_ref[rows : rows + lines, :]
    for piece, out_ref in enumerate(out_refs):
        out_ref[count:, :] = jnp.zeros((out_ref.shape[0] - count, width), BF16)
        scales = []
        for start in range(0, count, step):
            part = slice(piece * count + start, piece * count + start + step)
            total = mine_ref[part, :] + theirs_ref[part, :]
            top = jnp.max(jnp.abs(total), axis=1, keepdims=True)
            scale = jnp.maximum(top * 1.01, 1e-30).astype(BF16).astype(F32)
            out_ref[start : start + step, :] = encode(total, scale)
            scales.append(jnp.broadcast_to(scale, (step, 128)).T[0:1, :])
        if lines == 1:
            out_ref[count : count + 1, :count] = jnp.concatenate(scales, axis=1).astype(BF16)
            mass, used = all_masses[:, piece * count : (piece + 1) * count], slice(0, count)
        else:
            out_ref[count : count + lines, :] = jnp.concatenate(scales, axis=0).astype(BF16)
            mass, used = all_masses, slice(None)
        for number in range(1, 4):
            rounded = mass.astype(BF16)
            out_ref[count + number * lines : count + (number + 1) * lines, used] = rounded
            mass = mass - rounded.astype(F32)


def fold(pieces, mine, theirs, after):
    others, height, width = mine.shape
    rows, lines = shape_of(height, width)
    coded = (rows // pieces + round_up(4 * lines, 16), width)
    return pl.pallas_call(
        functools.partial(fold_body, rows, lines, pieces),
        grid=(others,),
        in_specs=[pl.BlockSpec((None, height, width), lambda d: (d, 0, 0))] * 2 + [ANY],
        out_specs=[pl.BlockSpec((None, *coded), lambda d: (d, 0, 0))] * pieces,
        out_shape=[jax.ShapeDtypeStruct((others, *coded), BF16)] * pieces,
        compiler_params=params(10),
        cost_estimate=pl.CostEstimate(
            flops=20 * others * height * width,
            bytes_accessed=10 * others * height * width,
            transcendentals=others * height * width,
        ),
    )(mine, theirs, after)


def shape_of(height, width):
    rows = height - 8
    while rows + round_up(-(-rows // width), 8) != height:
        rows -= 8
    return rows, -(-rows // width)


def finish_body(rows, lines, piece, as_units, mine_ref, theirs_ref, *refs):
    code_refs, (_, out_ref) = refs[:-2], refs[-2:]
    count, width = out_ref.shape
    step = divisor(count, 128) if lines == 1 else width
    mass = mine_ref[rows : rows + lines, :] + theirs_ref[rows : rows + lines, :]
    if lines == 1:
        mass = mass[:, piece * count : (piece + 1) * count]
    used = slice(0, count) if lines == 1 else slice(None)
    for ref in code_refs:
        for number in range(1, 4):
            start = count + number * lines
            mass = mass + ref[start : start + lines, used].astype(F32)

    def column(values, number):
        if lines == 1:
            line = values[:, number * step : (number + 1) * step]
        else:
            line = values[number : number + 1, :]
        return to_column(line, step)[:, 0:1]

    scales = [ref[count : count + lines, used].astype(F32) for ref in code_refs]
    for number in range(count // step):
        part = slice(number * step, (number + 1) * step)
        near = slice(piece * count + number * step, piece * count + (number + 1) * step)
        total = mine_ref[near, :] + theirs_ref[near, :]
        for ref, scale in zip(code_refs, scales):
            total = total + decode(ref[part, :], column(scale, number))
        means = total / jnp.maximum(column(mass, number), 1.0)
        out_ref[part, :] = normalize_rows(means).astype(BF16) if as_units else means


def finish(as_units, piece, pieces, mine, theirs, codes, after):
    height, width = mine.shape
    rows, lines = shape_of(height, width)
    count = rows // pieces
    return pl.pallas_call(
        functools.partial(finish_body, rows, lines, piece, as_units),
        in_specs=[VMEM] * (2 + len(codes)) + [ANY],
        out_specs=VMEM,
        out_shape=jax.ShapeDtypeStruct((count, width), BF16 if as_units else F32),
        compiler_params=params(10),
        cost_estimate=pl.CostEstimate(
            flops=30 * count * width,
            bytes_accessed=(12 + 2 * len(codes)) * count * width,
            transcendentals=2 * count * width,
        ),
    )(mine, theirs, *codes, after)


def keep_body(value_ref, after_ref, out_ref):
    pass


def keep_until(value, after):
    return pl.pallas_call(
        keep_body,
        in_specs=[VMEM, ANY],
        out_specs=VMEM,
        out_shape=jax.ShapeDtypeStruct(value.shape, value.dtype),
        input_output_aliases={0: 0},
        compiler_params=params(10),
    )(value, after)


def merge_body(*refs):
    refs[-1][0], refs[-1][1] = merge(refs[:-1])


def merged(sets):
    return pl.pallas_call(
        merge_body, out_shape=jax.ShapeDtypeStruct(sets[0].shape, F32), compiler_params=params(10)
    )(*sets)


def log_body(*refs):
    top, total = merge(refs[:-1])
    refs[-1][...] = top + jnp.log(total)


def log_norms(sets):
    return pl.pallas_call(
        log_body, out_shape=jax.ShapeDtypeStruct(sets[0].shape[1:], F32), compiler_params=params(10)
    )(*sets).reshape(-1)


def on_device(n_pts, n_cen, points, centroids):
    chips = n_pts // CORES

    def to_partner(value):
        return lax.ppermute(value, "pts", [(i, i ^ 1) for i in range(n_pts)])

    def to_chip(value, away):
        moves = [(i, (i + CORES * away) % n_pts) for i in range(n_pts)]
        return lax.ppermute(value, "pts", moves)

    def over_centroids(stats):
        if n_cen & (n_cen - 1):
            moves = [[(i, (i + away) % n_cen) for i in range(n_cen)] for away in range(1, n_cen)]
            return [stats] + [lax.ppermute(stats, "cen", move) for move in moves]
        done, sets = 1, [stats]
        while done < n_cen:
            if done > 1:
                sets = [merged(sets)]
            ways = 4 if (n_cen // done).bit_length() % 2 else 2
            for way in range(1, ways):
                moves = [(i, i ^ (way * done)) for i in range(n_cen)]
                sets.append(lax.ppermute(sets[0], "cen", moves))
            done *= ways
        return sets

    def sums_over_pts(by_rows, stats, tops, shifted):
        kept = mass = None

        def weighted(kind, after):
            nonlocal kept, mass
            if by_rows:
                return weigh(by_rows, kind, chips, stats, tops, shifted, points, after)
            if kind == FAR:
                *found, kept, mass = weigh(by_rows, kind, chips, stats, tops, shifted, points, after)
                return found
            *found, kept = weigh_kept(kind, n_pts, kept, mass, points, after)
            return found

        far_mine, far_theirs = weighted(FAR, stats[0])
        far_found = to_partner(far_theirs)
        (near_theirs,) = weighted(THEIRS, far_theirs)
        near_found = to_partner(near_theirs)
        coded = fold(pieces if by_rows else 1, far_mine, far_found, near_theirs)
        codes = [[to_chip(each[away - 1], away) for away in range(1, chips)] for each in coded]
        (near_mine,) = weighted(OWN, coded[0])
        found, away_found, after = [], [], coded[0]
        for piece, each in enumerate(codes):
            found.append(finish(by_rows, piece, len(codes), near_mine[0], near_found[0], each, after))
            if by_rows:
                away_found.append([to_chip(found[-1], -away) for away in range(1, chips)])
                after = away_found[-1][-1]
        return found, away_found

    pieces = 1
    units = first_units(centroids)
    shifted, own = scores(ITERS > 1, [units], points)
    stats = over_centroids(own)
    tops = [own]
    for iteration in range(1, ITERS):
        raw = iteration + 1 < ITERS
        mine, away_mine = sums_over_pts(True, stats, tops, shifted)
        near_units = mine + [to_partner(unit) for unit in mine]
        shifted, near_own = scores(raw, near_units, points, pieces, 0, shifted)
        far_units = []
        for units in zip(*away_mine):
            units = [keep_until(unit, near_own) for unit in units]
            far_units += units + [to_partner(unit) for unit in units]
        shifted, far_own = scores(raw, far_units, points, pieces, 1, shifted)
        tops = [near_own, far_own]
        stats = over_centroids(merged([near_own, far_own]))
    (means,), _ = sums_over_pts(False, stats, tops, shifted)
    return (means, log_norms(stats))


def solution(mesh):
    placed = (P("pts", None), P("cen", None))
    return jax.shard_map(
        functools.partial(on_device, mesh.shape["pts"], mesh.shape["cen"]),
        mesh=mesh,
        in_specs=placed,
        out_specs=(P("cen", "pts"), P("pts")),
        check_vma=False,
    )
```

```python
import functools

import jax
import jax.numpy as jnp
from jax import lax
from jax.experimental import pallas as pl
from jax.experimental.pallas import tpu as pltpu
from jax.sharding import PartitionSpec as P

ITERS = 2
F32 = jnp.float32
BF16 = jnp.bfloat16
LOAD_VMEM = 38
SCORE_VMEM = 34
WEIGH_VMEM = 34
KEPT_VMEM = 20
CHUNK_LINES = 2
WEIGH_SLOTS = 2
PIECES = 4
LEVELS = 30000.0
LOWEST = -117.0


def divisor(total, wanted):
    size = min(total, wanted)
    while total % size:
        size -= 1
    return size


def round_up(value, unit):
    return -(-value // unit) * unit


def normalize_rows(rows):
    return rows * lax.rsqrt(jnp.sum(rows * rows, axis=1, keepdims=True) + 1e-06)


CORES = 2


def place():
    me = lax.axis_index("pts")
    return lax.div(me, CORES), lax.rem(me, CORES)


def params(mebibytes):
    return pltpu.CompilerParams(vmem_limit_bytes=mebibytes * 2**20)


VMEM = pl.BlockSpec(memory_space=pltpu.VMEM)
ANY = pl.BlockSpec(memory_space=pl.ANY)


def merge(sets):
    top = functools.reduce(jnp.maximum, [stats[0] for stats in sets])
    return top, functools.reduce(jnp.add, [stats[1] * jnp.exp(stats[0] - top) for stats in sets])


def to_column(row, height):
    return jnp.broadcast_to(row, (128, height)).T


def encode(values, scale):
    steps = jnp.floor(jnp.abs(values) * (LEVELS / scale) + 0.5)
    power = jnp.floor(steps * (1.0 / 128.0))
    size = (1.0 + (steps * (1.0 / 128.0) - power)) * jnp.exp2(power + LOWEST)
    return jnp.where(values < 0.0, -size, size).astype(BF16)


def decode(codes, scale):
    wide = codes.astype(F32)
    size = jnp.abs(wide)
    power = jnp.floor(jnp.log2(size))
    steps = 128.0 * (power - LOWEST + (size * jnp.exp2(-power) - 1.0))
    return jnp.where(wide < 0.0, -steps, steps) * (scale * (1.0 / LEVELS))


def first_units_body(c_ref, sums_ref, units_ref):
    step = divisor(units_ref.shape[0], 128)
    for start in range(0, units_ref.shape[0], step):
        part = slice(start, start + step)
        scale = to_column(lax.rsqrt(sums_ref[:, part] + 1e-06), step)[:, 0:1]
        units_ref[part, :] = (c_ref[part, :] * scale).astype(BF16)


def copy_body(in_ref, out_ref):
    out_ref[...] = in_ref[...]


def first_units(centroids):
    centroids = pl.pallas_call(
        copy_body,
        in_specs=[VMEM],
        out_specs=VMEM,
        out_shape=jax.ShapeDtypeStruct(centroids.shape, F32),
        compiler_params=params(10),
    )(centroids)
    square_sums = jnp.sum(centroids * centroids, axis=1)[None]
    return pl.pallas_call(
        first_units_body,
        in_specs=[VMEM, VMEM],
        out_specs=VMEM,
        out_shape=jax.ShapeDtypeStruct(centroids.shape, BF16),
        compiler_params=params(10),
        cost_estimate=pl.CostEstimate(
            flops=4 * centroids.size, bytes_accessed=4 * centroids.size, transcendentals=0
        ),
    )(centroids, square_sums)


def total_of(values):
    rows, width = values.shape
    groups = divisor(rows // 8, 16)
    return jnp.sum(values.reshape(groups, rows // groups, width).sum(axis=0), axis=0, keepdims=True)


def score_points(raw, units, x_ref, e_parts, stat_ref, stage, semaphores):
    line = stat_ref.shape[2]
    lines = stage.shape[0]
    sub = divisor(line, 256)

    def copies(number, slot):
        columns = pl.ds(pl.multiple_of(number * line, line), line)
        return [
            pltpu.make_async_copy(stage.at[slot, rows, :], target(columns), semaphores.at[slot, part])
            for part, (rows, target) in enumerate(e_parts)
        ]

    def visit(step, carry):
        for slot in range(lines):
            number = step * lines + slot

            @pl.when(step > 0)
            def _():
                for copy in copies(number - lines, slot):
                    copy.wait()

            tops, totals = [], []
            for offset in range(0, line, sub):
                part = (slot, slice(None), slice(offset, offset + sub))
                stage[part] = lax.dot_general(
                    units[...],
                    x_ref[pl.ds(pl.multiple_of(number * line + offset, sub), sub), :],
                    (((1,), (1,)), ((), ())),
                    preferred_element_type=F32,
                )
                top = jnp.max(stage[part], axis=0, keepdims=True)
                shifted = jnp.exp(stage[part] - top)
                if not raw:
                    stage[part] = shifted
                tops.append(top)
                totals.append(total_of(shifted))
            stat_ref[0, pl.ds(number, 1), :] = jnp.concatenate(tops, axis=1)
            stat_ref[1, pl.ds(number, 1), :] = jnp.concatenate(totals, axis=1)
            for copy in copies(number, slot):
                copy.start()
        return carry

    steps = stat_ref.shape[1] // lines
    lax.fori_loop(0, steps, visit, 0)
    for slot in range(lines):
        for copy in copies((steps - 1) * lines + slot, slot):
            copy.wait()


def stat_shape(total):
    line = divisor(total, 512)
    return (2, total // line, line)


def first_scores_body(raw, units, x_ref, e_hbm, stat_ref, stage, semaphores):
    target = [(slice(None), lambda columns: e_hbm.at[:, columns])]
    score_points(raw, units, x_ref, target, stat_ref, stage, semaphores)


def next_scores_body(raw, count, pieces, away, *refs):
    unit_refs = refs[:count]
    x_ref = refs[count]
    e_hbm, stat_ref, units, stage, semaphores = refs[-5:]
    rows = unit_refs[0].shape[0]
    pair = CORES * pieces * rows
    chip, core = place()
    chips = e_hbm.shape[0] // pair
    for number, ref in enumerate(unit_refs):
        group, who, piece = number // (CORES * pieces), number // pieces % CORES, number % pieces
        of_pair = (core if who == 0 else 1 - core) * pieces + piece
        start = pl.multiple_of((group * CORES * pieces + of_pair) * rows, rows)
        units[pl.ds(start, rows), :] = ref[...]

    def target_of(number):
        start = pl.multiple_of(lax.rem(chip + away + number, chips) * pair, pair)
        return lambda columns: e_hbm.at[pl.ds(start, pair), columns]

    targets = [
        (slice(number * pair, (number + 1) * pair), target_of(number)) for number in range(count // (CORES * pieces))
    ]
    score_points(raw, units, x_ref, targets, stat_ref, stage, semaphores)


def scores(raw, blocks, points, pieces=1, away=None, shifted=None):
    total, width = points.shape
    count = len(blocks)
    rows = sum(block.shape[0] for block in blocks)
    all_rows = rows if shifted is None else shifted.shape[0]
    stat = stat_shape(total)
    parts = 1 if away is None else count // (CORES * pieces)
    more = [] if shifted is None or away == 0 else [shifted]
    scratch = [
        pltpu.VMEM((divisor(stat[1], 2), rows, stat[2]), F32),
        pltpu.SemaphoreType.DMA((divisor(stat[1], 2), parts)),
    ]
    if away is not None:
        scratch = [pltpu.VMEM((rows, width), BF16)] + scratch
    if away is None:
        body = functools.partial(first_scores_body, raw)
    else:
        body = functools.partial(next_scores_body, raw, count, pieces, away)
    return pl.pallas_call(
        body,
        in_specs=[VMEM] * (count + 1) + [ANY] * len(more),
        out_specs=[ANY, VMEM],
        out_shape=[
            jax.ShapeDtypeStruct((all_rows, total), F32),
            jax.ShapeDtypeStruct(stat, F32),
        ],
        input_output_aliases={count + 1: 0} if more else {},
        scratch_shapes=scratch,
        compiler_params=params(SCORE_VMEM),
        cost_estimate=pl.CostEstimate(
            flops=2 * rows * total * width,
            bytes_accessed=2 * total * width + 4 * rows * total,
            transcendentals=rows * total,
        ),
    )(*blocks, points, *more)


FAR, THEIRS, OWN = range(3)


def weigh_body(by_rows, n_sets, n_tops, n_found, cuts, kind, others, extra, pair, *refs):
    parts = CORES if kind == FAR else 1
    stat_refs, refs = refs[:n_sets], refs[n_sets:]
    top_refs, (e_hbm, x_ref, _), refs = refs[:n_tops], refs[n_tops : n_tops + 3], refs[n_tops + 3 :]
    found_refs, refs = refs[:n_found], refs[n_found:]
    cut_refs = ()
    if cuts:
        cut_refs, refs = refs[: len(cuts) - 1], refs[len(cuts) - 1 :]
        out_refs, refs = refs[-1:], refs[:-1]
    else:
        out_refs, refs = refs[:parts], refs[parts:]
    if not by_rows:
        (kept_ref, kept_mass_ref), refs = refs[:2], refs[2:]
    scale_refs, refs = refs[:2], refs[2:]
    n_weights = 2 if by_rows else 0
    weights_refs, (stage, mass_ref, sum_ref, semaphores) = refs[:n_weights], refs[n_weights:]
    chip, core = place()
    line = stat_refs[0].shape[2]
    total = x_ref.shape[0]
    height, span = sum_ref.shape
    slots, _, chunk = stage.shape
    steps = total // chunk
    lanes = min(line, 128)

    def block_of(other):
        if kind == FAR:
            return lax.rem(chip + 1 + other, others + 1)
        return chip * CORES + (core if kind == OWN else 1 - core)

    def copy_of(number):
        other, step = divmod(number, steps)
        rows = pl.ds(pl.multiple_of(block_of(other) * height, height), height) if by_rows else slice(None)
        columns = slice(step * chunk, (step + 1) * chunk)
        slot = number % slots
        return pltpu.make_async_copy(e_hbm.at[rows, columns], stage.at[slot], semaphores.at[slot])

    for number in range(min(slots, others * steps)):
        copy_of(number).start()
    top, all_total = merge(stat_refs)
    if by_rows:
        scale_refs[0][...] = top
        scale_refs[1][...] = 1.0 / all_total
    else:
        for ref, scale_ref in zip((top_refs[0], top_refs[-1]), scale_refs):
            scale_ref[...] = jnp.exp(ref[0] - top) / all_total

    def weights_of(values, group, number):
        one, two = (ref[number : number + 1, :] for ref in scale_refs)
        if by_rows:
            return jnp.exp(values - one) * two
        return values * jnp.where(chip == group, one, two)

    group_rows = height if by_rows else pair
    kept = not by_rows

    def weights_part(step):
        columns = slice(step * chunk, (step + 1) * chunk)
        return kept_ref.at[:, columns] if kept else weights_refs[step % 2]

    def weigh_step(number):
        step = number % steps
        weights_ref = weights_part(step)
        for group in range(height // group_rows):
            rows = slice(group * group_rows, (group + 1) * group_rows)
            mass = None
            for offset in range(0, chunk, line):
                values = stage[number % slots, rows, offset : offset + line]
                weights = weights_of(values, group, (step * chunk + offset) // line).astype(BF16)
                weights_ref[rows, offset : offset + line] = weights
                wide = weights.astype(F32)
                for lane in range(0, line, lanes):
                    piece = wide[:, lane : lane + lanes]
                    mass = piece if mass is None else mass + piece
            mass_ref[rows, :] = mass if step == 0 else mass_ref[rows, :] + mass

    weighed = steps if kept else others * steps
    for number in range(others * steps):
        other, step = divmod(number, steps)
        if number < weighed:
            copy_of(number).wait()
            weigh_step(number)
        if number + slots < weighed:
            copy_of(number + slots).start()
        columns = slice(None)
        if not by_rows:
            columns = pl.ds(pl.multiple_of(block_of(other) * span, span), span)
        product = jnp.dot(
            weights_part(step)[...],
            x_ref[step * chunk : (step + 1) * chunk, columns],
            preferred_element_type=F32,
        )
        sum_ref[...] = product if step == 0 else sum_ref[...] + product
        if step == steps - 1:
            mass = jnp.sum(mass_ref[...].T, axis=0, keepdims=True)
            if kept:
                kept_mass_ref[...] = mass
            write_sums(by_rows, other, core, out_refs, sum_ref, mass, extra)
    for number, ref in enumerate(cut_refs):
        ref[...] = out_refs[0][0, cuts[number] : cuts[number + 1], :]
    start = 0
    for ref in found_refs:
        out_refs[0][0, start : start + ref.shape[0], :] += ref[...]
        start += ref.shape[0]


def write_sums(by_rows, other, core, out_refs, sum_ref, mass, extra):
    parts = len(out_refs)
    rows = out_refs[0].shape[1] - extra
    width = out_refs[0].shape[2]
    for part, ref in enumerate(out_refs):
        side = lax.rem(core + part, parts)
        ref[other, rows:, :] = jnp.zeros((extra, width), F32)
        if by_rows:
            found = mass
            if parts > 1:
                found = jnp.where(side == 0, mass[:, :rows], mass[:, rows:])
                ref[other, :rows, :] = sum_ref[pl.ds(pl.multiple_of(side * rows, rows), rows), :]
            else:
                ref[other, :rows, :] = sum_ref[...]
            ref[other, rows : rows + 1, :rows] = found
        else:
            sums = sum_ref[...]
            if parts > 1:
                sums = jnp.where(side == 0, sums[:, :width], sums[:, width:])
            ref[other, :rows, :] = sums
            for number in range(rows // width):
                ref[other, rows + number : rows + number + 1, :] = mass[
                    :, number * width : (number + 1) * width
                ]


def weigh_kept_body(kind, extra, kept_ref, mass_ref, x_ref, _, out_ref, kept_out, sum_ref):
    chip, core = place()
    span = sum_ref.shape[1]
    total = x_ref.shape[0]
    block = chip * CORES + (core if kind == OWN else 1 - core)
    columns = pl.ds(pl.multiple_of(block * span, span), span)
    sum_ref[...] = jnp.dot(kept_ref[...], x_ref[:, columns], preferred_element_type=F32)
    write_sums(False, 0, core, [out_ref], sum_ref, mass_ref[...], extra)


def weigh_kept(kind, n_pts, kept, mass, points, after):
    total, width = points.shape
    rows, cols = kept.shape[0], width // n_pts
    extra = round_up(-(-rows // cols), 8)
    return pl.pallas_call(
        functools.partial(weigh_kept_body, kind, extra),
        in_specs=[VMEM] * 3 + [ANY],
        out_specs=[VMEM] * 2,
        input_output_aliases={0: 1},
        scratch_shapes=[pltpu.VMEM((rows, cols), F32)],
        out_shape=[
            jax.ShapeDtypeStruct((1, rows + extra, cols), F32),
            jax.ShapeDtypeStruct(kept.shape, BF16),
        ],
        compiler_params=params(KEPT_VMEM),
        cost_estimate=pl.CostEstimate(
            flops=2 * rows * cols * total, bytes_accessed=2 * total * (rows + cols), transcendentals=0
        ),
    )(kept, mass, points, after)


def weigh(by_rows, kind, chips, stats, tops, shifted, points, after, found=()):
    total, width = points.shape
    pair = shifted.shape[0] // chips
    parts, others = (CORES, chips - 1) if kind == FAR else (1, 1)
    line = stats[0].shape[2]
    chunk = line * divisor(total // line, CHUNK_LINES)
    slots = min(WEIGH_SLOTS, total // chunk)
    kept = []
    if not by_rows:
        kept = [
            jax.ShapeDtypeStruct((shifted.shape[0], total), BF16),
            jax.ShapeDtypeStruct((1, shifted.shape[0]), F32),
        ]
    if by_rows:
        rows, cols = pair // CORES, width
        sums = (rows * parts, width)
    else:
        rows, cols = shifted.shape[0], width // (CORES * chips)
        sums = (rows, cols * parts)
    n_tops = len(tops)
    extra = round_up(-(-rows // cols), 8)
    outs = [jax.ShapeDtypeStruct((others, rows + extra, cols), F32)] * parts
    cuts, whole = (), []
    if by_rows and kind == THEIRS:
        cuts = [round_up(rows * part // PIECES, 8) for part in range(PIECES)] + [rows + extra]
        outs = [jax.ShapeDtypeStruct((end - start, cols), F32) for start, end in zip(cuts, cuts[1:])]
        whole = [pltpu.VMEM((1, rows + extra, cols), F32)]
    return pl.pallas_call(
        functools.partial(
            weigh_body, by_rows, len(stats), n_tops, len(found), cuts, kind, others, extra, pair
        ),
        in_specs=[VMEM] * (len(stats) + n_tops) + [ANY, VMEM, ANY] + [VMEM] * len(found),
        out_specs=[VMEM] * (len(outs) + len(kept)),
        scratch_shapes=[pltpu.VMEM(stats[0].shape[1:], F32)] * 2
        + [pltpu.VMEM((sums[0], chunk), BF16)] * (2 if by_rows else 0)
        + [
            pltpu.VMEM((slots, sums[0], chunk), F32),
            pltpu.VMEM((sums[0], 128), F32),
            pltpu.VMEM(sums, F32),
            pltpu.SemaphoreType.DMA((slots,)),
        ]
        + whole,
        out_shape=outs + kept,
        compiler_params=params(WEIGH_VMEM),
        cost_estimate=pl.CostEstimate(
            flops=0 if found else 2 * others * sums[0] * sums[1] * total,
            bytes_accessed=0 if found else 2 * others * total * (sums[1] + 2 * sums[0]),
            transcendentals=0,
        ),
    )(*stats, *tops, shifted, points, after, *found)


def fold_body(rows, lines, pieces, mine_ref, theirs_ref, after_ref, *out_refs):
    width = out_refs[0].shape[1]
    count = rows // pieces
    step = divisor(count, 128) if lines == 1 else width
    all_masses = mine_ref[rows : rows + lines, :] + theirs_ref[rows : rows + lines, :]
    for piece, out_ref in enumerate(out_refs):
        out_ref[count:, :] = jnp.zeros((out_ref.shape[0] - count, width), BF16)
        scales = []
        for start in range(0, count, step):
            part = slice(piece * count + start, piece * count + start + step)
            total = mine_ref[part, :] + theirs_ref[part, :]
            top = jnp.max(jnp.abs(total), axis=1, keepdims=True)
            scale = jnp.maximum(top * 1.01, 1e-30).astype(BF16).astype(F32)
            out_ref[start : start + step, :] = encode(total, scale)
            scales.append(jnp.broadcast_to(scale, (step, 128)).T[0:1, :])
        if lines == 1:
            out_ref[count : count + 1, :count] = jnp.concatenate(scales, axis=1).astype(BF16)
            mass, used = all_masses[:, piece * count : (piece + 1) * count], slice(0, count)
        else:
            out_ref[count : count + lines, :] = jnp.concatenate(scales, axis=0).astype(BF16)
            mass, used = all_masses, slice(None)
        for number in range(1, 4):
            rounded = mass.astype(BF16)
            out_ref[count + number * lines : count + (number + 1) * lines, used] = rounded
            mass = mass - rounded.astype(F32)


def fold(pieces, mine, theirs, after):
    others, height, width = mine.shape
    rows, lines = shape_of(height, width)
    coded = (rows // pieces + round_up(4 * lines, 16), width)
    return pl.pallas_call(
        functools.partial(fold_body, rows, lines, pieces),
        grid=(others,),
        in_specs=[pl.BlockSpec((None, height, width), lambda d: (d, 0, 0))] * 2 + [ANY],
        out_specs=[pl.BlockSpec((None, *coded), lambda d: (d, 0, 0))] * pieces,
        out_shape=[jax.ShapeDtypeStruct((others, *coded), BF16)] * pieces,
        compiler_params=params(10),
        cost_estimate=pl.CostEstimate(
            flops=20 * others * height * width,
            bytes_accessed=10 * others * height * width,
            transcendentals=others * height * width,
        ),
    )(mine, theirs, after)


def plain_fold_body(mine_ref, theirs_ref, out_ref):
    out_ref[...] = mine_ref[...] + theirs_ref[...]


def plain_fold(mine, theirs):
    return pl.pallas_call(
        plain_fold_body,
        in_specs=[VMEM] * 2,
        out_specs=VMEM,
        out_shape=jax.ShapeDtypeStruct(mine.shape, F32),
        compiler_params=params(10),
    )(mine, theirs)


def shape_of(height, width):
    rows = height - 8
    while rows + round_up(-(-rows // width), 8) != height:
        rows -= 8
    return rows, -(-rows // width)


def finish_body(rows, lines, piece, as_units, n_near, *refs):
    near_refs, code_refs, (_, out_ref) = refs[:n_near], refs[n_near:-2], refs[-2:]
    count, width = out_ref.shape
    step = divisor(count, 128) if lines == 1 else width
    mass = functools.reduce(jnp.add, [ref[rows : rows + lines, :] for ref in near_refs])
    if lines == 1:
        mass = mass[:, piece * count : (piece + 1) * count]
    used = slice(0, count) if lines == 1 else slice(None)
    for ref in code_refs:
        for number in range(0, 1) if as_units else range(1, 4):
            start = count + number * lines
            mass = mass + ref[start : start + lines, used].astype(F32)

    def column(values, number):
        if lines == 1:
            line = values[:, number * step : (number + 1) * step]
        else:
            line = values[number : number + 1, :]
        return to_column(line, step)[:, 0:1]

    scales = [ref[count : count + lines, used].astype(F32) for ref in code_refs]
    for number in range(count // step):
        part = slice(number * step, (number + 1) * step)
        near = slice(piece * count + number * step, piece * count + (number + 1) * step)
        total = functools.reduce(jnp.add, [ref[near, :] for ref in near_refs])
        for ref, scale in zip(code_refs, scales):
            found = ref[part, :]
            total = total + (found if as_units else decode(found, column(scale, number)))
        means = total / jnp.maximum(column(mass, number), 1.0)
        out_ref[part, :] = normalize_rows(means).astype(BF16) if as_units else means


def finish(as_units, piece, pieces, near, codes, after):
    height, width = near[0].shape
    rows, lines = shape_of(height, width)
    count = rows // pieces
    return pl.pallas_call(
        functools.partial(finish_body, rows, lines, piece, as_units, len(near)),
        in_specs=[VMEM] * (len(near) + len(codes)) + [ANY],
        out_specs=VMEM,
        out_shape=jax.ShapeDtypeStruct((count, width), BF16 if as_units else F32),
        compiler_params=params(10),
        cost_estimate=pl.CostEstimate(
            flops=30 * count * width,
            bytes_accessed=(12 + 2 * len(codes)) * count * width,
            transcendentals=2 * count * width,
        ),
    )(*near, *codes, after)


def keep_body(value_ref, after_ref, out_ref):
    pass


def keep_until(value, after):
    return pl.pallas_call(
        keep_body,
        in_specs=[VMEM, ANY],
        out_specs=VMEM,
        out_shape=jax.ShapeDtypeStruct(value.shape, value.dtype),
        input_output_aliases={0: 0},
        compiler_params=params(10),
    )(value, after)


def merge_body(*refs):
    refs[-1][0], refs[-1][1] = merge(refs[:-1])


def merged(sets):
    return pl.pallas_call(
        merge_body, out_shape=jax.ShapeDtypeStruct(sets[0].shape, F32), compiler_params=params(10)
    )(*sets)


def log_body(*refs):
    top, total = merge(refs[:-1])
    refs[-1][...] = top + jnp.log(total)


def log_norms(sets):
    return pl.pallas_call(
        log_body, out_shape=jax.ShapeDtypeStruct(sets[0].shape[1:], F32), compiler_params=params(10)
    )(*sets).reshape(-1)


def on_device(n_pts, n_cen, points, centroids):
    chips = n_pts // CORES

    def to_partner(value):
        return lax.ppermute(value, "pts", [(i, i ^ 1) for i in range(n_pts)])

    def to_chip(value, away):
        moves = [(i, (i + CORES * away) % n_pts) for i in range(n_pts)]
        return lax.ppermute(value, "pts", moves)

    def over_centroids(stats):
        if n_cen & (n_cen - 1):
            moves = [[(i, (i + away) % n_cen) for i in range(n_cen)] for away in range(1, n_cen)]
            return [stats] + [lax.ppermute(stats, "cen", move) for move in moves]
        done, sets = 1, [stats]
        while done < n_cen:
            if done > 1:
                sets = [merged(sets)]
            ways = 4 if (n_cen // done).bit_length() % 2 else 2
            for way in range(1, ways):
                moves = [(i, i ^ (way * done)) for i in range(n_cen)]
                sets.append(lax.ppermute(sets[0], "cen", moves))
            done *= ways
        return sets

    def sums_over_pts(by_rows, stats, tops, shifted):
        kept = mass = None

        def weighted(kind, after, found=()):
            nonlocal kept, mass
            if by_rows:
                return weigh(by_rows, kind, chips, stats, tops, shifted, points, after, found)
            if kind == FAR:
                *found, kept, mass = weigh(by_rows, kind, chips, stats, tops, shifted, points, after)
                return found
            *found, kept = weigh_kept(kind, n_pts, kept, mass, points, after)
            return found

        far_mine, far_theirs = weighted(FAR, stats[0])
        far_found = to_partner(far_theirs)
        if by_rows:
            coded = [plain_fold(far_mine, far_found)]
            codes = [[to_chip(each[away - 1], away) for away in range(1, chips)] for each in coded]
            near_found = [to_partner(piece) for piece in weighted(THEIRS, coded[0])]
            near = [each[0] for each in weighted(OWN, coded[0], near_found)]
        else:
            (near_theirs,) = weighted(THEIRS, far_theirs)
            near_found = to_partner(near_theirs)
            coded = fold(1, far_mine, far_found, near_theirs)
            codes = [[to_chip(each[away - 1], away) for away in range(1, chips)] for each in coded]
            (near_mine,) = weighted(OWN, coded[0])
            near = [near_mine[0], near_found[0]]
        found, away_found, after = [], [], coded[0]
        for piece, each in enumerate(codes):
            found.append(finish(by_rows, piece, len(codes), near, each, after))
            if by_rows:
                away_found.append([to_chip(found[-1], -away) for away in range(1, chips)])
                after = away_found[-1][-1]
        return found, away_found

    pieces = 1
    units = first_units(centroids)
    shifted, own = scores(ITERS > 1, [units], points)
    stats = over_centroids(own)
    tops = [own]
    for iteration in range(1, ITERS):
        raw = iteration + 1 < ITERS
        mine, away_mine = sums_over_pts(True, stats, tops, shifted)
        near_units = mine + [to_partner(unit) for unit in mine]
        shifted, near_own = scores(raw, near_units, points, pieces, 0, shifted)
        far_units = []
        for units in zip(*away_mine):
            units = [keep_until(unit, near_own) for unit in units]
            far_units += units + [to_partner(unit) for unit in units]
        shifted, far_own = scores(raw, far_units, points, pieces, 1, shifted)
        tops = [near_own, far_own]
        stats = over_centroids(merged([near_own, far_own]))
    (means,), _ = sums_over_pts(False, stats, tops, shifted)
    return (means, log_norms(stats))


def solution(mesh):
    placed = (P("pts", None), P("cen", None))
    return jax.shard_map(
        functools.partial(on_device, mesh.shape["pts"], mesh.shape["cen"]),
        mesh=mesh,
        in_specs=placed,
        out_specs=(P("cen", "pts"), P("pts")),
        check_vma=False,
    )
```

```python
import functools

import jax
import jax.numpy as jnp
from jax import lax
from jax.experimental import pallas as pl
from jax.experimental.pallas import tpu as pltpu
from jax.sharding import PartitionSpec as P

ITERS = 2
F32 = jnp.float32
BF16 = jnp.bfloat16
LOAD_VMEM = 38
SCORE_VMEM = 34
WEIGH_VMEM = 34
KEPT_VMEM = 20
CHUNK_LINES = 2
WEIGH_SLOTS = 2
PIECES = 4
LEVELS = 30000.0
LOWEST = -117.0


def divisor(total, wanted):
    size = min(total, wanted)
    while total % size:
        size -= 1
    return size


def round_up(value, unit):
    return -(-value // unit) * unit


def normalize_rows(rows):
    return rows * lax.rsqrt(jnp.sum(rows * rows, axis=1, keepdims=True) + 1e-06)


CORES = 2


def place():
    me = lax.axis_index("pts")
    return lax.div(me, CORES), lax.rem(me, CORES)


def params(mebibytes):
    return pltpu.CompilerParams(vmem_limit_bytes=mebibytes * 2**20)


VMEM = pl.BlockSpec(memory_space=pltpu.VMEM)
ANY = pl.BlockSpec(memory_space=pl.ANY)


def merge(sets):
    top = functools.reduce(jnp.maximum, [stats[0] for stats in sets])
    return top, functools.reduce(jnp.add, [stats[1] * jnp.exp(stats[0] - top) for stats in sets])


def to_column(row, height):
    return jnp.broadcast_to(row, (128, height)).T


def encode(values, scale):
    steps = jnp.floor(jnp.abs(values) * (LEVELS / scale) + 0.5)
    power = jnp.floor(steps * (1.0 / 128.0))
    size = (1.0 + (steps * (1.0 / 128.0) - power)) * jnp.exp2(power + LOWEST)
    return jnp.where(values < 0.0, -size, size).astype(BF16)


def decode(codes, scale):
    wide = codes.astype(F32)
    size = jnp.abs(wide)
    power = jnp.floor(jnp.log2(size))
    steps = 128.0 * (power - LOWEST + (size * jnp.exp2(-power) - 1.0))
    return jnp.where(wide < 0.0, -steps, steps) * (scale * (1.0 / LEVELS))


def first_units_body(c_ref, sums_ref, units_ref):
    step = divisor(units_ref.shape[0], 128)
    for start in range(0, units_ref.shape[0], step):
        part = slice(start, start + step)
        scale = to_column(lax.rsqrt(sums_ref[:, part] + 1e-06), step)[:, 0:1]
        units_ref[part, :] = (c_ref[part, :] * scale).astype(BF16)


def copy_body(in_ref, out_ref):
    out_ref[...] = in_ref[...]


def first_units(centroids):
    centroids = pl.pallas_call(
        copy_body,
        in_specs=[VMEM],
        out_specs=VMEM,
        out_shape=jax.ShapeDtypeStruct(centroids.shape, F32),
        compiler_params=params(10),
    )(centroids)
    square_sums = jnp.sum(centroids * centroids, axis=1)[None]
    return pl.pallas_call(
        first_units_body,
        in_specs=[VMEM, VMEM],
        out_specs=VMEM,
        out_shape=jax.ShapeDtypeStruct(centroids.shape, BF16),
        compiler_params=params(10),
        cost_estimate=pl.CostEstimate(
            flops=4 * centroids.size, bytes_accessed=4 * centroids.size, transcendentals=0
        ),
    )(centroids, square_sums)


def total_of(values):
    rows, width = values.shape
    groups = divisor(rows // 8, 16)
    return jnp.sum(values.reshape(groups, rows // groups, width).sum(axis=0), axis=0, keepdims=True)


def score_points(raw, units, x_ref, e_parts, stat_ref, stage, semaphores):
    line = stat_ref.shape[2]
    lines = stage.shape[0]
    sub = divisor(line, 256)

    def copies(number, slot):
        columns = pl.ds(pl.multiple_of(number * line, line), line)
        return [
            pltpu.make_async_copy(stage.at[slot, rows, :], target(columns), semaphores.at[slot, part])
            for part, (rows, target) in enumerate(e_parts)
        ]

    def visit(step, carry):
        for slot in range(lines):
            number = step * lines + slot

            @pl.when(step > 0)
            def _():
                for copy in copies(number - lines, slot):
                    copy.wait()

            tops, totals = [], []
            for offset in range(0, line, sub):
                part = (slot, slice(None), slice(offset, offset + sub))
                logits = lax.dot_general(
                    units[...],
                    x_ref[pl.ds(pl.multiple_of(number * line + offset, sub), sub), :],
                    (((1,), (1,)), ((), ())),
                    preferred_element_type=F32,
                )
                top = jnp.max(logits, axis=0, keepdims=True)
                shifted = jnp.exp(logits - top)
                stage[part] = logits if raw else shifted
                tops.append(top)
                totals.append(total_of(shifted))
            stat_ref[0, pl.ds(number, 1), :] = jnp.concatenate(tops, axis=1)
            stat_ref[1, pl.ds(number, 1), :] = jnp.concatenate(totals, axis=1)
            for copy in copies(number, slot):
                copy.start()
        return carry

    steps = stat_ref.shape[1] // lines
    lax.fori_loop(0, steps, visit, 0)
    for slot in range(lines):
        for copy in copies((steps - 1) * lines + slot, slot):
            copy.wait()


def stat_shape(total):
    line = divisor(total, 512)
    return (2, total // line, line)


def first_scores_body(raw, units, x_ref, e_hbm, stat_ref, stage, semaphores):
    target = [(slice(None), lambda columns: e_hbm.at[:, columns])]
    score_points(raw, units, x_ref, target, stat_ref, stage, semaphores)


def next_scores_body(raw, count, pieces, away, *refs):
    unit_refs = refs[:count]
    x_ref = refs[count]
    e_hbm, stat_ref, units, stage, semaphores = refs[-5:]
    rows = unit_refs[0].shape[0]
    pair = CORES * pieces * rows
    chip, core = place()
    chips = e_hbm.shape[0] // pair
    for number, ref in enumerate(unit_refs):
        group, who, piece = number // (CORES * pieces), number // pieces % CORES, number % pieces
        of_pair = (core if who == 0 else 1 - core) * pieces + piece
        start = pl.multiple_of((group * CORES * pieces + of_pair) * rows, rows)
        units[pl.ds(start, rows), :] = ref[...]

    def target_of(number):
        start = pl.multiple_of(lax.rem(chip + away + number, chips) * pair, pair)
        return lambda columns: e_hbm.at[pl.ds(start, pair), columns]

    targets = [
        (slice(number * pair, (number + 1) * pair), target_of(number)) for number in range(count // (CORES * pieces))
    ]
    score_points(raw, units, x_ref, targets, stat_ref, stage, semaphores)


def scores(raw, blocks, points, pieces=1, away=None, shifted=None):
    total, width = points.shape
    count = len(blocks)
    rows = sum(block.shape[0] for block in blocks)
    all_rows = rows if shifted is None else shifted.shape[0]
    stat = stat_shape(total)
    parts = 1 if away is None else count // (CORES * pieces)
    more = [] if shifted is None or away == 0 else [shifted]
    scratch = [
        pltpu.VMEM((divisor(stat[1], 2), rows, stat[2]), F32),
        pltpu.SemaphoreType.DMA((divisor(stat[1], 2), parts)),
    ]
    if away is not None:
        scratch = [pltpu.VMEM((rows, width), BF16)] + scratch
    if away is None:
        body = functools.partial(first_scores_body, raw)
    else:
        body = functools.partial(next_scores_body, raw, count, pieces, away)
    return pl.pallas_call(
        body,
        in_specs=[VMEM] * (count + 1) + [ANY] * len(more),
        out_specs=[ANY, VMEM],
        out_shape=[
            jax.ShapeDtypeStruct((all_rows, total), F32),
            jax.ShapeDtypeStruct(stat, F32),
        ],
        input_output_aliases={count + 1: 0} if more else {},
        scratch_shapes=scratch,
        compiler_params=params(SCORE_VMEM),
        cost_estimate=pl.CostEstimate(
            flops=2 * rows * total * width,
            bytes_accessed=2 * total * width + 4 * rows * total,
            transcendentals=rows * total,
        ),
    )(*blocks, points, *more)


FAR, THEIRS, OWN = range(3)


def weigh_body(by_rows, n_sets, n_tops, n_found, cuts, kind, others, extra, pair, *refs):
    parts = CORES if kind == FAR else 1
    stat_refs, refs = refs[:n_sets], refs[n_sets:]
    top_refs, (e_hbm, x_ref, _), refs = refs[:n_tops], refs[n_tops : n_tops + 3], refs[n_tops + 3 :]
    found_refs, refs = refs[:n_found], refs[n_found:]
    cut_refs = ()
    if cuts:
        cut_refs, refs = refs[: len(cuts) - 1], refs[len(cuts) - 1 :]
        out_refs, refs = refs[-1:], refs[:-1]
    else:
        out_refs, refs = refs[:parts], refs[parts:]
    if not by_rows:
        (kept_ref, kept_mass_ref), refs = refs[:2], refs[2:]
    scale_refs, refs = refs[:2], refs[2:]
    n_weights = 2 if by_rows else 0
    weights_refs, (stage, mass_ref, sum_ref, semaphores) = refs[:n_weights], refs[n_weights:]
    chip, core = place()
    line = stat_refs[0].shape[2]
    total = x_ref.shape[0]
    height, span = sum_ref.shape
    slots, _, chunk = stage.shape
    steps = total // chunk
    lanes = min(line, 128)

    def block_of(other):
        if kind == FAR:
            return lax.rem(chip + 1 + other, others + 1)
        return chip * CORES + (core if kind == OWN else 1 - core)

    def copy_of(number):
        other, step = divmod(number, steps)
        rows = pl.ds(pl.multiple_of(block_of(other) * height, height), height) if by_rows else slice(None)
        columns = slice(step * chunk, (step + 1) * chunk)
        slot = number % slots
        return pltpu.make_async_copy(e_hbm.at[rows, columns], stage.at[slot], semaphores.at[slot])

    for number in range(min(slots, others * steps)):
        copy_of(number).start()
    top, all_total = merge(stat_refs)
    if by_rows:
        scale_refs[0][...] = top
        scale_refs[1][...] = 1.0 / all_total
    else:
        for ref, scale_ref in zip((top_refs[0], top_refs[-1]), scale_refs):
            scale_ref[...] = jnp.exp(ref[0] - top) / all_total

    def weights_of(values, group, number):
        one, two = (ref[number : number + 1, :] for ref in scale_refs)
        if by_rows:
            return jnp.exp(values - one) * two
        return values * jnp.where(chip == group, one, two)

    group_rows = height if by_rows else pair
    kept = not by_rows

    def weights_part(step):
        columns = slice(step * chunk, (step + 1) * chunk)
        return kept_ref.at[:, columns] if kept else weights_refs[step % 2]

    def weigh_step(number):
        step = number % steps
        weights_ref = weights_part(step)
        for group in range(height // group_rows):
            rows = slice(group * group_rows, (group + 1) * group_rows)
            mass = None
            for offset in range(0, chunk, line):
                values = stage[number % slots, rows, offset : offset + line]
                weights = weights_of(values, group, (step * chunk + offset) // line).astype(BF16)
                weights_ref[rows, offset : offset + line] = weights
                wide = weights.astype(F32)
                for lane in range(0, line, lanes):
                    piece = wide[:, lane : lane + lanes]
                    mass = piece if mass is None else mass + piece
            mass_ref[rows, :] = mass if step == 0 else mass_ref[rows, :] + mass

    weighed = steps if kept else others * steps
    for number in range(others * steps):
        other, step = divmod(number, steps)
        if number < weighed:
            copy_of(number).wait()
            weigh_step(number)
        if number + slots < weighed:
            copy_of(number + slots).start()
        columns = slice(None)
        if not by_rows:
            columns = pl.ds(pl.multiple_of(block_of(other) * span, span), span)
        product = jnp.dot(
            weights_part(step)[...],
            x_ref[step * chunk : (step + 1) * chunk, columns],
            preferred_element_type=F32,
        )
        sum_ref[...] = product if step == 0 else sum_ref[...] + product
        if step == steps - 1:
            mass = jnp.sum(mass_ref[...].T, axis=0, keepdims=True)
            if kept:
                kept_mass_ref[...] = mass
            write_sums(by_rows, other, core, out_refs, sum_ref, mass, extra)
    for number, ref in enumerate(cut_refs):
        ref[...] = out_refs[0][0, cuts[number] : cuts[number + 1], :]
    start = 0
    for ref in found_refs:
        out_refs[0][0, start : start + ref.shape[0], :] += ref[...]
        start += ref.shape[0]


def write_sums(by_rows, other, core, out_refs, sum_ref, mass, extra):
    parts = len(out_refs)
    rows = out_refs[0].shape[1] - extra
    width = out_refs[0].shape[2]
    for part, ref in enumerate(out_refs):
        side = lax.rem(core + part, parts)
        ref[other, rows:, :] = jnp.zeros((extra, width), F32)
        if by_rows:
            found = mass
            if parts > 1:
                found = jnp.where(side == 0, mass[:, :rows], mass[:, rows:])
                ref[other, :rows, :] = sum_ref[pl.ds(pl.multiple_of(side * rows, rows), rows), :]
            else:
                ref[other, :rows, :] = sum_ref[...]
            ref[other, rows : rows + 1, :rows] = found
        else:
            sums = sum_ref[...]
            if parts > 1:
                sums = jnp.where(side == 0, sums[:, :width], sums[:, width:])
            ref[other, :rows, :] = sums
            for number in range(rows // width):
                ref[other, rows + number : rows + number + 1, :] = mass[
                    :, number * width : (number + 1) * width
                ]


def weigh_kept_body(kind, extra, kept_ref, mass_ref, x_ref, _, out_ref, kept_out, sum_ref):
    chip, core = place()
    span = sum_ref.shape[1]
    total = x_ref.shape[0]
    block = chip * CORES + (core if kind == OWN else 1 - core)
    columns = pl.ds(pl.multiple_of(block * span, span), span)
    sum_ref[...] = jnp.dot(kept_ref[...], x_ref[:, columns], preferred_element_type=F32)
    write_sums(False, 0, core, [out_ref], sum_ref, mass_ref[...], extra)


def weigh_kept(kind, n_pts, kept, mass, points, after):
    total, width = points.shape
    rows, cols = kept.shape[0], width // n_pts
    extra = round_up(-(-rows // cols), 8)
    return pl.pallas_call(
        functools.partial(weigh_kept_body, kind, extra),
        in_specs=[VMEM] * 3 + [ANY],
        out_specs=[VMEM] * 2,
        input_output_aliases={0: 1},
        scratch_shapes=[pltpu.VMEM((rows, cols), F32)],
        out_shape=[
            jax.ShapeDtypeStruct((1, rows + extra, cols), F32),
            jax.ShapeDtypeStruct(kept.shape, BF16),
        ],
        compiler_params=params(KEPT_VMEM),
        cost_estimate=pl.CostEstimate(
            flops=2 * rows * cols * total, bytes_accessed=2 * total * (rows + cols), transcendentals=0
        ),
    )(kept, mass, points, after)


def weigh(by_rows, kind, chips, stats, tops, shifted, points, after, found=()):
    total, width = points.shape
    pair = shifted.shape[0] // chips
    parts, others = (CORES, chips - 1) if kind == FAR else (1, 1)
    line = stats[0].shape[2]
    chunk = line * divisor(total // line, CHUNK_LINES)
    slots = min(WEIGH_SLOTS, total // chunk)
    kept = []
    if not by_rows:
        kept = [
            jax.ShapeDtypeStruct((shifted.shape[0], total), BF16),
            jax.ShapeDtypeStruct((1, shifted.shape[0]), F32),
        ]
    if by_rows:
        rows, cols = pair // CORES, width
        sums = (rows * parts, width)
    else:
        rows, cols = shifted.shape[0], width // (CORES * chips)
        sums = (rows, cols * parts)
    n_tops = len(tops)
    extra = round_up(-(-rows // cols), 8)
    outs = [jax.ShapeDtypeStruct((others, rows + extra, cols), F32)] * parts
    cuts, whole = (), []
    if by_rows and kind == THEIRS:
        cuts = [round_up(rows * part // PIECES, 8) for part in range(PIECES)] + [rows + extra]
        outs = [jax.ShapeDtypeStruct((end - start, cols), F32) for start, end in zip(cuts, cuts[1:])]
        whole = [pltpu.VMEM((1, rows + extra, cols), F32)]
    return pl.pallas_call(
        functools.partial(
            weigh_body, by_rows, len(stats), n_tops, len(found), cuts, kind, others, extra, pair
        ),
        in_specs=[VMEM] * (len(stats) + n_tops) + [ANY, VMEM, ANY] + [VMEM] * len(found),
        out_specs=[VMEM] * (len(outs) + len(kept)),
        scratch_shapes=[pltpu.VMEM(stats[0].shape[1:], F32)] * 2
        + [pltpu.VMEM((sums[0], chunk), BF16)] * (2 if by_rows else 0)
        + [
            pltpu.VMEM((slots, sums[0], chunk), F32),
            pltpu.VMEM((sums[0], 128), F32),
            pltpu.VMEM(sums, F32),
            pltpu.SemaphoreType.DMA((slots,)),
        ]
        + whole,
        out_shape=outs + kept,
        compiler_params=params(WEIGH_VMEM),
        cost_estimate=pl.CostEstimate(
            flops=0 if found else 2 * others * sums[0] * sums[1] * total,
            bytes_accessed=0 if found else 2 * others * total * (sums[1] + 2 * sums[0]),
            transcendentals=0,
        ),
    )(*stats, *tops, shifted, points, after, *found)


def fold_body(rows, lines, pieces, mine_ref, theirs_ref, after_ref, *out_refs):
    width = out_refs[0].shape[1]
    count = rows // pieces
    step = divisor(count, 128) if lines == 1 else width
    all_masses = mine_ref[rows : rows + lines, :] + theirs_ref[rows : rows + lines, :]
    for piece, out_ref in enumerate(out_refs):
        out_ref[count:, :] = jnp.zeros((out_ref.shape[0] - count, width), BF16)
        scales = []
        for start in range(0, count, step):
            part = slice(piece * count + start, piece * count + start + step)
            total = mine_ref[part, :] + theirs_ref[part, :]
            top = jnp.max(jnp.abs(total), axis=1, keepdims=True)
            scale = jnp.maximum(top * 1.01, 1e-30).astype(BF16).astype(F32)
            out_ref[start : start + step, :] = encode(total, scale)
            scales.append(jnp.broadcast_to(scale, (step, 128)).T[0:1, :])
        if lines == 1:
            out_ref[count : count + 1, :count] = jnp.concatenate(scales, axis=1).astype(BF16)
            mass, used = all_masses[:, piece * count : (piece + 1) * count], slice(0, count)
        else:
            out_ref[count : count + lines, :] = jnp.concatenate(scales, axis=0).astype(BF16)
            mass, used = all_masses, slice(None)
        for number in range(1, 4):
            rounded = mass.astype(BF16)
            out_ref[count + number * lines : count + (number + 1) * lines, used] = rounded
            mass = mass - rounded.astype(F32)


def fold(pieces, mine, theirs, after):
    others, height, width = mine.shape
    rows, lines = shape_of(height, width)
    coded = (rows // pieces + round_up(4 * lines, 16), width)
    return pl.pallas_call(
        functools.partial(fold_body, rows, lines, pieces),
        grid=(others,),
        in_specs=[pl.BlockSpec((None, height, width), lambda d: (d, 0, 0))] * 2 + [ANY],
        out_specs=[pl.BlockSpec((None, *coded), lambda d: (d, 0, 0))] * pieces,
        out_shape=[jax.ShapeDtypeStruct((others, *coded), BF16)] * pieces,
        compiler_params=params(10),
        cost_estimate=pl.CostEstimate(
            flops=20 * others * height * width,
            bytes_accessed=10 * others * height * width,
            transcendentals=others * height * width,
        ),
    )(mine, theirs, after)


def shape_of(height, width):
    rows = height - 8
    while rows + round_up(-(-rows // width), 8) != height:
        rows -= 8
    return rows, -(-rows // width)


def finish_body(rows, lines, piece, as_units, n_near, *refs):
    near_refs, code_refs, (_, out_ref) = refs[:n_near], refs[n_near:-2], refs[-2:]
    count, width = out_ref.shape
    step = divisor(count, 128) if lines == 1 else width
    mass = functools.reduce(jnp.add, [ref[rows : rows + lines, :] for ref in near_refs])
    if lines == 1:
        mass = mass[:, piece * count : (piece + 1) * count]
    used = slice(0, count) if lines == 1 else slice(None)
    for ref in code_refs:
        for number in range(1, 4):
            start = count + number * lines
            mass = mass + ref[start : start + lines, used].astype(F32)

    def column(values, number):
        if lines == 1:
            line = values[:, number * step : (number + 1) * step]
        else:
            line = values[number : number + 1, :]
        return to_column(line, step)[:, 0:1]

    scales = [ref[count : count + lines, used].astype(F32) for ref in code_refs]
    for number in range(count // step):
        part = slice(number * step, (number + 1) * step)
        near = slice(piece * count + number * step, piece * count + (number + 1) * step)
        total = functools.reduce(jnp.add, [ref[near, :] for ref in near_refs])
        for ref, scale in zip(code_refs, scales):
            total = total + decode(ref[part, :], column(scale, number))
        means = total / jnp.maximum(column(mass, number), 1.0)
        out_ref[part, :] = normalize_rows(means).astype(BF16) if as_units else means


def finish(as_units, piece, pieces, near, codes, after):
    height, width = near[0].shape
    rows, lines = shape_of(height, width)
    count = rows // pieces
    return pl.pallas_call(
        functools.partial(finish_body, rows, lines, piece, as_units, len(near)),
        in_specs=[VMEM] * (len(near) + len(codes)) + [ANY],
        out_specs=VMEM,
        out_shape=jax.ShapeDtypeStruct((count, width), BF16 if as_units else F32),
        compiler_params=params(10),
        cost_estimate=pl.CostEstimate(
            flops=30 * count * width,
            bytes_accessed=(12 + 2 * len(codes)) * count * width,
            transcendentals=2 * count * width,
        ),
    )(*near, *codes, after)


def keep_body(value_ref, after_ref, out_ref):
    pass


def keep_until(value, after):
    return pl.pallas_call(
        keep_body,
        in_specs=[VMEM, ANY],
        out_specs=VMEM,
        out_shape=jax.ShapeDtypeStruct(value.shape, value.dtype),
        input_output_aliases={0: 0},
        compiler_params=params(10),
    )(value, after)


def merge_body(*refs):
    refs[-1][0], refs[-1][1] = merge(refs[:-1])


def merged(sets):
    return pl.pallas_call(
        merge_body, out_shape=jax.ShapeDtypeStruct(sets[0].shape, F32), compiler_params=params(10)
    )(*sets)


def log_body(*refs):
    top, total = merge(refs[:-1])
    refs[-1][...] = top + jnp.log(total)


def log_norms(sets):
    return pl.pallas_call(
        log_body, out_shape=jax.ShapeDtypeStruct(sets[0].shape[1:], F32), compiler_params=params(10)
    )(*sets).reshape(-1)


def on_device(n_pts, n_cen, points, centroids):
    chips = n_pts // CORES

    def to_partner(value):
        return lax.ppermute(value, "pts", [(i, i ^ 1) for i in range(n_pts)])

    def to_chip(value, away):
        moves = [(i, (i + CORES * away) % n_pts) for i in range(n_pts)]
        return lax.ppermute(value, "pts", moves)

    def over_centroids(stats):
        if n_cen & (n_cen - 1):
            moves = [[(i, (i + away) % n_cen) for i in range(n_cen)] for away in range(1, n_cen)]
            return [stats] + [lax.ppermute(stats, "cen", move) for move in moves]
        done, sets = 1, [stats]
        while done < n_cen:
            if done > 1:
                sets = [merged(sets)]
            ways = 4 if (n_cen // done).bit_length() % 2 else 2
            for way in range(1, ways):
                moves = [(i, i ^ (way * done)) for i in range(n_cen)]
                sets.append(lax.ppermute(sets[0], "cen", moves))
            done *= ways
        return sets

    def sums_over_pts(by_rows, stats, tops, shifted):
        kept = mass = None

        def weighted(kind, after, found=()):
            nonlocal kept, mass
            if by_rows:
                return weigh(by_rows, kind, chips, stats, tops, shifted, points, after, found)
            if kind == FAR:
                *found, kept, mass = weigh(by_rows, kind, chips, stats, tops, shifted, points, after)
                return found
            *found, kept = weigh_kept(kind, n_pts, kept, mass, points, after)
            return found

        far_mine, far_theirs = weighted(FAR, stats[0])
        far_found = to_partner(far_theirs)
        if by_rows:
            coded = fold(pieces, far_mine, far_found, far_theirs)
            codes = [[to_chip(each[away - 1], away) for away in range(1, chips)] for each in coded]
            near_found = [to_partner(piece) for piece in weighted(THEIRS, coded[0])]
            near = [each[0] for each in weighted(OWN, coded[0], near_found)]
        else:
            (near_theirs,) = weighted(THEIRS, far_theirs)
            near_found = to_partner(near_theirs)
            coded = fold(1, far_mine, far_found, near_theirs)
            codes = [[to_chip(each[away - 1], away) for away in range(1, chips)] for each in coded]
            (near_mine,) = weighted(OWN, coded[0])
            near = [near_mine[0], near_found[0]]
        found, away_found, after = [], [], coded[0]
        for piece, each in enumerate(codes):
            found.append(finish(by_rows, piece, len(codes), near, each, after))
            if by_rows:
                away_found.append([to_chip(found[-1], -away) for away in range(1, chips)])
                after = away_found[-1][-1]
        return found, away_found

    pieces = 1
    units = first_units(centroids)
    shifted, own = scores(ITERS > 1, [units], points)
    stats = over_centroids(own)
    tops = [own]
    for iteration in range(1, ITERS):
        raw = iteration + 1 < ITERS
        mine, away_mine = sums_over_pts(True, stats, tops, shifted)
        near_units = mine + [to_partner(unit) for unit in mine]
        shifted, near_own = scores(raw, near_units, points, pieces, 0, shifted)
        far_units = []
        for units in zip(*away_mine):
            units = [keep_until(unit, near_own) for unit in units]
            far_units += units + [to_partner(unit) for unit in units]
        shifted, far_own = scores(raw, far_units, points, pieces, 1, shifted)
        tops = [near_own, far_own]
        stats = over_centroids(merged([near_own, far_own]))
    (means,), _ = sums_over_pts(False, stats, tops, shifted)
    return (means, log_norms(stats))


def solution(mesh):
    placed = (P("pts", None), P("cen", None))
    return jax.shard_map(
        functools.partial(on_device, mesh.shape["pts"], mesh.shape["cen"]),
        mesh=mesh,
        in_specs=placed,
        out_specs=(P("cen", "pts"), P("pts")),
        check_vma=False,
    )
```

```python
import functools

import jax
import jax.numpy as jnp
from jax import lax
from jax.experimental import pallas as pl
from jax.experimental.pallas import tpu as pltpu
from jax.sharding import PartitionSpec as P

ITERS = 2
F32 = jnp.float32
BF16 = jnp.bfloat16
LOAD_VMEM = 38
SCORE_VMEM = 34
WEIGH_VMEM = 34
KEPT_VMEM = 20
CHUNK_LINES = 2
WEIGH_SLOTS = 2
PIECES = 4
LEVELS = 30000.0
LOWEST = -117.0


def divisor(total, wanted):
    size = min(total, wanted)
    while total % size:
        size -= 1
    return size


def round_up(value, unit):
    return -(-value // unit) * unit


def normalize_rows(rows):
    return rows * lax.rsqrt(jnp.sum(rows * rows, axis=1, keepdims=True) + 1e-06)


CORES = 2


def place():
    me = lax.axis_index("pts")
    return lax.div(me, CORES), lax.rem(me, CORES)


def params(mebibytes):
    return pltpu.CompilerParams(vmem_limit_bytes=mebibytes * 2**20)


VMEM = pl.BlockSpec(memory_space=pltpu.VMEM)
ANY = pl.BlockSpec(memory_space=pl.ANY)


def merge(sets):
    top = functools.reduce(jnp.maximum, [stats[0] for stats in sets])
    return top, functools.reduce(jnp.add, [stats[1] * jnp.exp(stats[0] - top) for stats in sets])


def to_column(row, height):
    return jnp.broadcast_to(row, (128, height)).T


def encode(values, scale):
    steps = jnp.floor(jnp.abs(values) * (LEVELS / scale) + 0.5)
    power = jnp.floor(steps * (1.0 / 128.0))
    size = (1.0 + (steps * (1.0 / 128.0) - power)) * jnp.exp2(power + LOWEST)
    return jnp.where(values < 0.0, -size, size).astype(BF16)


def decode(codes, scale):
    wide = codes.astype(F32)
    size = jnp.abs(wide)
    power = jnp.floor(jnp.log2(size))
    steps = 128.0 * (power - LOWEST + (size * jnp.exp2(-power) - 1.0))
    return jnp.where(wide < 0.0, -steps, steps) * (scale * (1.0 / LEVELS))


def first_units_body(c_ref, sums_ref, units_ref):
    step = divisor(units_ref.shape[0], 128)
    for start in range(0, units_ref.shape[0], step):
        part = slice(start, start + step)
        scale = to_column(lax.rsqrt(sums_ref[:, part] + 1e-06), step)[:, 0:1]
        units_ref[part, :] = (c_ref[part, :] * scale).astype(BF16)


def copy_body(in_ref, out_ref):
    out_ref[...] = in_ref[...]


def first_units(centroids):
    centroids = pl.pallas_call(
        copy_body,
        in_specs=[VMEM],
        out_specs=VMEM,
        out_shape=jax.ShapeDtypeStruct(centroids.shape, F32),
        compiler_params=params(10),
    )(centroids)
    square_sums = jnp.sum(centroids * centroids, axis=1)[None]
    return pl.pallas_call(
        first_units_body,
        in_specs=[VMEM, VMEM],
        out_specs=VMEM,
        out_shape=jax.ShapeDtypeStruct(centroids.shape, BF16),
        compiler_params=params(10),
        cost_estimate=pl.CostEstimate(
            flops=4 * centroids.size, bytes_accessed=4 * centroids.size, transcendentals=0
        ),
    )(centroids, square_sums)


def total_of(values):
    rows, width = values.shape
    groups = divisor(rows // 8, 16)
    return jnp.sum(values.reshape(groups, rows // groups, width).sum(axis=0), axis=0, keepdims=True)


def score_points(raw, units, x_ref, e_parts, stat_ref, stage, semaphores):
    line = stat_ref.shape[2]
    lines = stage.shape[0]
    sub = divisor(line, 512)

    def copies(number, slot):
        columns = pl.ds(pl.multiple_of(number * line, line), line)
        return [
            pltpu.make_async_copy(stage.at[slot, rows, :], target(columns), semaphores.at[slot, part])
            for part, (rows, target) in enumerate(e_parts)
        ]

    def visit(step, carry):
        for slot in range(lines):
            number = step * lines + slot

            @pl.when(step > 0)
            def _():
                for copy in copies(number - lines, slot):
                    copy.wait()

            tops, totals = [], []
            for offset in range(0, line, sub):
                part = (slot, slice(None), slice(offset, offset + sub))
                logits = lax.dot_general(
                    units[...],
                    x_ref[pl.ds(pl.multiple_of(number * line + offset, sub), sub), :],
                    (((1,), (1,)), ((), ())),
                    preferred_element_type=F32,
                )
                top = jnp.max(logits, axis=0, keepdims=True)
                shifted = jnp.exp(logits - top)
                stage[part] = logits if raw else shifted
                tops.append(top)
                totals.append(total_of(shifted))
            stat_ref[0, pl.ds(number, 1), :] = jnp.concatenate(tops, axis=1)
            stat_ref[1, pl.ds(number, 1), :] = jnp.concatenate(totals, axis=1)
            for copy in copies(number, slot):
                copy.start()
        return carry

    steps = stat_ref.shape[1] // lines
    lax.fori_loop(0, steps, visit, 0)
    for slot in range(lines):
        for copy in copies((steps - 1) * lines + slot, slot):
            copy.wait()


def stat_shape(total):
    line = divisor(total, 512)
    return (2, total // line, line)


def first_scores_body(raw, units, x_ref, e_hbm, stat_ref, stage, semaphores):
    target = [(slice(None), lambda columns: e_hbm.at[:, columns])]
    score_points(raw, units, x_ref, target, stat_ref, stage, semaphores)


def next_scores_body(raw, count, pieces, away, *refs):
    unit_refs = refs[:count]
    x_ref = refs[count]
    e_hbm, stat_ref, units, stage, semaphores = refs[-5:]
    rows = unit_refs[0].shape[0]
    pair = CORES * pieces * rows
    chip, core = place()
    chips = e_hbm.shape[0] // pair
    for number, ref in enumerate(unit_refs):
        group, who, piece = number // (CORES * pieces), number // pieces % CORES, number % pieces
        of_pair = (core if who == 0 else 1 - core) * pieces + piece
        start = pl.multiple_of((group * CORES * pieces + of_pair) * rows, rows)
        units[pl.ds(start, rows), :] = ref[...]

    def target_of(number):
        start = pl.multiple_of(lax.rem(chip + away + number, chips) * pair, pair)
        return lambda columns: e_hbm.at[pl.ds(start, pair), columns]

    targets = [
        (slice(number * pair, (number + 1) * pair), target_of(number)) for number in range(count // (CORES * pieces))
    ]
    score_points(raw, units, x_ref, targets, stat_ref, stage, semaphores)


def scores(raw, blocks, points, pieces=1, away=None, shifted=None):
    total, width = points.shape
    count = len(blocks)
    rows = sum(block.shape[0] for block in blocks)
    all_rows = rows if shifted is None else shifted.shape[0]
    stat = stat_shape(total)
    parts = 1 if away is None else count // (CORES * pieces)
    more = [] if shifted is None or away == 0 else [shifted]
    scratch = [
        pltpu.VMEM((divisor(stat[1], 2), rows, stat[2]), F32),
        pltpu.SemaphoreType.DMA((divisor(stat[1], 2), parts)),
    ]
    if away is not None:
        scratch = [pltpu.VMEM((rows, width), BF16)] + scratch
    if away is None:
        body = functools.partial(first_scores_body, raw)
    else:
        body = functools.partial(next_scores_body, raw, count, pieces, away)
    return pl.pallas_call(
        body,
        in_specs=[VMEM] * (count + 1) + [ANY] * len(more),
        out_specs=[ANY, VMEM],
        out_shape=[
            jax.ShapeDtypeStruct((all_rows, total), F32),
            jax.ShapeDtypeStruct(stat, F32),
        ],
        input_output_aliases={count + 1: 0} if more else {},
        scratch_shapes=scratch,
        compiler_params=params(SCORE_VMEM),
        cost_estimate=pl.CostEstimate(
            flops=2 * rows * total * width,
            bytes_accessed=2 * total * width + 4 * rows * total,
            transcendentals=rows * total,
        ),
    )(*blocks, points, *more)


FAR, THEIRS, OWN = range(3)


def weigh_body(by_rows, n_sets, n_tops, n_found, cuts, kind, others, extra, pair, *refs):
    parts = CORES if kind == FAR else 1
    stat_refs, refs = refs[:n_sets], refs[n_sets:]
    top_refs, (e_hbm, x_ref, _), refs = refs[:n_tops], refs[n_tops : n_tops + 3], refs[n_tops + 3 :]
    found_refs, refs = refs[:n_found], refs[n_found:]
    cut_refs = ()
    if cuts:
        cut_refs, refs = refs[: len(cuts) - 1], refs[len(cuts) - 1 :]
        out_refs, refs = refs[-1:], refs[:-1]
    else:
        out_refs, refs = refs[:parts], refs[parts:]
    if not by_rows:
        (kept_ref, kept_mass_ref), refs = refs[:2], refs[2:]
    scale_refs, refs = refs[:2], refs[2:]
    n_weights = 2 if by_rows else 0
    weights_refs, (stage, mass_ref, sum_ref, semaphores) = refs[:n_weights], refs[n_weights:]
    chip, core = place()
    line = stat_refs[0].shape[2]
    total = x_ref.shape[0]
    height, span = sum_ref.shape
    slots, _, chunk = stage.shape
    steps = total // chunk
    lanes = min(line, 128)

    def block_of(other):
        if kind == FAR:
            return lax.rem(chip + 1 + other, others + 1)
        return chip * CORES + (core if kind == OWN else 1 - core)

    def copy_of(number):
        other, step = divmod(number, steps)
        rows = pl.ds(pl.multiple_of(block_of(other) * height, height), height) if by_rows else slice(None)
        columns = slice(step * chunk, (step + 1) * chunk)
        slot = number % slots
        return pltpu.make_async_copy(e_hbm.at[rows, columns], stage.at[slot], semaphores.at[slot])

    for number in range(min(slots, others * steps)):
        copy_of(number).start()
    top, all_total = merge(stat_refs)
    if by_rows:
        scale_refs[0][...] = top
        scale_refs[1][...] = 1.0 / all_total
    else:
        for ref, scale_ref in zip((top_refs[0], top_refs[-1]), scale_refs):
            scale_ref[...] = jnp.exp(ref[0] - top) / all_total

    def weights_of(values, group, number):
        one, two = (ref[number : number + 1, :] for ref in scale_refs)
        if by_rows:
            return jnp.exp(values - one) * two
        return values * jnp.where(chip == group, one, two)

    group_rows = height if by_rows else pair
    kept = not by_rows

    def weights_part(step):
        columns = slice(step * chunk, (step + 1) * chunk)
        return kept_ref.at[:, columns] if kept else weights_refs[step % 2]

    def weigh_step(number):
        step = number % steps
        weights_ref = weights_part(step)
        for group in range(height // group_rows):
            rows = slice(group * group_rows, (group + 1) * group_rows)
            mass = None
            for offset in range(0, chunk, line):
                values = stage[number % slots, rows, offset : offset + line]
                weights = weights_of(values, group, (step * chunk + offset) // line).astype(BF16)
                weights_ref[rows, offset : offset + line] = weights
                wide = weights.astype(F32)
                for lane in range(0, line, lanes):
                    piece = wide[:, lane : lane + lanes]
                    mass = piece if mass is None else mass + piece
            mass_ref[rows, :] = mass if step == 0 else mass_ref[rows, :] + mass

    weighed = steps if kept else others * steps
    for number in range(others * steps):
        other, step = divmod(number, steps)
        if number < weighed:
            copy_of(number).wait()
            weigh_step(number)
        if number + slots < weighed:
            copy_of(number + slots).start()
        columns = slice(None)
        if not by_rows:
            columns = pl.ds(pl.multiple_of(block_of(other) * span, span), span)
        product = jnp.dot(
            weights_part(step)[...],
            x_ref[step * chunk : (step + 1) * chunk, columns],
            preferred_element_type=F32,
        )
        sum_ref[...] = product if step == 0 else sum_ref[...] + product
        if step == steps - 1:
            mass = jnp.sum(mass_ref[...].T, axis=0, keepdims=True)
            if kept:
                kept_mass_ref[...] = mass
            write_sums(by_rows, other, core, out_refs, sum_ref, mass, extra)
    for number, ref in enumerate(cut_refs):
        ref[...] = out_refs[0][0, cuts[number] : cuts[number + 1], :]
    start = 0
    for ref in found_refs:
        out_refs[0][0, start : start + ref.shape[0], :] += ref[...]
        start += ref.shape[0]


def write_sums(by_rows, other, core, out_refs, sum_ref, mass, extra):
    parts = len(out_refs)
    rows = out_refs[0].shape[1] - extra
    width = out_refs[0].shape[2]
    for part, ref in enumerate(out_refs):
        side = lax.rem(core + part, parts)
        ref[other, rows:, :] = jnp.zeros((extra, width), F32)
        if by_rows:
            found = mass
            if parts > 1:
                found = jnp.where(side == 0, mass[:, :rows], mass[:, rows:])
                ref[other, :rows, :] = sum_ref[pl.ds(pl.multiple_of(side * rows, rows), rows), :]
            else:
                ref[other, :rows, :] = sum_ref[...]
            ref[other, rows : rows + 1, :rows] = found
        else:
            sums = sum_ref[...]
            if parts > 1:
                sums = jnp.where(side == 0, sums[:, :width], sums[:, width:])
            ref[other, :rows, :] = sums
            for number in range(rows // width):
                ref[other, rows + number : rows + number + 1, :] = mass[
                    :, number * width : (number + 1) * width
                ]


def weigh_kept_body(kind, extra, kept_ref, mass_ref, x_ref, _, out_ref, kept_out, sum_ref):
    chip, core = place()
    span = sum_ref.shape[1]
    total = x_ref.shape[0]
    block = chip * CORES + (core if kind == OWN else 1 - core)
    columns = pl.ds(pl.multiple_of(block * span, span), span)
    sum_ref[...] = jnp.dot(kept_ref[...], x_ref[:, columns], preferred_element_type=F32)
    write_sums(False, 0, core, [out_ref], sum_ref, mass_ref[...], extra)


def weigh_kept(kind, n_pts, kept, mass, points, after):
    total, width = points.shape
    rows, cols = kept.shape[0], width // n_pts
    extra = round_up(-(-rows // cols), 8)
    return pl.pallas_call(
        functools.partial(weigh_kept_body, kind, extra),
        in_specs=[VMEM] * 3 + [ANY],
        out_specs=[VMEM] * 2,
        input_output_aliases={0: 1},
        scratch_shapes=[pltpu.VMEM((rows, cols), F32)],
        out_shape=[
            jax.ShapeDtypeStruct((1, rows + extra, cols), F32),
            jax.ShapeDtypeStruct(kept.shape, BF16),
        ],
        compiler_params=params(KEPT_VMEM),
        cost_estimate=pl.CostEstimate(
            flops=2 * rows * cols * total, bytes_accessed=2 * total * (rows + cols), transcendentals=0
        ),
    )(kept, mass, points, after)


def weigh(by_rows, kind, chips, stats, tops, shifted, points, after, found=()):
    total, width = points.shape
    pair = shifted.shape[0] // chips
    parts, others = (CORES, chips - 1) if kind == FAR else (1, 1)
    line = stats[0].shape[2]
    chunk = line * divisor(total // line, CHUNK_LINES)
    slots = min(WEIGH_SLOTS, total // chunk)
    kept = []
    if not by_rows:
        kept = [
            jax.ShapeDtypeStruct((shifted.shape[0], total), BF16),
            jax.ShapeDtypeStruct((1, shifted.shape[0]), F32),
        ]
    if by_rows:
        rows, cols = pair // CORES, width
        sums = (rows * parts, width)
    else:
        rows, cols = shifted.shape[0], width // (CORES * chips)
        sums = (rows, cols * parts)
    n_tops = len(tops)
    extra = round_up(-(-rows // cols), 8)
    outs = [jax.ShapeDtypeStruct((others, rows + extra, cols), F32)] * parts
    cuts, whole = (), []
    if by_rows and kind == THEIRS:
        cuts = [round_up(rows * part // PIECES, 8) for part in range(PIECES)] + [rows + extra]
        outs = [jax.ShapeDtypeStruct((end - start, cols), F32) for start, end in zip(cuts, cuts[1:])]
        whole = [pltpu.VMEM((1, rows + extra, cols), F32)]
    return pl.pallas_call(
        functools.partial(
            weigh_body, by_rows, len(stats), n_tops, len(found), cuts, kind, others, extra, pair
        ),
        in_specs=[VMEM] * (len(stats) + n_tops) + [ANY, VMEM, ANY] + [VMEM] * len(found),
        out_specs=[VMEM] * (len(outs) + len(kept)),
        scratch_shapes=[pltpu.VMEM(stats[0].shape[1:], F32)] * 2
        + [pltpu.VMEM((sums[0], chunk), BF16)] * (2 if by_rows else 0)
        + [
            pltpu.VMEM((slots, sums[0], chunk), F32),
            pltpu.VMEM((sums[0], 128), F32),
            pltpu.VMEM(sums, F32),
            pltpu.SemaphoreType.DMA((slots,)),
        ]
        + whole,
        out_shape=outs + kept,
        compiler_params=params(WEIGH_VMEM),
        cost_estimate=pl.CostEstimate(
            flops=0 if found else 2 * others * sums[0] * sums[1] * total,
            bytes_accessed=0 if found else 2 * others * total * (sums[1] + 2 * sums[0]),
            transcendentals=0,
        ),
    )(*stats, *tops, shifted, points, after, *found)


def fold_body(rows, lines, pieces, mine_ref, theirs_ref, after_ref, *out_refs):
    width = out_refs[0].shape[1]
    count = rows // pieces
    step = divisor(count, 128) if lines == 1 else width
    all_masses = mine_ref[rows : rows + lines, :] + theirs_ref[rows : rows + lines, :]
    for piece, out_ref in enumerate(out_refs):
        out_ref[count:, :] = jnp.zeros((out_ref.shape[0] - count, width), BF16)
        scales = []
        for start in range(0, count, step):
            part = slice(piece * count + start, piece * count + start + step)
            total = mine_ref[part, :] + theirs_ref[part, :]
            top = jnp.max(jnp.abs(total), axis=1, keepdims=True)
            scale = jnp.maximum(top * 1.01, 1e-30).astype(BF16).astype(F32)
            out_ref[start : start + step, :] = encode(total, scale)
            scales.append(jnp.broadcast_to(scale, (step, 128)).T[0:1, :])
        if lines == 1:
            out_ref[count : count + 1, :count] = jnp.concatenate(scales, axis=1).astype(BF16)
            mass, used = all_masses[:, piece * count : (piece + 1) * count], slice(0, count)
        else:
            out_ref[count : count + lines, :] = jnp.concatenate(scales, axis=0).astype(BF16)
            mass, used = all_masses, slice(None)
        for number in range(1, 4):
            rounded = mass.astype(BF16)
            out_ref[count + number * lines : count + (number + 1) * lines, used] = rounded
            mass = mass - rounded.astype(F32)


def fold(pieces, mine, theirs, after):
    others, height, width = mine.shape
    rows, lines = shape_of(height, width)
    coded = (rows // pieces + round_up(4 * lines, 16), width)
    return pl.pallas_call(
        functools.partial(fold_body, rows, lines, pieces),
        grid=(others,),
        in_specs=[pl.BlockSpec((None, height, width), lambda d: (d, 0, 0))] * 2 + [ANY],
        out_specs=[pl.BlockSpec((None, *coded), lambda d: (d, 0, 0))] * pieces,
        out_shape=[jax.ShapeDtypeStruct((others, *coded), BF16)] * pieces,
        compiler_params=params(10),
        cost_estimate=pl.CostEstimate(
            flops=20 * others * height * width,
            bytes_accessed=10 * others * height * width,
            transcendentals=others * height * width,
        ),
    )(mine, theirs, after)


def shape_of(height, width):
    rows = height - 8
    while rows + round_up(-(-rows // width), 8) != height:
        rows -= 8
    return rows, -(-rows // width)


def finish_body(rows, lines, piece, as_units, n_near, *refs):
    near_refs, code_refs, (_, out_ref) = refs[:n_near], refs[n_near:-2], refs[-2:]
    count, width = out_ref.shape
    step = divisor(count, 128) if lines == 1 else width
    mass = functools.reduce(jnp.add, [ref[rows : rows + lines, :] for ref in near_refs])
    if lines == 1:
        mass = mass[:, piece * count : (piece + 1) * count]
    used = slice(0, count) if lines == 1 else slice(None)
    for ref in code_refs:
        for number in range(1, 4):
            start = count + number * lines
            mass = mass + ref[start : start + lines, used].astype(F32)

    def column(values, number):
        if lines == 1:
            line = values[:, number * step : (number + 1) * step]
        else:
            line = values[number : number + 1, :]
        return to_column(line, step)[:, 0:1]

    scales = [ref[count : count + lines, used].astype(F32) for ref in code_refs]
    for number in range(count // step):
        part = slice(number * step, (number + 1) * step)
        near = slice(piece * count + number * step, piece * count + (number + 1) * step)
        total = functools.reduce(jnp.add, [ref[near, :] for ref in near_refs])
        for ref, scale in zip(code_refs, scales):
            total = total + decode(ref[part, :], column(scale, number))
        means = total / jnp.maximum(column(mass, number), 1.0)
        out_ref[part, :] = normalize_rows(means).astype(BF16) if as_units else means


def finish(as_units, piece, pieces, near, codes, after):
    height, width = near[0].shape
    rows, lines = shape_of(height, width)
    count = rows // pieces
    return pl.pallas_call(
        functools.partial(finish_body, rows, lines, piece, as_units, len(near)),
        in_specs=[VMEM] * (len(near) + len(codes)) + [ANY],
        out_specs=VMEM,
        out_shape=jax.ShapeDtypeStruct((count, width), BF16 if as_units else F32),
        compiler_params=params(10),
        cost_estimate=pl.CostEstimate(
            flops=30 * count * width,
            bytes_accessed=(12 + 2 * len(codes)) * count * width,
            transcendentals=2 * count * width,
        ),
    )(*near, *codes, after)


def keep_body(value_ref, after_ref, out_ref):
    pass


def keep_until(value, after):
    return pl.pallas_call(
        keep_body,
        in_specs=[VMEM, ANY],
        out_specs=VMEM,
        out_shape=jax.ShapeDtypeStruct(value.shape, value.dtype),
        input_output_aliases={0: 0},
        compiler_params=params(10),
    )(value, after)


def merge_body(*refs):
    refs[-1][0], refs[-1][1] = merge(refs[:-1])


def merged(sets):
    return pl.pallas_call(
        merge_body, out_shape=jax.ShapeDtypeStruct(sets[0].shape, F32), compiler_params=params(10)
    )(*sets)


def log_body(*refs):
    top, total = merge(refs[:-1])
    refs[-1][...] = top + jnp.log(total)


def log_norms(sets):
    return pl.pallas_call(
        log_body, out_shape=jax.ShapeDtypeStruct(sets[0].shape[1:], F32), compiler_params=params(10)
    )(*sets).reshape(-1)


def on_device(n_pts, n_cen, points, centroids):
    chips = n_pts // CORES

    def to_partner(value):
        return lax.ppermute(value, "pts", [(i, i ^ 1) for i in range(n_pts)])

    def to_chip(value, away):
        moves = [(i, (i + CORES * away) % n_pts) for i in range(n_pts)]
        return lax.ppermute(value, "pts", moves)

    def over_centroids(stats):
        if n_cen & (n_cen - 1):
            moves = [[(i, (i + away) % n_cen) for i in range(n_cen)] for away in range(1, n_cen)]
            return [stats] + [lax.ppermute(stats, "cen", move) for move in moves]
        done, sets = 1, [stats]
        while done < n_cen:
            if done > 1:
                sets = [merged(sets)]
            ways = 4 if (n_cen // done).bit_length() % 2 else 2
            for way in range(1, ways):
                moves = [(i, i ^ (way * done)) for i in range(n_cen)]
                sets.append(lax.ppermute(sets[0], "cen", moves))
            done *= ways
        return sets

    def sums_over_pts(by_rows, stats, tops, shifted):
        kept = mass = None

        def weighted(kind, after, found=()):
            nonlocal kept, mass
            if by_rows:
                return weigh(by_rows, kind, chips, stats, tops, shifted, points, after, found)
            if kind == FAR:
                *found, kept, mass = weigh(by_rows, kind, chips, stats, tops, shifted, points, after)
                return found
            *found, kept = weigh_kept(kind, n_pts, kept, mass, points, after)
            return found

        far_mine, far_theirs = weighted(FAR, stats[0])
        far_found = to_partner(far_theirs)
        if by_rows:
            coded = fold(pieces, far_mine, far_found, far_theirs)
            codes = [[to_chip(each[away - 1], away) for away in range(1, chips)] for each in coded]
            near_found = [to_partner(piece) for piece in weighted(THEIRS, coded[0])]
            near = [each[0] for each in weighted(OWN, coded[0], near_found)]
        else:
            (near_theirs,) = weighted(THEIRS, far_theirs)
            near_found = to_partner(near_theirs)
            coded = fold(1, far_mine, far_found, near_theirs)
            codes = [[to_chip(each[away - 1], away) for away in range(1, chips)] for each in coded]
            (near_mine,) = weighted(OWN, coded[0])
            near = [near_mine[0], near_found[0]]
        found, away_found, after = [], [], coded[0]
        for piece, each in enumerate(codes):
            found.append(finish(by_rows, piece, len(codes), near, each, after))
            if by_rows:
                away_found.append([to_chip(found[-1], -away) for away in range(1, chips)])
                after = away_found[-1][-1]
        return found, away_found

    pieces = 1
    units = first_units(centroids)
    shifted, own = scores(ITERS > 1, [units], points)
    stats = over_centroids(own)
    tops = [own]
    for iteration in range(1, ITERS):
        raw = iteration + 1 < ITERS
        mine, away_mine = sums_over_pts(True, stats, tops, shifted)
        near_units = mine + [to_partner(unit) for unit in mine]
        shifted, near_own = scores(raw, near_units, points, pieces, 0, shifted)
        far_units = []
        for units in zip(*away_mine):
            units = [keep_until(unit, near_own) for unit in units]
            far_units += units + [to_partner(unit) for unit in units]
        shifted, far_own = scores(raw, far_units, points, pieces, 1, shifted)
        tops = [near_own, far_own]
        stats = over_centroids(merged([near_own, far_own]))
    (means,), _ = sums_over_pts(False, stats, tops, shifted)
    return (means, log_norms(stats))


def solution(mesh):
    placed = (P("pts", None), P("cen", None))
    return jax.shard_map(
        functools.partial(on_device, mesh.shape["pts"], mesh.shape["cen"]),
        mesh=mesh,
        in_specs=placed,
        out_specs=(P("cen", "pts"), P("pts")),
        check_vma=False,
    )
```
